128 devices in a mesh: dom: 8 (over x, core), blk: 16 (over z, y).
Axes of the slice: x: 4, y: 4, z: 4, core: 2. Of those that a mesh axis runs over, the one named last changes fastest.
Arguments:
- ginv: float32 [8, 2048, 2048], P('dom', 'blk'), as said below
- couple: float32 [8, 2048, 2048], P('dom', 'blk'), may hold values from -0.109375 to 0.109375
- arrow_rhs: float32 [8, 64, 2048], P('dom', None, 'blk'), may hold values from -6 to 6
- arrow_in: float32 [64, 2048], P(None, 'blk'), may hold values from -6 to 6
- tip_cov: float32 [64, 64], replicated, as said below
- bnd_next: float32 [64, 2048], P(None, 'blk'), may hold values from -6 to 6
Outputs:
- arrow_rows: float32 [8, 64, 2048], P('dom', None, 'blk')
- cross_cov: float32 [8, 64, 2048], P('dom', None, 'blk')
The draws below stay inside these ranges and needn't reach their ends.
Inputs may be any that keep to these rules, and one draw needn't show every extreme that they name: `ginv`: every block is zero above its diagonal, with diagonal entries between 0.5 and 1.5. `tip_cov`: Symmetric.
All inputs are finite; a program needn't handle non-finite values.
Results may differ from the reference program's by a relative error of at most 0.00013.
Values sent between devices are 32-bit elements; how exact they have to be, the bound alone decides.
No kernel may reach another device: no remote copies, remote signals or barrier semaphores. Data moves between devices by JAX's collectives and lax.ppermute only.
A program may use at most 64 MiB of HBM per device.

```python
import jax
import jax.numpy as jnp
from jax import lax

B = 2048
A = 64
TSTEPS = 8


def draw_ginv(key, part):
    first_key, second_key = jax.random.split(jax.random.fold_in(key, 11))
    diagonal = jax.random.uniform(first_key, (TSTEPS, B), jnp.float32, 0.6, 1.4)
    lower_part = jax.random.normal(second_key, (TSTEPS, B, B), jnp.float32) * (0.6 / jnp.sqrt(B * 1.0))
    lower_part = jnp.tril(lower_part, -1)
    return lower_part + diagonal[:, :, None] * jnp.eye(B, dtype=jnp.float32)[None]


def draw_tip_cov(key, part):
    first_key, second_key = jax.random.split(jax.random.fold_in(key, 23))
    entries = jax.random.normal(first_key, (A, A), jnp.float32) * (0.3 / jnp.sqrt(A * 1.0))
    diagonal = jax.random.uniform(second_key, (A,), jnp.float32, 0.2, 0.6)
    return 0.5 * (entries + entries.T) + jnp.diag(diagonal)


def shard_levels(key, extent, cuts, smallest, top_value):
    factor_of = 1.0
    for dim, shards_of in cuts:
        heights = jax.random.uniform(jax.random.fold_in(jax.random.fold_in(key, 6), dim), (shards_of,), jnp.float32, smallest / len(cuts), top_value / len(cuts))
        factor_of = factor_of * jnp.repeat(jnp.exp(heights), extent[dim] // shards_of).reshape((-1,) + (1,) * (len(extent) - 1 - dim))
    return factor_of


def noise(own_key, shape, deviation, most, shards=(), kind=jnp.bfloat16):
    factor_of = shard_levels(own_key, shape, shards, -0.22, 0.18) if shards else 1.0
    values = jax.random.normal(own_key, shape, jnp.float32) * deviation * factor_of
    return jnp.minimum(jnp.maximum(values, -most), most).astype(kind)


def setup_inputs(seed: int = 0) -> dict:
    keys = jax.random.split(jax.random.key(seed), 7)
    return {
        "ginv": draw_ginv(jax.random.fold_in(keys[6], 71), 0),
        "couple": noise(keys[1], (TSTEPS, B, B), (B * 3 // 2) ** -0.5, 0.109375, ((0, 8), (1, 16)), jnp.float32),
        "arrow_rhs": noise(keys[2], (TSTEPS, A, B), 1.0, 6.0, ((0, 8), (2, 16)), jnp.float32),
        "arrow_in": noise(keys[3], (A, B), 1.0, 6.0, ((1, 16),), jnp.float32),
        "tip_cov": draw_tip_cov(jax.random.fold_in(keys[6], 71), 0),
        "bnd_next": noise(keys[5], (A, B), 1.0, 6.0, ((1, 16),), jnp.float32),
    }


highest = lax.Precision.HIGHEST


def reference(ginv, couple, arrow_rhs, arrow_in, tip_cov, bnd_next):
    step_count = ginv.shape[0]
    row_list = []
    previous = arrow_in
    for step_index in range(step_count):
        update = arrow_rhs[step_index] - jnp.dot(previous, couple[step_index].T, precision=highest)
        arrow_row = jnp.dot(update, ginv[step_index].T, precision=highest)
        row_list.append(arrow_row)
        previous = arrow_row
    onward = bnd_next
    cov_list = [None] * step_count
    for step_index in range(step_count - 1, -1, -1):
        combined = onward + jnp.dot(tip_cov, row_list[step_index], precision=highest)
        covariance = -jnp.dot(combined, ginv[step_index], precision=highest)
        cov_list[step_index] = covariance
        onward = jnp.dot(covariance, couple[step_index], precision=highest)
    return jnp.stack(row_list), jnp.stack(cov_list)
```

```python
import jax
import jax.numpy as jnp
from jax import lax
from jax.sharding import PartitionSpec as P

both = ("dom", "blk")
SIDE = 4
STEPS = 8
high = lax.Precision.HIGH


def device_of(t, z, y):
    return t * SIDE * SIDE + (z % SIDE) * SIDE + y % SIDE


def pairs(target, steps=range(STEPS)):
    return [
        (device_of(t, z, y), device_of(*target(t, z, y)))
        for t in steps
        for z in range(SIDE)
        for y in range(SIDE)
    ]


def sent(value, target, steps=range(STEPS)):
    return lax.ppermute(value, both, pairs(target, steps))


def dot(a, b):
    return jnp.dot(a, b, precision=high)


def dot_t(a, b):
    return lax.dot_general(a, b, (((1,), (1,)), ((), ())), precision=high)


def ring_gather(block, shift):
    half = block.shape[0] // 2
    before = sent(block, lambda t, z, y: shift(t, z, y, 1))
    after = sent(block, lambda t, z, y: shift(t, z, y, -1))
    far_top = sent(before[:half], lambda t, z, y: shift(t, z, y, 1))
    far_bottom = sent(after[half:], lambda t, z, y: shift(t, z, y, -1))
    return [block, after, jnp.concatenate([far_top, far_bottom]), before]


def rolled_down(value, amount):
    rows = value.shape[0]
    return lax.dynamic_slice_in_dim(
        jnp.concatenate([value, value]), (rows - amount) % rows, rows, 0
    )


def on_device(ginv, couple, arrow_rhs, arrow_in, tip_cov, bnd_next):
    g_rows = ginv[0]
    e_rows = couple[0]
    width = g_rows.shape[1]
    rows = g_rows.shape[0]
    panel = width // SIDE
    step = lax.axis_index("dom")
    place = lax.axis_index("blk")
    z, y = place // SIDE, place % SIDE

    along_y = [[SIDE * i + j for j in range(SIDE)] for i in range(SIDE)]
    e_cols = jnp.stack([e_rows[:, panel * i : panel * (i + 1)] for i in range(SIDE)])
    e_block = lax.all_to_all(e_cols, "blk", 0, 0, axis_index_groups=along_y)
    e_block = e_block.reshape(panel, panel)

    g_ring = ring_gather(g_rows, lambda t, z, y, k: (t, z, y + k))
    e_ring = ring_gather(e_block, lambda t, z, y, k: (t, z + k, y))

    small = jnp.concatenate([arrow_rhs[0], arrow_in, bnd_next])
    small = lax.all_gather(small, "blk", axis=1, tiled=True)
    arrow = arrow_in.shape[0]
    rhs_in = lax.dynamic_slice_in_dim(small[: 2 * arrow], y * panel, panel, 1)
    bnd = lax.dynamic_slice_in_dim(small[2 * arrow :], z * panel, panel, 1)
    rhs = rhs_in[:arrow]

    g_panel = rolled_down(jnp.concatenate(g_ring), y * rows)
    w = 0.0
    for k in range(SIDE):
        g_part = lax.dynamic_slice_in_dim(g_panel, (z + k) % SIDE * panel, panel, 1)
        w = w + dot(g_part, e_ring[k])
    g_block = lax.dynamic_slice_in_dim(g_panel, y * panel, panel, 1)

    base = dot_t(rhs, g_block)
    incoming = jnp.where(step == 0, rhs_in[arrow:], 0.0)
    for s in range(STEPS):
        partial = base - dot_t(incoming, w)
        if s < STEPS - 1:
            for k in range(SIDE):
                incoming = incoming + sent(
                    partial, lambda t, z, y: (t + 1, y + k, z), [s]
                )
    arrow_panel = jnp.where(step == STEPS - 1, partial, 0.0)
    for k in range(1, SIDE):
        arrow_panel = arrow_panel + sent(partial, lambda t, z, y: (t, z, y + k), [STEPS - 1])
    arrow_panel = arrow_panel + sent(
        incoming, lambda t, z, y: (t - 1, y, z), range(1, STEPS)
    )
    tip_term = jnp.dot(tip_cov, arrow_panel, precision=lax.Precision.HIGHEST)

    combined = tip_term + jnp.where(step == STEPS - 1, bnd, 0.0)
    for s in range(STEPS - 1, 0, -1):
        partial = -dot(combined, w)
        for k in range(SIDE):
            combined = combined + sent(
                partial, lambda t, z, y: (t - 1, y, z + k), [s]
            )
    partial = -dot(combined, g_block)
    covariance = 0.0
    for k in range(SIDE):
        piece = lax.dynamic_slice_in_dim(partial, (z + k) % SIDE * rows, rows, 1)
        covariance = covariance + sent(piece, lambda t, z, y: (t, y, z + k))
    arrow_local = lax.dynamic_slice_in_dim(arrow_panel, y * rows, rows, 1)
    return (arrow_local[None], covariance[None])


def solution(mesh):
    return jax.shard_map(
        on_device,
        mesh=mesh,
        in_specs=(
            P("dom", "blk", None),
            P("dom", "blk", None),
            P("dom", None, "blk"),
            P(None, "blk"),
            P(),
            P(None, "blk"),
        ),
        out_specs=(P("dom", None, "blk"), P("dom", None, "blk")),
        check_vma=False,
    )
```

```python
import jax
import jax.numpy as jnp
from jax import lax
from jax.experimental import pallas as pl
from jax.experimental.pallas import tpu as pltpu
from jax.sharding import PartitionSpec as P

both = ("dom", "blk")
SIDE = 4
STEPS = 8
VMEM_LIMIT = 48 * 1024 * 1024
f32 = jnp.float32
bf16 = jnp.bfloat16


def device_of(t, z, y):
    return t * SIDE * SIDE + (z % SIDE) * SIDE + y % SIDE


def pairs(target, steps):
    return [
        (device_of(t, z, y), device_of(*target(t, z, y)))
        for t in steps
        for z in range(SIDE)
        for y in range(SIDE)
    ]


def by_minor(k):
    return pairs(lambda t, z, y: (t, z + k * (t % 2), y + k * (1 - t % 2)), range(STEPS))


def by_major(k):
    return pairs(lambda t, z, y: (t, z + k * (1 - t % 2), y + k * (t % 2)), range(STEPS))


def to_next(s, k):
    along_z = s % 2
    steps = range(s % 2, STEPS - 1, 2)
    return pairs(lambda t, z, y: (t + 1, z + k * along_z, y + k * (1 - along_z)), steps)


def to_earlier(s, k):
    along_z = 1 - s % 2
    steps = range(2 - s % 2, STEPS, 2)
    return pairs(lambda t, z, y: (t - 1, z + k * along_z, y + k * (1 - along_z)), steps)


def permuted(value, where):
    return lax.ppermute(value, both, where)


def ring_gather(block, where):
    half = block.shape[0] // 2
    after = permuted(block, where(-1))
    before = permuted(block, where(1))
    top = permuted(before[:half], where(1))
    bottom = permuted(after[half:], where(-1))
    return block, after, top, bottom, before


def halves(value):
    high = value.astype(bf16)
    return high, (value - high.astype(f32)).astype(bf16)


def product(a, b_high, b_low, dims):
    a_high, a_low = halves(a)

    def one(x, y):
        return lax.dot_general(x, y, (dims, ((), ())), preferred_element_type=f32)

    return one(a_high, b_high) + (one(a_high, b_low) + one(a_low, b_high))


PLAIN = ((1,), (0,))
TURNED = ((1,), (1,))


def cell_start(odd, i, j, rows):
    cell = jnp.where(odd != 0, SIDE * j + i, SIDE * i + j)
    return pl.multiple_of(cell * rows, rows)


def pieces_kernel(place, e_ref, *outs):
    rows = e_ref.shape[0]
    odd, minor = place[0], place[2]
    for k in range(SIDE):
        for i in range(SIDE):
            start = cell_start(odd, i, (minor + k) % SIDE, rows)
            outs[k][:, rows * i : rows * (i + 1)] = e_ref[:, pl.ds(start, rows)]


def form_kernel(
    place, g_own, g_after, g_top, g_bottom, g_before, e_own, e_after, e_top, e_bottom, e_before, small,
    w_high, w_low, g_high, g_low, base, first, bound, partial, total, chunk,
):
    odd, major, minor, is_first, is_last = (place[i] for i in range(5))
    rows = g_own.shape[0]
    panel = rows * SIDE
    half = rows // 2
    arrow = small.shape[0] // 3

    def g_cols(j, start):
        if j == 0:
            return [(0, g_own[:, pl.ds(start, rows)])]
        if j == 1:
            return [(0, g_after[:, pl.ds(start, rows)])]
        if j == 3:
            return [(0, g_before[:, pl.ds(start, rows)])]
        return [(0, g_top[:, pl.ds(start, rows)]), (half, g_bottom[:, pl.ds(start, rows)])]

    for i in range(SIDE):
        for j in range(SIDE):
            for c in range(SIDE):
                start = cell_start(odd, (major + i) % SIDE, (minor + c) % SIDE, rows)
                for offset, value in g_cols(j, start):
                    top = rows * j + offset
                    chunk[top : top + value.shape[0], rows * c : rows * (c + 1)] = value
        if i == 0:
            e_value = e_own[...]
        elif i == 1:
            e_value = e_after[...]
        elif i == 3:
            e_value = e_before[...]
        else:
            e_value = jnp.concatenate([e_top[...], e_bottom[...]])
        e_high, e_low = halves(e_value)
        term = product(chunk[...], e_high, e_low, PLAIN)
        if i == 0:
            total[...] = term
        else:
            total[...] += term

    for j in range(SIDE):
        high, low = halves(total[rows * j : rows * (j + 1), :])
        target = pl.ds(pl.multiple_of((minor + j) % SIDE * rows, rows), rows)
        w_high[target, :] = high
        w_low[target, :] = low
        for i in range(SIDE):
            start = cell_start(odd, i, minor, rows)
            for offset, value in g_cols(j, start):
                spot = pl.ds(pl.multiple_of((minor + j) % SIDE * rows + offset, half), value.shape[0])
                high, low = halves(value)
                g_high[spot, rows * i : rows * (i + 1)] = high
                g_low[spot, rows * i : rows * (i + 1)] = low

    for i in range(SIDE):
        cols = slice(rows * i, rows * (i + 1))
        start = cell_start(odd, i, minor, rows)
        chunk[: 2 * arrow, cols] = small[: 2 * arrow, pl.ds(start, rows)]
        start = cell_start(odd, major, i, rows)
        bound[:, cols] = jnp.where(is_last != 0, small[2 * arrow :, pl.ds(start, rows)], 0.0)
    first[...] = jnp.where(is_first != 0, chunk[arrow : 2 * arrow, :], 0.0)
    base[...] = product(chunk[:arrow, :], g_high[...], g_low[...], TURNED)
    partial[...] = base[...] - product(first[...], w_high[...], w_low[...], TURNED)


def forward_kernel(flag, old, r0, r1, r2, r3, base, w_high, w_low, new, partial):
    arrived = (r0[...] + r1[...]) + (r2[...] + r3[...])
    new[...] = jnp.where(flag[0] != 0, arrived, old[...])
    partial[...] = base[...] - product(new[...], w_high[...], w_low[...], TURNED)


def turn_kernel(place, own, r1, r2, r3, tip, bound, w_high, w_low, rows_out, tip_term, combined, partial):
    arrow_panel = (own[...] + r1[...]) + (r2[...] + r3[...])
    panel_high, panel_low = halves(arrow_panel)
    tip_term[...] = product(tip[...], panel_high, panel_low, PLAIN)
    combined[...] = tip_term[...] + bound[...]
    partial[...] = -product(combined[...], w_high[...], w_low[...], PLAIN)
    width = rows_out.shape[1]
    minor = place[2]
    chosen = arrow_panel[:, :width]
    for j in range(1, SIDE):
        chosen = jnp.where(minor == j, arrow_panel[:, width * j : width * (j + 1)], chosen)
    rows_out[...] = chosen


def backward_kernel(flag, old, r0, r1, r2, r3, tip_term, w_high, w_low, new, partial):
    arrived = (r0[...] + r1[...]) + (r2[...] + r3[...])
    new[...] = jnp.where(flag[0] != 0, tip_term[...] + arrived, old[...])
    partial[...] = -product(new[...], w_high[...], w_low[...], PLAIN)


def closing_kernel(place, flag, old, r0, r1, r2, r3, tip_term, g_high, g_low, p0, p1, p2, p3, scratch):
    arrived = (r0[...] + r1[...]) + (r2[...] + r3[...])
    combined = jnp.where(flag[0] != 0, tip_term[...] + arrived, old[...])
    scratch[...] = -product(combined, g_high[...], g_low[...], PLAIN)
    width = p0.shape[1]
    major = place[1]
    for k, out in enumerate((p0, p1, p2, p3)):
        start = pl.multiple_of((major + k) % SIDE * width, width)
        out[...] = scratch[:, pl.ds(start, width)]


def call(kernel, scalars, arrays, outs, scratch=()):
    smem = pl.BlockSpec(memory_space=pltpu.SMEM)
    vmem = pl.BlockSpec(memory_space=pltpu.VMEM)
    return pl.pallas_call(
        kernel,
        out_shape=[jax.ShapeDtypeStruct(shape, dtype) for shape, dtype in outs],
        in_specs=[smem] * len(scalars) + [vmem] * len(arrays),
        out_specs=[vmem] * len(outs),
        scratch_shapes=[pltpu.VMEM(shape, dtype) for shape, dtype in scratch],
        compiler_params=pltpu.CompilerParams(vmem_limit_bytes=VMEM_LIMIT),
    )(*scalars, *arrays)


def on_device(ginv, couple, arrow_rhs, arrow_in, tip_cov, bnd_next):
    g_rows = ginv[0]
    e_rows = couple[0]
    rows = g_rows.shape[0]
    panel = rows * SIDE
    arrow = arrow_in.shape[0]
    step = lax.axis_index("dom")
    spot = lax.axis_index("blk")
    odd = step % 2
    z, y = spot // SIDE, spot % SIDE
    major = jnp.where(odd == 0, z, y)
    minor = jnp.where(odd == 0, y, z)
    place = jnp.stack([odd, major, minor, step == 0, step == STEPS - 1]).astype(jnp.int32)
    wide = ((arrow, panel), f32)
    narrow = ((arrow, rows), f32)
    half_block = ((panel, panel), bf16)

    small = jnp.concatenate([arrow_rhs[0], arrow_in, bnd_next])
    small = lax.all_gather(small, "blk", axis=1, tiled=True)

    pieces = call(pieces_kernel, [place], [e_rows], [((rows, panel), f32)] * SIDE)
    e_block = jnp.concatenate(
        [pieces[0]] + [permuted(pieces[k], by_minor(k)) for k in range(SIDE - 1, 0, -1)]
    )
    g_ring = ring_gather(g_rows, by_minor)
    e_ring = ring_gather(e_block, by_major)

    w_high, w_low, g_high, g_low, base, incoming, bound, partial = call(
        form_kernel,
        [place],
        [*g_ring, *e_ring, small],
        [half_block] * 4 + [wide] * 4,
        [((panel, panel), f32)] * 2,
    )
    for s in range(STEPS - 1):
        arrived = [permuted(partial, to_next(s, k)) for k in range(SIDE)]
        flag = (step == s + 1).astype(jnp.int32)[None]
        incoming, partial = call(
            forward_kernel, [flag], [incoming, *arrived, base, w_high, w_low], [wide] * 2
        )
    arrived = [permuted(partial, by_minor(k)) for k in range(1, SIDE)]
    arrow_local, tip_term, combined, partial = call(
        turn_kernel,
        [place],
        [partial, *arrived, tip_cov, bound, w_high, w_low],
        [narrow] + [wide] * 3,
    )
    for s in range(STEPS - 1, 0, -1):
        arrived = [permuted(partial, to_earlier(s, k)) for k in range(SIDE)]
        flag = (step == s - 1).astype(jnp.int32)[None]
        if s > 1:
            combined, partial = call(
                backward_kernel, [flag], [combined, *arrived, tip_term, w_high, w_low], [wide] * 2
            )
    parts = call(
        closing_kernel,
        [place, flag],
        [combined, *arrived, tip_term, g_high, g_low],
        [narrow] * SIDE,
        [wide],
    )
    covariance = parts[0]
    for k in range(1, SIDE):
        covariance = covariance + permuted(parts[k], by_major(k))
    return (arrow_local[None], covariance[None])


def solution(mesh):
    return jax.shard_map(
        on_device,
        mesh=mesh,
        in_specs=(
            P("dom", "blk", None),
            P("dom", "blk", None),
            P("dom", None, "blk"),
            P(None, "blk"),
            P(),
            P(None, "blk"),
        ),
        out_specs=(P("dom", None, "blk"), P("dom", None, "blk")),
        check_vma=False,
    )
```

```python
import jax
import jax.numpy as jnp
from jax import lax
from jax.experimental import pallas as pl
from jax.experimental.pallas import tpu as pltpu
from jax.sharding import PartitionSpec as P

both = ("dom", "blk")
SIDE = 4
STEPS = 8
FARTHEST_FIRST = (2, 1, 3, 0)
VMEM_LIMIT = 48 * 1024 * 1024
f32 = jnp.float32
bf16 = jnp.bfloat16


def device_of(t, z, y):
    return t * SIDE * SIDE + (z % SIDE) * SIDE + y % SIDE


def pairs(target, steps):
    return [
        (device_of(t, z, y), device_of(*target(t, z, y)))
        for t in steps
        for z in range(SIDE)
        for y in range(SIDE)
    ]


def by_minor(k):
    return pairs(lambda t, z, y: (t, z + k * (t % 2), y + k * (1 - t % 2)), range(STEPS))


def by_major(k):
    return pairs(lambda t, z, y: (t, z + k * (1 - t % 2), y + k * (t % 2)), range(STEPS))


def together(s, groups):
    return next(group for group in groups if s in group)


def to_next(s, k):
    along_z = s % 2
    steps = together(s, ((0, 4), (2, 6), (1, 3, 5)))
    return pairs(lambda t, z, y: (t + 1, z + k * along_z, y + k * (1 - along_z)), steps)


def to_earlier(s, k):
    along_z = 1 - s % 2
    steps = together(s, ((7, 3), (5, 1), (6, 2), (4,)))
    return pairs(lambda t, z, y: (t - 1, z + k * along_z, y + k * (1 - along_z)), steps)


def permuted(value, where):
    return lax.ppermute(value, both, where)


def ring_gather(block, where):
    half = block.shape[0] // 2
    after = permuted(block, where(-1))
    before = permuted(block, where(1))
    top = permuted(before[:half], where(1))
    bottom = permuted(after[half:], where(-1))
    return block, after, top, bottom, before


def halves(value):
    high = value.astype(bf16)
    return high, (value - high.astype(f32)).astype(bf16)


def product(a, b_high, b_low, dims):
    a_high, a_low = halves(a)

    def one(x, y):
        return lax.dot_general(x, y, (dims, ((), ())), preferred_element_type=f32)

    return one(a_high, b_high) + (one(a_high, b_low) + one(a_low, b_high))


PLAIN = ((1,), (0,))
TURNED = ((1,), (1,))


def cell_start(odd, i, j, rows):
    cell = jnp.where(odd != 0, SIDE * j + i, SIDE * i + j)
    return pl.multiple_of(cell * rows, rows)


def pieces_kernel(place, e_ref, *outs):
    rows = e_ref.shape[0]
    odd, minor = place[0], place[2]
    for k in range(SIDE):
        for i in range(SIDE):
            start = cell_start(odd, i, (minor + k) % SIDE, rows)
            outs[k][:, rows * i : rows * (i + 1)] = e_ref[:, pl.ds(start, rows)]


def form_kernel(
    place, g_own, g_after, g_top, g_bottom, g_before, e_own, e_after, e_top, e_bottom, e_before, small,
    w_high, w_low, g_high, g_low, base, first, bound, partial, total, chunk,
):
    odd, major, minor, is_first, is_last = (place[i] for i in range(5))
    rows = g_own.shape[0]
    panel = rows * SIDE
    half = rows // 2
    arrow = small.shape[0] // 3

    def g_cols(j, start):
        if j == 0:
            return [(0, g_own[:, pl.ds(start, rows)])]
        if j == 1:
            return [(0, g_after[:, pl.ds(start, rows)])]
        if j == 3:
            return [(0, g_before[:, pl.ds(start, rows)])]
        return [(0, g_top[:, pl.ds(start, rows)]), (half, g_bottom[:, pl.ds(start, rows)])]

    for i in range(SIDE):
        for j in range(SIDE):
            for c in range(SIDE):
                start = cell_start(odd, (major + i) % SIDE, (minor + c) % SIDE, rows)
                for offset, value in g_cols(j, start):
                    top = rows * j + offset
                    chunk[top : top + value.shape[0], rows * c : rows * (c + 1)] = value
        if i == 0:
            e_value = e_own[...]
        elif i == 1:
            e_value = e_after[...]
        elif i == 3:
            e_value = e_before[...]
        else:
            e_value = jnp.concatenate([e_top[...], e_bottom[...]])
        e_high, e_low = halves(e_value)
        term = product(chunk[...], e_high, e_low, PLAIN)
        if i == 0:
            total[...] = term
        else:
            total[...] += term

    for j in range(SIDE):
        high, low = halves(total[rows * j : rows * (j + 1), :])
        target = pl.ds(pl.multiple_of((minor + j) % SIDE * rows, rows), rows)
        w_high[target, :] = high
        w_low[target, :] = low
        for i in range(SIDE):
            start = cell_start(odd, i, minor, rows)
            for offset, value in g_cols(j, start):
                spot = pl.ds(pl.multiple_of((minor + j) % SIDE * rows + offset, half), value.shape[0])
                high, low = halves(value)
                g_high[spot, rows * i : rows * (i + 1)] = high
                g_low[spot, rows * i : rows * (i + 1)] = low

    for i in range(SIDE):
        cols = slice(rows * i, rows * (i + 1))
        start = cell_start(odd, i, minor, rows)
        chunk[: 2 * arrow, cols] = small[: 2 * arrow, pl.ds(start, rows)]
        start = cell_start(odd, major, i, rows)
        bound[:, cols] = jnp.where(is_last != 0, small[2 * arrow :, pl.ds(start, rows)], 0.0)
    first[...] = jnp.where(is_first != 0, chunk[arrow : 2 * arrow, :], 0.0)
    base[...] = product(chunk[:arrow, :], g_high[...], g_low[...], TURNED)
    partial[...] = base[...] - product(first[...], w_high[...], w_low[...], TURNED)


def forward_kernel(flag, old, r0, r1, r2, r3, base, w_high, w_low, new, partial):
    arrived = (r0[...] + r1[...]) + (r2[...] + r3[...])
    new[...] = jnp.where(flag[0] != 0, arrived, old[...])
    partial[...] = base[...] - product(new[...], w_high[...], w_low[...], TURNED)


def turn_kernel(place, own, r1, r2, r3, tip, bound, w_high, w_low, rows_out, tip_term, combined, partial):
    arrow_panel = (own[...] + r1[...]) + (r2[...] + r3[...])
    panel_high, panel_low = halves(arrow_panel)
    tip_term[...] = product(tip[...], panel_high, panel_low, PLAIN)
    combined[...] = tip_term[...] + bound[...]
    partial[...] = -product(combined[...], w_high[...], w_low[...], PLAIN)
    width = rows_out.shape[1]
    minor = place[2]
    chosen = arrow_panel[:, :width]
    for j in range(1, SIDE):
        chosen = jnp.where(minor == j, arrow_panel[:, width * j : width * (j + 1)], chosen)
    rows_out[...] = chosen


def backward_kernel(flag, old, r0, r1, r2, r3, tip_term, w_high, w_low, new, partial):
    arrived = (r0[...] + r1[...]) + (r2[...] + r3[...])
    new[...] = jnp.where(flag[0] != 0, tip_term[...] + arrived, old[...])
    partial[...] = -product(new[...], w_high[...], w_low[...], PLAIN)


def closing_kernel(place, flag, old, r0, r1, r2, r3, tip_term, g_high, g_low, p0, p1, p2, p3, scratch):
    arrived = (r0[...] + r1[...]) + (r2[...] + r3[...])
    combined = jnp.where(flag[0] != 0, tip_term[...] + arrived, old[...])
    scratch[...] = -product(combined, g_high[...], g_low[...], PLAIN)
    width = p0.shape[1]
    major = place[1]
    for k, out in enumerate((p0, p1, p2, p3)):
        start = pl.multiple_of((major + k) % SIDE * width, width)
        out[...] = scratch[:, pl.ds(start, width)]


def call(kernel, scalars, arrays, outs, scratch=()):
    smem = pl.BlockSpec(memory_space=pltpu.SMEM)
    vmem = pl.BlockSpec(memory_space=pltpu.VMEM)
    return pl.pallas_call(
        kernel,
        out_shape=[jax.ShapeDtypeStruct(shape, dtype) for shape, dtype in outs],
        in_specs=[smem] * len(scalars) + [vmem] * len(arrays),
        out_specs=[vmem] * len(outs),
        scratch_shapes=[pltpu.VMEM(shape, dtype) for shape, dtype in scratch],
        compiler_params=pltpu.CompilerParams(vmem_limit_bytes=VMEM_LIMIT),
    )(*scalars, *arrays)


def on_device(ginv, couple, arrow_rhs, arrow_in, tip_cov, bnd_next):
    g_rows = ginv[0]
    e_rows = couple[0]
    rows = g_rows.shape[0]
    panel = rows * SIDE
    arrow = arrow_in.shape[0]
    step = lax.axis_index("dom")
    spot = lax.axis_index("blk")
    odd = step % 2
    z, y = spot // SIDE, spot % SIDE
    major = jnp.where(odd == 0, z, y)
    minor = jnp.where(odd == 0, y, z)
    place = jnp.stack([odd, major, minor, step == 0, step == STEPS - 1]).astype(jnp.int32)
    wide = ((arrow, panel), f32)
    narrow = ((arrow, rows), f32)
    half_block = ((panel, panel), bf16)

    small = jnp.concatenate([arrow_rhs[0], arrow_in, bnd_next])
    small = lax.all_gather(small, "blk", axis=1, tiled=True)

    pieces = call(pieces_kernel, [place], [e_rows], [((rows, panel), f32)] * SIDE)
    e_block = jnp.concatenate(
        [pieces[0]] + [permuted(pieces[k], by_minor(k)) for k in range(SIDE - 1, 0, -1)]
    )
    g_ring = ring_gather(g_rows, by_minor)
    e_ring = ring_gather(e_block, by_major)

    w_high, w_low, g_high, g_low, base, incoming, bound, partial = call(
        form_kernel,
        [place],
        [*g_ring, *e_ring, small],
        [half_block] * 4 + [wide] * 4,
        [((panel, panel), f32)] * 2,
    )
    for s in range(STEPS - 1):
        arrived = [permuted(partial, to_next(s, k)) for k in FARTHEST_FIRST]
        flag = (step == s + 1).astype(jnp.int32)[None]
        incoming, partial = call(
            forward_kernel, [flag], [incoming, *arrived, base, w_high, w_low], [wide] * 2
        )
    arrived = [permuted(partial, by_minor(k)) for k in FARTHEST_FIRST[:-1]]
    arrow_local, tip_term, combined, partial = call(
        turn_kernel,
        [place],
        [partial, *arrived, tip_cov, bound, w_high, w_low],
        [narrow] + [wide] * 3,
    )
    for s in range(STEPS - 1, 0, -1):
        arrived = [permuted(partial, to_earlier(s, k)) for k in FARTHEST_FIRST]
        flag = (step == s - 1).astype(jnp.int32)[None]
        if s > 1:
            combined, partial = call(
                backward_kernel, [flag], [combined, *arrived, tip_term, w_high, w_low], [wide] * 2
            )
    parts = call(
        closing_kernel,
        [place, flag],
        [combined, *arrived, tip_term, g_high, g_low],
        [narrow] * SIDE,
        [wide],
    )
    covariance = parts[0]
    for k in FARTHEST_FIRST[:-1]:
        covariance = covariance + permuted(parts[k], by_major(k))
    return (arrow_local[None], covariance[None])


def solution(mesh):
    return jax.shard_map(
        on_device,
        mesh=mesh,
        in_specs=(
            P("dom", "blk", None),
            P("dom", "blk", None),
            P("dom", None, "blk"),
            P(None, "blk"),
            P(),
            P(None, "blk"),
        ),
        out_specs=(P("dom", None, "blk"), P("dom", None, "blk")),
        check_vma=False,
    )
```

```python
import jax
import jax.numpy as jnp
from jax import lax
from jax.experimental import pallas as pl
from jax.experimental.pallas import tpu as pltpu
from jax.sharding import PartitionSpec as P

both = ("dom", "blk")
SIDE = 4
STEPS = 8
FARTHEST_FIRST = (2, 1, 3, 0)
VMEM_LIMIT = 48 * 1024 * 1024
f32 = jnp.float32
bf16 = jnp.bfloat16


def device_of(t, z, y):
    return t * SIDE * SIDE + (z % SIDE) * SIDE + y % SIDE


def pairs(target, steps):
    return [
        (device_of(t, z, y), device_of(*target(t, z, y)))
        for t in steps
        for z in range(SIDE)
        for y in range(SIDE)
    ]


def by_minor(k):
    return pairs(lambda t, z, y: (t, z + k * (t % 2), y + k * (1 - t % 2)), range(STEPS))


def by_major(k):
    return pairs(lambda t, z, y: (t, z + k * (1 - t % 2), y + k * (t % 2)), range(STEPS))


def together(s, groups):
    return next(group for group in groups if s in group)


def to_next(s, k):
    along_z = s % 2
    steps = together(s, ((0, 4), (2, 6), (1, 3, 5)))
    return pairs(lambda t, z, y: (t + 1, z + k * along_z, y + k * (1 - along_z)), steps)


def to_earlier(s, k):
    along_z = 1 - s % 2
    steps = together(s, ((7, 3), (5, 1), (6, 2), (4,)))
    return pairs(lambda t, z, y: (t - 1, z + k * along_z, y + k * (1 - along_z)), steps)


def permuted(value, where):
    return lax.ppermute(value, both, where)


def ring_near(block, where):
    return permuted(block, where(-1)), permuted(block, where(1))


def ring_far(after, before, where):
    half = after.shape[0] // 2
    return permuted(before[:half], where(1)), permuted(after[half:], where(-1))


def halves(value):
    high = value.astype(bf16)
    return high, (value - high.astype(f32)).astype(bf16)


def product(a, b_high, b_low, dims):
    a_high, a_low = halves(a)

    def one(x, y):
        return lax.dot_general(x, y, (dims, ((), ())), preferred_element_type=f32)

    return one(a_high, b_high) + (one(a_high, b_low) + one(a_low, b_high))


PLAIN = ((1,), (0,))
TURNED = ((1,), (1,))


def cell_start(odd, i, j, rows):
    cell = jnp.where(odd != 0, SIDE * j + i, SIDE * i + j)
    return pl.multiple_of(cell * rows, rows)


def pieces_kernel(place, e_ref, *outs):
    rows = e_ref.shape[0]
    odd, minor = place[0], place[2]
    for k in range(SIDE):
        for i in range(SIDE):
            start = cell_start(odd, i, (minor + k) % SIDE, rows)
            outs[k][:, rows * i : rows * (i + 1)] = e_ref[:, pl.ds(start, rows)]


def near_kernel(
    place, g_own, g_after, g_before, own0, own1, after0, after1, before0, before1,
    total, e_high, e_low, far_high, far_low, block_high, block_low, g_near, e_near, chunk, sems,
):
    odd, major, minor = place[0], place[1], place[2]
    rows = g_own.shape[0]
    panel = rows * SIDE
    copies = []
    for n, source in enumerate((g_own, g_after, g_before)):
        copies.append((source, g_near.at[pl.ds(rows * n, rows)]))
    for n, (first, others) in enumerate(((own0, own1), (after0, after1), (before0, before1))):
        copies.append((first, e_near.at[pl.ds(panel * n, rows)]))
        copies.append((others, e_near.at[pl.ds(panel * n + rows, panel - rows)]))
    copies = [pltpu.make_async_copy(x, y, sems.at[n]) for n, (x, y) in enumerate(copies)]
    for copy in copies:
        copy.start()
    for copy in copies[:3]:
        copy.wait()

    def collect(i):
        for c in range(SIDE):
            start = cell_start(odd, (major + i) % SIDE, (minor + c) % SIDE, rows)
            chunk[:, rows * c : rows * (c + 1)] = g_near[:, pl.ds(start, rows)]
        return chunk[...]

    high, low = halves(collect(2))
    far_high[...] = high
    far_low[...] = low
    for i in range(SIDE):
        start = cell_start(odd, i, minor, rows)
        high, low = halves(g_near[:, pl.ds(start, rows)])
        block_high[:, rows * i : rows * (i + 1)] = high
        block_low[:, rows * i : rows * (i + 1)] = low
    for n, i in enumerate((0, 1, 3)):
        copies[3 + 2 * n].wait()
        copies[4 + 2 * n].wait()
        span = slice(panel * n, panel * (n + 1))
        high, low = halves(e_near[span, :])
        e_high[span, :] = high
        e_low[span, :] = low
        term = product(collect(i), high, low, PLAIN)
        if n == 0:
            total[...] = term
        else:
            total[...] += term


def far_kernel(
    place, near, e_high, e_low, far_high, far_low, block_high, block_low, small,
    g_top, g_bottom, e0_top, e0_bottom, e1_top, e1_bottom,
    w_high, w_low, g_high, g_low, base, first, bound, partial,
    total, g_far, e_far, chunk, panels, sems,
):
    odd, major, minor, is_first, is_last = (place[i] for i in range(5))
    rows = g_far.shape[0]
    panel = rows * SIDE
    half = rows // 2
    arrow = small.shape[0] // 3
    split = (panel - rows) // 2
    copies = [
        (g_top, g_far.at[pl.ds(0, half)]),
        (g_bottom, g_far.at[pl.ds(half, half)]),
        (e0_top, e_far.at[pl.ds(0, half)]),
        (e0_bottom, e_far.at[pl.ds(half, half)]),
        (e1_top, e_far.at[pl.ds(rows, split)]),
        (e1_bottom, e_far.at[pl.ds(rows + split, split)]),
    ]
    copies = [pltpu.make_async_copy(x, y, sems.at[n]) for n, (x, y) in enumerate(copies)]
    for copy in copies:
        copy.start()

    for i in range(SIDE):
        cols = slice(rows * i, rows * (i + 1))
        start = cell_start(odd, i, minor, rows)
        panels[:, cols] = small[: 2 * arrow, pl.ds(start, rows)]
        start = cell_start(odd, major, i, rows)
        bound[:, cols] = jnp.where(is_last != 0, small[2 * arrow :, pl.ds(start, rows)], 0.0)
    first[...] = jnp.where(is_first != 0, panels[arrow:, :], 0.0)

    def target(j):
        return pl.ds(pl.multiple_of((minor + j) % SIDE * rows, rows), rows)

    for n, j in enumerate((0, 1, 3)):
        g_high[target(j), :] = block_high[rows * n : rows * (n + 1), :]
        g_low[target(j), :] = block_low[rows * n : rows * (n + 1), :]

    copies[0].wait()
    copies[1].wait()
    for i in range(SIDE):
        start = cell_start(odd, i, minor, rows)
        high, low = halves(g_far[:, pl.ds(start, rows)])
        g_high[target(2), rows * i : rows * (i + 1)] = high
        g_low[target(2), rows * i : rows * (i + 1)] = low
    base[...] = product(panels[:arrow, :], g_high[...], g_low[...], TURNED)

    def collect(i):
        for c in range(SIDE):
            start = cell_start(odd, (major + i) % SIDE, (minor + c) % SIDE, rows)
            chunk[:, rows * c : rows * (c + 1)] = g_far[:, pl.ds(start, rows)]
        return chunk[...]

    far = None
    for n, i in enumerate((0, 1, 3)):
        span = slice(panel * n, panel * (n + 1))
        term = product(collect(i), e_high[span, :], e_low[span, :], PLAIN)
        far = term if far is None else far + term
    for copy in copies[2:]:
        copy.wait()
    high, low = halves(e_far[...])
    far = far + product(collect(2), high, low, PLAIN)

    def one(x, y):
        return lax.dot_general(x, y, (PLAIN, ((), ())), preferred_element_type=f32)

    total[...] = near[...] + (one(far_high[...], high) + (one(far_high[...], low) + one(far_low[...], high)))
    for n, j in enumerate((0, 1, 3)):
        part_high, part_low = halves(total[rows * n : rows * (n + 1), :])
        w_high[target(j), :] = part_high
        w_low[target(j), :] = part_low
    part_high, part_low = halves(far)
    w_high[target(2), :] = part_high
    w_low[target(2), :] = part_low
    partial[...] = base[...] - product(first[...], w_high[...], w_low[...], TURNED)


def forward_kernel(flag, old, r0, r1, r2, r3, base, w_high, w_low, new, partial):
    arrived = (r0[...] + r1[...]) + (r2[...] + r3[...])
    new[...] = jnp.where(flag[0] != 0, arrived, old[...])
    partial[...] = base[...] - product(new[...], w_high[...], w_low[...], TURNED)


def turn_kernel(place, own, r1, r2, r3, tip, bound, w_high, w_low, rows_out, tip_term, combined, partial):
    arrow_panel = (own[...] + r1[...]) + (r2[...] + r3[...])
    panel_high, panel_low = halves(arrow_panel)
    tip_term[...] = product(tip[...], panel_high, panel_low, PLAIN)
    combined[...] = tip_term[...] + bound[...]
    partial[...] = -product(combined[...], w_high[...], w_low[...], PLAIN)
    width = rows_out.shape[1]
    minor = place[2]
    chosen = arrow_panel[:, :width]
    for j in range(1, SIDE):
        chosen = jnp.where(minor == j, arrow_panel[:, width * j : width * (j + 1)], chosen)
    rows_out[...] = chosen


def backward_kernel(flag, old, r0, r1, r2, r3, tip_term, w_high, w_low, new, partial):
    arrived = (r0[...] + r1[...]) + (r2[...] + r3[...])
    new[...] = jnp.where(flag[0] != 0, tip_term[...] + arrived, old[...])
    partial[...] = -product(new[...], w_high[...], w_low[...], PLAIN)


def closing_kernel(place, flag, old, r0, r1, r2, r3, tip_term, g_high, g_low, p0, p1, p2, p3, scratch):
    arrived = (r0[...] + r1[...]) + (r2[...] + r3[...])
    combined = jnp.where(flag[0] != 0, tip_term[...] + arrived, old[...])
    scratch[...] = -product(combined, g_high[...], g_low[...], PLAIN)
    width = p0.shape[1]
    major = place[1]
    for k, out in enumerate((p0, p1, p2, p3)):
        start = pl.multiple_of((major + k) % SIDE * width, width)
        out[...] = scratch[:, pl.ds(start, width)]


def call(kernel, scalars, arrays, outs, scratch=(), anywhere=()):
    smem = pl.BlockSpec(memory_space=pltpu.SMEM)
    vmem = pl.BlockSpec(memory_space=pltpu.VMEM)
    return pl.pallas_call(
        kernel,
        out_shape=[jax.ShapeDtypeStruct(shape, dtype) for shape, dtype in outs],
        in_specs=[smem] * len(scalars) + [vmem] * len(arrays)
        + [pl.BlockSpec(memory_space=pl.ANY)] * len(anywhere),
        out_specs=[vmem] * len(outs),
        scratch_shapes=list(scratch),
        compiler_params=pltpu.CompilerParams(vmem_limit_bytes=VMEM_LIMIT),
    )(*scalars, *arrays, *anywhere)


def on_device(ginv, couple, arrow_rhs, arrow_in, tip_cov, bnd_next):
    g_rows = ginv[0]
    e_rows = couple[0]
    rows = g_rows.shape[0]
    panel = rows * SIDE
    arrow = arrow_in.shape[0]
    step = lax.axis_index("dom")
    spot = lax.axis_index("blk")
    odd = step % 2
    z, y = spot // SIDE, spot % SIDE
    major = jnp.where(odd == 0, z, y)
    minor = jnp.where(odd == 0, y, z)
    place = jnp.stack([odd, major, minor, step == 0, step == STEPS - 1]).astype(jnp.int32)
    wide = ((arrow, panel), f32)
    narrow = ((arrow, rows), f32)
    half_block = ((panel, panel), bf16)

    small = jnp.concatenate([arrow_rhs[0], arrow_in, bnd_next])
    small = lax.all_gather(small, "blk", axis=1, tiled=True)

    pieces = call(pieces_kernel, [place], [e_rows], [((rows, panel), f32)] * SIDE)
    got = {k: permuted(pieces[k], by_minor(k)) for k in FARTHEST_FIRST[:-1]}
    own0 = pieces[0]
    after0, before0 = ring_near(own0, by_major)
    g_rows, got[2] = lax.optimization_barrier((g_rows, got[2]))
    own1 = jnp.concatenate([got[3], got[2], got[1]])
    g_after, g_before = ring_near(g_rows, by_minor)
    after1, before1 = ring_near(own1, by_major)
    e0_far = ring_far(after0, before0, by_major)
    g_far = ring_far(g_after, g_before, by_minor)
    e1_far = ring_far(after1, before1, by_major)

    three = panel - rows
    near = call(
        near_kernel,
        [place],
        [],
        [((three, panel), f32)]
        + [((3 * panel, panel), bf16)] * 2
        + [((three, panel), bf16)] * 4,
        [
            pltpu.VMEM((three, panel * SIDE), f32),
            pltpu.VMEM((3 * panel, panel), f32),
            pltpu.VMEM((three, panel), f32),
            pltpu.SemaphoreType.DMA((9,)),
        ],
        [g_rows, g_after, g_before, own0, own1, after0, after1, before0, before1],
    )
    w_high, w_low, g_high, g_low, base, incoming, bound, partial = call(
        far_kernel,
        [place],
        [*near, small],
        [half_block] * 4 + [wide] * 4,
        [
            pltpu.VMEM((three, panel), f32),
            pltpu.VMEM((rows, panel * SIDE), f32),
            pltpu.VMEM((panel, panel), f32),
            pltpu.VMEM((rows, panel), f32),
            pltpu.VMEM((2 * arrow, panel), f32),
            pltpu.SemaphoreType.DMA((6,)),
        ],
        [*g_far, *e0_far, *e1_far],
    )
    for s in range(STEPS - 1):
        arrived = [permuted(partial, to_next(s, k)) for k in FARTHEST_FIRST]
        flag = (step == s + 1).astype(jnp.int32)[None]
        incoming, partial = call(
            forward_kernel, [flag], [incoming, *arrived, base, w_high, w_low], [wide] * 2
        )
    arrived = [permuted(partial, by_minor(k)) for k in FARTHEST_FIRST[:-1]]
    arrow_local, tip_term, combined, partial = call(
        turn_kernel,
        [place],
        [partial, *arrived, tip_cov, bound, w_high, w_low],
        [narrow] + [wide] * 3,
    )
    for s in range(STEPS - 1, 0, -1):
        arrived = [permuted(partial, to_earlier(s, k)) for k in FARTHEST_FIRST]
        flag = (step == s - 1).astype(jnp.int32)[None]
        if s > 1:
            combined, partial = call(
                backward_kernel, [flag], [combined, *arrived, tip_term, w_high, w_low], [wide] * 2
            )
    parts = call(
        closing_kernel,
        [place, flag],
        [combined, *arrived, tip_term, g_high, g_low],
        [narrow] * SIDE,
        [pltpu.VMEM(*wide)],
    )
    covariance = parts[0]
    for k in FARTHEST_FIRST[:-1]:
        covariance = covariance + permuted(parts[k], by_major(k))
    return (arrow_local[None], covariance[None])


def solution(mesh):
    return jax.shard_map(
        on_device,
        mesh=mesh,
        in_specs=(
            P("dom", "blk", None),
            P("dom", "blk", None),
            P("dom", None, "blk"),
            P(None, "blk"),
            P(),
            P(None, "blk"),
        ),
        out_specs=(P("dom", None, "blk"), P("dom", None, "blk")),
        check_vma=False,
    )
```

```python
import jax
import jax.numpy as jnp
from jax import lax
from jax.experimental import pallas as pl
from jax.experimental.pallas import tpu as pltpu
from jax.sharding import PartitionSpec as P

both = ("dom", "blk")
SIDE = 4
STEPS = 8
FARTHEST_FIRST = (2, 1, 3, 0)
FORM_VMEM = 16 * 1024 * 1024
STEP_VMEM = 6 * 1024 * 1024
f32 = jnp.float32
bf16 = jnp.bfloat16


def device_of(t, z, y):
    return t * SIDE * SIDE + (z % SIDE) * SIDE + y % SIDE


def pairs(target, steps):
    return [
        (device_of(t, z, y), device_of(*target(t, z, y)))
        for t in steps
        for z in range(SIDE)
        for y in range(SIDE)
    ]


def by_minor(k):
    return pairs(lambda t, z, y: (t, z + k * (t % 2), y + k * (1 - t % 2)), range(STEPS))


def by_major(k):
    return pairs(lambda t, z, y: (t, z + k * (1 - t % 2), y + k * (t % 2)), range(STEPS))


def together(s, groups):
    return next(group for group in groups if s in group)


def to_next(s, k):
    along_z = s % 2
    steps = together(s, ((0, 4), (2, 6), (1, 3, 5)))
    return pairs(lambda t, z, y: (t + 1, z + k * along_z, y + k * (1 - along_z)), steps)


def to_earlier(s, k):
    along_z = 1 - s % 2
    steps = together(s, ((7, 3), (5, 1), (6, 4, 2)))
    return pairs(lambda t, z, y: (t - 1, z + k * along_z, y + k * (1 - along_z)), steps)


def permuted(value, where):
    return lax.ppermute(value, both, where)


def ring_near(block, where):
    return permuted(block, where(-1)), permuted(block, where(1))


def ring_far(after, before, where):
    half = after.shape[0] // 2
    return permuted(before[:half], where(1)), permuted(after[half:], where(-1))


def halves(value):
    high = value.astype(bf16)
    return high, (value - high.astype(f32)).astype(bf16)


def product(a, b_high, b_low, dims):
    a_high, a_low = halves(a)

    def one(x, y):
        return lax.dot_general(x, y, (dims, ((), ())), preferred_element_type=f32)

    return one(a_high, b_high) + (one(a_high, b_low) + one(a_low, b_high))


PLAIN = ((1,), (0,))
TURNED = ((1,), (1,))


def cell_start(odd, i, j, rows):
    cell = jnp.where(odd != 0, SIDE * j + i, SIDE * i + j)
    return pl.multiple_of(cell * rows, rows)


def pieces_kernel(place, e_ref, *outs):
    rows = e_ref.shape[0]
    odd, minor = place[0], place[2]
    for k in range(SIDE):
        for i in range(SIDE):
            start = cell_start(odd, i, (minor + k) % SIDE, rows)
            outs[k][:, rows * i : rows * (i + 1)] = e_ref[:, pl.ds(start, rows)]


def near_kernel(
    place, g_own, g_after, g_before, e_own, e_after, e_before,
    total, e_high, e_low, far_high, far_low, block_high, block_low, g_near, e_near, chunk, sems,
):
    odd, major, minor = place[0], place[1], place[2]
    rows = g_own.shape[0]
    panel = rows * SIDE
    copies = []
    for n, source in enumerate((g_own, g_after, g_before)):
        copies.append((source, g_near.at[pl.ds(rows * n, rows)]))
    for n, source in enumerate((e_own, e_after, e_before)):
        copies.append((source, e_near.at[pl.ds(panel * n, panel)]))
    copies = [pltpu.make_async_copy(x, y, sems.at[n]) for n, (x, y) in enumerate(copies)]
    for copy in copies:
        copy.start()
    for copy in copies[:3]:
        copy.wait()

    def collect(i):
        for c in range(SIDE):
            start = cell_start(odd, (major + i) % SIDE, (minor + c) % SIDE, rows)
            chunk[:, rows * c : rows * (c + 1)] = g_near[:, pl.ds(start, rows)]
        return chunk[...]

    high, low = halves(collect(2))
    far_high[...] = high
    far_low[...] = low
    for i in range(SIDE):
        start = cell_start(odd, i, minor, rows)
        high, low = halves(g_near[:, pl.ds(start, rows)])
        block_high[:, rows * i : rows * (i + 1)] = high
        block_low[:, rows * i : rows * (i + 1)] = low
    for n, i in enumerate((0, 1, 3)):
        copies[3 + n].wait()
        span = slice(panel * n, panel * (n + 1))
        high, low = halves(e_near[span, :])
        e_high[span, :] = high
        e_low[span, :] = low
        term = product(collect(i), high, low, PLAIN)
        if n == 0:
            total[...] = term
        else:
            total[...] += term


def far_kernel(
    place, near, e_high, e_low, far_high, far_low, block_high, block_low, small,
    g_top, g_bottom, e_top, e_bottom,
    w_high, w_low, g_high, g_low, base, first, bound, partial,
    total, g_far, e_far, chunk, panels, sems,
):
    odd, major, minor, is_first, is_last = (place[i] for i in range(5))
    rows = g_far.shape[0]
    panel = rows * SIDE
    half = rows // 2
    arrow = small.shape[0] // 3
    copies = [
        (g_top, g_far.at[pl.ds(0, half)]),
        (g_bottom, g_far.at[pl.ds(half, half)]),
        (e_top, e_far.at[pl.ds(0, panel // 2)]),
        (e_bottom, e_far.at[pl.ds(panel // 2, panel // 2)]),
    ]
    copies = [pltpu.make_async_copy(x, y, sems.at[n]) for n, (x, y) in enumerate(copies)]
    for copy in copies:
        copy.start()

    for i in range(SIDE):
        cols = slice(rows * i, rows * (i + 1))
        start = cell_start(odd, i, minor, rows)
        panels[:, cols] = small[: 2 * arrow, pl.ds(start, rows)]
        start = cell_start(odd, major, i, rows)
        bound[:, cols] = jnp.where(is_last != 0, small[2 * arrow :, pl.ds(start, rows)], 0.0)
    first[...] = jnp.where(is_first != 0, panels[arrow:, :], 0.0)

    def target(j):
        return pl.ds(pl.multiple_of((minor + j) % SIDE * rows, rows), rows)

    for n, j in enumerate((0, 1, 3)):
        g_high[target(j), :] = block_high[rows * n : rows * (n + 1), :]
        g_low[target(j), :] = block_low[rows * n : rows * (n + 1), :]

    copies[0].wait()
    copies[1].wait()
    for i in range(SIDE):
        start = cell_start(odd, i, minor, rows)
        high, low = halves(g_far[:, pl.ds(start, rows)])
        g_high[target(2), rows * i : rows * (i + 1)] = high
        g_low[target(2), rows * i : rows * (i + 1)] = low
    base[...] = product(panels[:arrow, :], g_high[...], g_low[...], TURNED)

    def collect(i):
        for c in range(SIDE):
            start = cell_start(odd, (major + i) % SIDE, (minor + c) % SIDE, rows)
            chunk[:, rows * c : rows * (c + 1)] = g_far[:, pl.ds(start, rows)]
        return chunk[...]

    far = None
    for n, i in enumerate((0, 1, 3)):
        span = slice(panel * n, panel * (n + 1))
        term = product(collect(i), e_high[span, :], e_low[span, :], PLAIN)
        far = term if far is None else far + term
    for copy in copies[2:]:
        copy.wait()
    high, low = halves(e_far[...])
    far = far + product(collect(2), high, low, PLAIN)

    def one(x, y):
        return lax.dot_general(x, y, (PLAIN, ((), ())), preferred_element_type=f32)

    total[...] = near[...] + (one(far_high[...], high) + (one(far_high[...], low) + one(far_low[...], high)))
    for n, j in enumerate((0, 1, 3)):
        part_high, part_low = halves(total[rows * n : rows * (n + 1), :])
        w_high[target(j), :] = part_high
        w_low[target(j), :] = part_low
    part_high, part_low = halves(far)
    w_high[target(2), :] = part_high
    w_low[target(2), :] = part_low
    partial[...] = base[...] - product(first[...], w_high[...], w_low[...], TURNED)


def forward_kernel(flag, old, r0, r1, r2, r3, base, w_high, w_low, new, partial):
    arrived = (r0[...] + r1[...]) + (r2[...] + r3[...])
    new[...] = jnp.where(flag[0] != 0, arrived, old[...])
    partial[...] = base[...] - product(new[...], w_high[...], w_low[...], TURNED)


def turn_kernel(place, own, r1, r2, r3, tip, bound, w_high, w_low, rows_out, tip_term, combined, partial):
    arrow_panel = (own[...] + r1[...]) + (r2[...] + r3[...])
    panel_high, panel_low = halves(arrow_panel)
    tip_term[...] = product(tip[...], panel_high, panel_low, PLAIN)
    combined[...] = tip_term[...] + bound[...]
    partial[...] = -product(combined[...], w_high[...], w_low[...], PLAIN)
    width = rows_out.shape[1]
    minor = place[2]
    chosen = arrow_panel[:, :width]
    for j in range(1, SIDE):
        chosen = jnp.where(minor == j, arrow_panel[:, width * j : width * (j + 1)], chosen)
    rows_out[...] = chosen


def backward_kernel(flag, old, r0, r1, r2, r3, tip_term, w_high, w_low, new, partial):
    arrived = (r0[...] + r1[...]) + (r2[...] + r3[...])
    new[...] = jnp.where(flag[0] != 0, tip_term[...] + arrived, old[...])
    partial[...] = -product(new[...], w_high[...], w_low[...], PLAIN)


def closing_kernel(place, flag, old, r0, r1, r2, r3, tip_term, g_high, g_low, p0, p1, p2, p3, scratch):
    arrived = (r0[...] + r1[...]) + (r2[...] + r3[...])
    combined = jnp.where(flag[0] != 0, tip_term[...] + arrived, old[...])
    scratch[...] = -product(combined, g_high[...], g_low[...], PLAIN)
    width = p0.shape[1]
    major = place[1]
    for k, out in enumerate((p0, p1, p2, p3)):
        start = pl.multiple_of((major + k) % SIDE * width, width)
        out[...] = scratch[:, pl.ds(start, width)]


def call(kernel, scalars, arrays, outs, scratch=(), anywhere=(), vmem=STEP_VMEM):
    smem = pl.BlockSpec(memory_space=pltpu.SMEM)
    held = pl.BlockSpec(memory_space=pltpu.VMEM)
    return pl.pallas_call(
        kernel,
        out_shape=[jax.ShapeDtypeStruct(shape, dtype) for shape, dtype in outs],
        in_specs=[smem] * len(scalars) + [held] * len(arrays)
        + [pl.BlockSpec(memory_space=pl.ANY)] * len(anywhere),
        out_specs=[held] * len(outs),
        scratch_shapes=list(scratch),
        compiler_params=pltpu.CompilerParams(vmem_limit_bytes=vmem),
    )(*scalars, *arrays, *anywhere)


def on_device(ginv, couple, arrow_rhs, arrow_in, tip_cov, bnd_next):
    g_rows = ginv[0]
    e_rows = couple[0]
    rows = g_rows.shape[0]
    panel = rows * SIDE
    arrow = arrow_in.shape[0]
    step = lax.axis_index("dom")
    spot = lax.axis_index("blk")
    odd = step % 2
    z, y = spot // SIDE, spot % SIDE
    major = jnp.where(odd == 0, z, y)
    minor = jnp.where(odd == 0, y, z)
    place = jnp.stack([odd, major, minor, step == 0, step == STEPS - 1]).astype(jnp.int32)
    wide = ((arrow, panel), f32)
    narrow = ((arrow, rows), f32)
    half_block = ((panel, panel), bf16)

    small = jnp.concatenate([arrow_rhs[0], arrow_in, bnd_next])
    small = lax.all_gather(small, "blk", axis=1, tiled=True)

    pieces = call(pieces_kernel, [place], [e_rows], [((rows, panel), f32)] * SIDE)
    got = {k: permuted(pieces[k], by_minor(k)) for k in FARTHEST_FIRST[:-1]}
    g_rows, got[2] = lax.optimization_barrier((g_rows, got[2]))
    e_own = jnp.concatenate([pieces[0], got[3], got[2], got[1]])
    g_after, g_before = ring_near(g_rows, by_minor)
    e_after, e_before = ring_near(e_own, by_major)
    g_far = ring_far(g_after, g_before, by_minor)
    e_far = ring_far(e_after, e_before, by_major)

    three = panel - rows
    near = call(
        near_kernel,
        [place],
        [],
        [((three, panel), f32)]
        + [((3 * panel, panel), bf16)] * 2
        + [((three, panel), bf16)] * 4,
        [
            pltpu.VMEM((three, panel * SIDE), f32),
            pltpu.VMEM((3 * panel, panel), f32),
            pltpu.VMEM((three, panel), f32),
            pltpu.SemaphoreType.DMA((6,)),
        ],
        [g_rows, g_after, g_before, e_own, e_after, e_before],
        vmem=FORM_VMEM,
    )
    w_high, w_low, g_high, g_low, base, incoming, bound, partial = call(
        far_kernel,
        [place],
        [*near, small],
        [half_block] * 4 + [wide] * 4,
        [
            pltpu.VMEM((three, panel), f32),
            pltpu.VMEM((rows, panel * SIDE), f32),
            pltpu.VMEM((panel, panel), f32),
            pltpu.VMEM((rows, panel), f32),
            pltpu.VMEM((2 * arrow, panel), f32),
            pltpu.SemaphoreType.DMA((4,)),
        ],
        [*g_far, *e_far],
        vmem=FORM_VMEM,
    )
    for s in range(STEPS - 1):
        arrived = [permuted(partial, to_next(s, k)) for k in FARTHEST_FIRST]
        flag = (step == s + 1).astype(jnp.int32)[None]
        incoming, partial = call(
            forward_kernel, [flag], [incoming, *arrived, base, w_high, w_low], [wide] * 2
        )
    arrived = [permuted(partial, by_minor(k)) for k in FARTHEST_FIRST[:-1]]
    arrow_local, tip_term, combined, partial = call(
        turn_kernel,
        [place],
        [partial, *arrived, tip_cov, bound, w_high, w_low],
        [narrow] + [wide] * 3,
    )
    for s in range(STEPS - 1, 0, -1):
        arrived = [permuted(partial, to_earlier(s, k)) for k in FARTHEST_FIRST]
        flag = (step == s - 1).astype(jnp.int32)[None]
        if s > 1:
            combined, partial = call(
                backward_kernel, [flag], [combined, *arrived, tip_term, w_high, w_low], [wide] * 2
            )
    parts = call(
        closing_kernel,
        [place, flag],
        [combined, *arrived, tip_term, g_high, g_low],
        [narrow] * SIDE,
        [pltpu.VMEM(*wide)],
    )
    covariance = parts[0]
    for k in FARTHEST_FIRST[:-1]:
        covariance = covariance + permuted(parts[k], by_major(k))
    return (arrow_local[None], covariance[None])


def solution(mesh):
    return jax.shard_map(
        on_device,
        mesh=mesh,
        in_specs=(
            P("dom", "blk", None),
            P("dom", "blk", None),
            P("dom", None, "blk"),
            P(None, "blk"),
            P(),
            P(None, "blk"),
        ),
        out_specs=(P("dom", None, "blk"), P("dom", None, "blk")),
        check_vma=False,
    )
```

```python
import jax
import jax.numpy as jnp
from jax import lax
from jax.experimental import pallas as pl
from jax.experimental.pallas import tpu as pltpu
from jax.sharding import PartitionSpec as P

both = ("dom", "blk")
SIDE = 4
STEPS = 8
FARTHEST_FIRST = (2, 1, 3, 0)
FORM_VMEM = 16 * 1024 * 1024
STEP_VMEM = 6 * 1024 * 1024
f32 = jnp.float32
bf16 = jnp.bfloat16


def device_of(t, z, y):
    return t * SIDE * SIDE + (z % SIDE) * SIDE + y % SIDE


def pairs(target, steps):
    return [
        (device_of(t, z, y), device_of(*target(t, z, y)))
        for t in steps
        for z in range(SIDE)
        for y in range(SIDE)
    ]


def by_minor(k):
    return pairs(lambda t, z, y: (t, z + k * (t % 2), y + k * (1 - t % 2)), range(STEPS))


def by_major(k):
    return pairs(lambda t, z, y: (t, z + k * (1 - t % 2), y + k * (t % 2)), range(STEPS))


def together(s, groups):
    return next(group for group in groups if s in group)


def to_next(s, k):
    along_z = s % 2
    steps = together(s, ((0, 4), (2, 6), (1, 3, 5)))
    return pairs(lambda t, z, y: (t + 1, z + k * along_z, y + k * (1 - along_z)), steps)


def to_earlier(s, k):
    along_z = 1 - s % 2
    steps = together(s, ((7, 3), (5, 1), (6, 2), (4,)))
    return pairs(lambda t, z, y: (t - 1, z + k * along_z, y + k * (1 - along_z)), steps)


def permuted(value, where):
    return lax.ppermute(value, both, where)


def ring_near(block, where):
    return permuted(block, where(-1)), permuted(block, where(1))


def ring_far(after, before, where):
    half = after.shape[0] // 2
    return permuted(before[:half], where(1)), permuted(after[half:], where(-1))


def halves(value):
    high = value.astype(bf16)
    return high, (value - high.astype(f32)).astype(bf16)


def product(a, b_high, b_low, dims):
    a_high, a_low = halves(a)

    def one(x, y):
        return lax.dot_general(x, y, (dims, ((), ())), preferred_element_type=f32)

    return one(a_high, b_high) + (one(a_high, b_low) + one(a_low, b_high))


PLAIN = ((1,), (0,))
TURNED = ((1,), (1,))


def cell_start(odd, i, j, rows):
    cell = jnp.where(odd != 0, SIDE * j + i, SIDE * i + j)
    return pl.multiple_of(cell * rows, rows)


def pieces_kernel(place, e_ref, rhs, entering, bnd, p0, p1, p2, p3, extra):
    rows = e_ref.shape[0]
    odd, minor = place[0], place[2]
    tail = bnd.shape[0] // SIDE
    for i in range(SIDE):
        cols = slice(rows * i, rows * (i + 1))
        for k, out in enumerate((p0, p1, p2, p3)):
            start = cell_start(odd, i, (minor + k) % SIDE, rows)
            out[:rows, cols] = e_ref[:, pl.ds(start, rows)]
            if k:
                out[rows:, cols] = bnd[tail * i : tail * (i + 1), :]
        source = rhs if i < SIDE // 2 else entering
        top = 2 * tail * (i % (SIDE // 2))
        extra[:, cols] = source[top : top + 2 * tail, :]


def spread_panel(out, source, top, height, start, rows):
    cols = pl.ds(pl.multiple_of(start, rows), rows)
    for q in range(SIDE):
        out[height * q : height * (q + 1), cols] = source[top : top + height, rows * q : rows * (q + 1)]


def near_kernel(
    place, bnd, g_own, g_after, g_before, e_own, e_after, e_before, got1, got2, got3,
    total, e_high, e_low, far_high, far_low, block_high, block_low, panels, bound,
    g_near, e_near, chunk, extra, tails, sems,
):
    odd, major, minor, is_last = place[0], place[1], place[2], place[4]
    rows = g_own.shape[0]
    panel = rows * SIDE
    lead, tail = extra.shape[0] // 3, tails.shape[0] // 3
    copies = []
    for n, source in enumerate((g_own, g_after, g_before)):
        copies.append((source, g_near.at[pl.ds(rows * n, rows)]))
    for n, source in enumerate((e_own, e_after, e_before)):
        copies.append((source.at[pl.ds(0, panel)], e_near.at[pl.ds(panel * n, panel)]))
    for n, source in enumerate((e_own, e_after, e_before)):
        copies.append((source.at[pl.ds(panel, lead)], extra.at[pl.ds(lead * n, lead)]))
    for n, source in enumerate((got1, got2, got3)):
        copies.append((source.at[pl.ds(rows, tail)], tails.at[pl.ds(tail * n, tail)]))
    copies = [pltpu.make_async_copy(x, y, sems.at[n]) for n, (x, y) in enumerate(copies)]
    for copy in copies:
        copy.start()
    for copy in copies[:3]:
        copy.wait()

    def collect(i):
        for c in range(SIDE):
            start = cell_start(odd, (major + i) % SIDE, (minor + c) % SIDE, rows)
            chunk[:, rows * c : rows * (c + 1)] = g_near[:, pl.ds(start, rows)]
        return chunk[...]

    high, low = halves(collect(2))
    far_high[...] = high
    far_low[...] = low
    for i in range(SIDE):
        start = cell_start(odd, i, minor, rows)
        high, low = halves(g_near[:, pl.ds(start, rows)])
        block_high[:, rows * i : rows * (i + 1)] = high
        block_low[:, rows * i : rows * (i + 1)] = low
    for n, i in enumerate((0, 1, 3)):
        copies[3 + n].wait()
        span = slice(panel * n, panel * (n + 1))
        high, low = halves(e_near[span, :])
        e_high[span, :] = high
        e_low[span, :] = low
        term = product(collect(i), high, low, PLAIN)
        if n == 0:
            total[...] = term
        else:
            total[...] += term

    for copy in copies[6:]:
        copy.wait()
    for n, i in enumerate((0, 1, 3)):
        spread_panel(panels, extra, lead * n, lead, (major + i) % SIDE * rows, rows)
    spread_panel(panels, extra, 0, lead, (major + 2) % SIDE * rows, rows)
    keep = is_last != 0
    bound[:, pl.ds(pl.multiple_of(minor * rows, rows), rows)] = jnp.where(keep, bnd[...], 0.0)
    for n in range(3):
        spot = (minor - n + SIDE - 1) % SIDE * rows
        spread_panel(bound, tails, tail * n, tail, spot, rows)
    bound[...] = jnp.where(keep, bound[...], 0.0)


def far_kernel(
    place, near, e_high, e_low, far_high, far_low, block_high, block_low, panels_near,
    g_top, g_bottom, e_top, e_bottom,
    w_high, w_low, base, partial, g_high_out, g_low_out,
    total, g_far, e_far, chunk, panels, g_high, g_low, sems,
):
    odd, major, minor, is_first = (place[i] for i in range(4))
    rows = g_far.shape[0]
    panel = rows * SIDE
    half = rows // 2
    lead = e_far.shape[0] - panel
    arrow = panels.shape[0] // 2
    edge = e_far.shape[0] // 2
    copies = [
        (g_top, g_far.at[pl.ds(0, half)]),
        (g_bottom, g_far.at[pl.ds(half, half)]),
        (e_top, e_far.at[pl.ds(0, edge)]),
        (e_bottom, e_far.at[pl.ds(edge, edge)]),
    ]
    copies = [pltpu.make_async_copy(x, y, sems.at[n]) for n, (x, y) in enumerate(copies)]
    for copy in copies:
        copy.start()
    panels[...] = panels_near[...]

    def target(j):
        return pl.ds(pl.multiple_of((minor + j) % SIDE * rows, rows), rows)

    for n, j in enumerate((0, 1, 3)):
        g_high[target(j), :] = block_high[rows * n : rows * (n + 1), :]
        g_low[target(j), :] = block_low[rows * n : rows * (n + 1), :]

    copies[0].wait()
    copies[1].wait()
    for i in range(SIDE):
        start = cell_start(odd, i, minor, rows)
        high, low = halves(g_far[:, pl.ds(start, rows)])
        g_high[target(2), rows * i : rows * (i + 1)] = high
        g_low[target(2), rows * i : rows * (i + 1)] = low
    kept = [
        pltpu.make_async_copy(g_high, g_high_out, sems.at[4]),
        pltpu.make_async_copy(g_low, g_low_out, sems.at[5]),
    ]
    for copy in kept:
        copy.start()

    def collect(i):
        for c in range(SIDE):
            start = cell_start(odd, (major + i) % SIDE, (minor + c) % SIDE, rows)
            chunk[:, rows * c : rows * (c + 1)] = g_far[:, pl.ds(start, rows)]
        return chunk[...]

    far = None
    for n, i in enumerate((0, 1, 3)):
        span = slice(panel * n, panel * (n + 1))
        term = product(collect(i), e_high[span, :], e_low[span, :], PLAIN)
        far = term if far is None else far + term
    for copy in copies[2:]:
        copy.wait()
    high, low = halves(e_far[:panel, :])
    far = far + product(collect(2), high, low, PLAIN)

    def one(x, y):
        return lax.dot_general(x, y, (PLAIN, ((), ())), preferred_element_type=f32)

    total[...] = near[...] + (one(far_high[...], high) + (one(far_high[...], low) + one(far_low[...], high)))
    for n, j in enumerate((0, 1, 3)):
        part_high, part_low = halves(total[rows * n : rows * (n + 1), :])
        w_high[target(j), :] = part_high
        w_low[target(j), :] = part_low
    part_high, part_low = halves(far)
    w_high[target(2), :] = part_high
    w_low[target(2), :] = part_low
    spread_panel(panels, e_far, panel, lead, (major + 2) % SIDE * rows, rows)
    base[...] = product(panels[:arrow, :], g_high[...], g_low[...], TURNED)
    first = jnp.where(is_first != 0, panels[arrow:, :], 0.0)
    partial[...] = base[...] - product(first, w_high[...], w_low[...], TURNED)
    for copy in kept:
        copy.wait()


def forward_kernel(flag, old, r0, r1, r2, r3, base, w_high, w_low, partial):
    @pl.when(flag[0] != 0)
    def _():
        arrived = (r0[...] + r1[...]) + (r2[...] + r3[...])
        partial[...] = base[...] - product(arrived, w_high[...], w_low[...], TURNED)

    @pl.when(flag[0] == 0)
    def _():
        partial[...] = old[...]


def turn_kernel(place, own, r1, r2, r3, tip, bound, w_high, w_low, rows_out, tip_term, combined, partial):
    arrow_panel = (own[...] + r1[...]) + (r2[...] + r3[...])
    panel_high, panel_low = halves(arrow_panel)
    tip_term[...] = product(tip[...], panel_high, panel_low, PLAIN)
    combined[...] = tip_term[...] + bound[...]
    partial[...] = -product(combined[...], w_high[...], w_low[...], PLAIN)
    width = rows_out.shape[1]
    minor = place[2]
    chosen = arrow_panel[:, :width]
    for j in range(1, SIDE):
        chosen = jnp.where(minor == j, arrow_panel[:, width * j : width * (j + 1)], chosen)
    rows_out[...] = chosen


def backward_kernel(flag, old, r0, r1, r2, r3, tip_term, w_high, w_low, combined, partial):
    @pl.when(flag[0] != 0)
    def _():
        combined[...] = tip_term[...] + ((r0[...] + r1[...]) + (r2[...] + r3[...]))
        partial[...] = -product(combined[...], w_high[...], w_low[...], PLAIN)

    @pl.when(flag[0] == 0)
    def _():
        combined[...] = old[...]
        partial[...] = jnp.zeros_like(partial)


def closing_kernel(
    place, flag, old, r0, r1, r2, r3, tip_term, g_high_in, g_low_in, p0, p1, p2, p3, scratch, g_high, g_low, sems
):
    copies = [
        pltpu.make_async_copy(g_high_in, g_high, sems.at[0]),
        pltpu.make_async_copy(g_low_in, g_low, sems.at[1]),
    ]
    for copy in copies:
        copy.start()
    arrived = (r0[...] + r1[...]) + (r2[...] + r3[...])
    combined = jnp.where(flag[0] != 0, tip_term[...] + arrived, old[...])
    for copy in copies:
        copy.wait()
    scratch[...] = -product(combined, g_high[...], g_low[...], PLAIN)
    width = p0.shape[1]
    major = place[1]
    for k, out in enumerate((p0, p1, p2, p3)):
        start = pl.multiple_of((major + k) % SIDE * width, width)
        out[...] = scratch[:, pl.ds(start, width)]


def call(kernel, scalars, arrays, outs, scratch=(), anywhere=(), vmem=STEP_VMEM, far_outs=()):
    smem = pl.BlockSpec(memory_space=pltpu.SMEM)
    held = pl.BlockSpec(memory_space=pltpu.VMEM)
    return pl.pallas_call(
        kernel,
        out_shape=[jax.ShapeDtypeStruct(shape, dtype) for shape, dtype in [*outs, *far_outs]],
        in_specs=[smem] * len(scalars) + [held] * len(arrays)
        + [pl.BlockSpec(memory_space=pl.ANY)] * len(anywhere),
        out_specs=[held] * len(outs) + [pl.BlockSpec(memory_space=pltpu.HBM)] * len(far_outs),
        scratch_shapes=list(scratch),
        compiler_params=pltpu.CompilerParams(vmem_limit_bytes=vmem),
    )(*scalars, *arrays, *anywhere)


def on_device(ginv, couple, arrow_rhs, arrow_in, tip_cov, bnd_next):
    g_rows = ginv[0]
    e_rows = couple[0]
    rows = g_rows.shape[0]
    panel = rows * SIDE
    arrow = arrow_in.shape[0]
    step = lax.axis_index("dom")
    spot = lax.axis_index("blk")
    odd = step % 2
    z, y = spot // SIDE, spot % SIDE
    major = jnp.where(odd == 0, z, y)
    minor = jnp.where(odd == 0, y, z)
    place = jnp.stack([odd, major, minor, step == 0, step == STEPS - 1]).astype(jnp.int32)
    wide = ((arrow, panel), f32)
    narrow = ((arrow, rows), f32)
    half_block = ((panel, panel), bf16)

    tail = arrow // SIDE
    lead = 2 * tail
    *pieces, extra = call(
        pieces_kernel,
        [place],
        [e_rows, arrow_rhs[0], arrow_in, bnd_next],
        [((rows, panel), f32)] + [((rows + tail, panel), f32)] * 3 + [((lead, panel), f32)],
    )
    got = {k: permuted(pieces[k], by_minor(k)) for k in FARTHEST_FIRST[:-1]}
    g_rows, got[2] = lax.optimization_barrier((g_rows, got[2]))
    e_own = jnp.concatenate([pieces[0], got[3][:rows], got[2][:rows], got[1][:rows], extra])
    g_after, g_before = ring_near(g_rows, by_minor)
    e_after, e_before = ring_near(e_own, by_major)
    g_far = ring_far(g_after, g_before, by_minor)
    e_far = ring_far(e_after, e_before, by_major)

    three = panel - rows
    *near, bound = call(
        near_kernel,
        [place],
        [bnd_next],
        [((three, panel), f32)]
        + [((3 * panel, panel), bf16)] * 2
        + [((three, panel), bf16)] * 4
        + [((2 * arrow, panel), f32), wide],
        [
            pltpu.VMEM((three, panel * SIDE), f32),
            pltpu.VMEM((3 * panel, panel), f32),
            pltpu.VMEM((three, panel), f32),
            pltpu.VMEM((3 * lead, panel), f32),
            pltpu.VMEM((3 * tail, panel), f32),
            pltpu.SemaphoreType.DMA((12,)),
        ],
        [g_rows, g_after, g_before, e_own, e_after, e_before, got[1], got[2], got[3]],
        vmem=FORM_VMEM,
    )
    w_high, w_low, base, partial, g_high, g_low = call(
        far_kernel,
        [place],
        near,
        [half_block] * 2 + [wide] * 2,
        [
            pltpu.VMEM((three, panel), f32),
            pltpu.VMEM((rows, panel * SIDE), f32),
            pltpu.VMEM((panel + lead, panel), f32),
            pltpu.VMEM((rows, panel), f32),
            pltpu.VMEM((2 * arrow, panel), f32),
            pltpu.VMEM((panel, panel), bf16),
            pltpu.VMEM((panel, panel), bf16),
            pltpu.SemaphoreType.DMA((6,)),
        ],
        [*g_far, *e_far],
        vmem=FORM_VMEM,
        far_outs=[half_block] * 2,
    )
    for s in range(STEPS - 1):
        arrived = [permuted(partial, to_next(s, k)) for k in FARTHEST_FIRST]
        flag = (step == s + 1).astype(jnp.int32)[None]
        (partial,) = call(forward_kernel, [flag], [partial, *arrived, base, w_high, w_low], [wide])
    arrived = [permuted(partial, by_minor(k)) for k in FARTHEST_FIRST[:-1]]
    arrow_local, tip_term, combined, partial = call(
        turn_kernel,
        [place],
        [partial, *arrived, tip_cov, bound, w_high, w_low],
        [narrow] + [wide] * 3,
    )
    for s in range(STEPS - 1, 0, -1):
        arrived = [permuted(partial, to_earlier(s, k)) for k in FARTHEST_FIRST]
        flag = (step == s - 1).astype(jnp.int32)[None]
        if s > 1:
            combined, partial = call(
                backward_kernel, [flag], [combined, *arrived, tip_term, w_high, w_low], [wide] * 2
            )
    parts = call(
        closing_kernel,
        [place, flag],
        [combined, *arrived, tip_term],
        [narrow] * SIDE,
        [
            pltpu.VMEM(*wide),
            pltpu.VMEM((panel, panel), bf16),
            pltpu.VMEM((panel, panel), bf16),
            pltpu.SemaphoreType.DMA((2,)),
        ],
        [g_high, g_low],
    )
    covariance = parts[0]
    for k in FARTHEST_FIRST[:-1]:
        covariance = covariance + permuted(parts[k], by_major(k))
    return (arrow_local[None], covariance[None])


def solution(mesh):
    return jax.shard_map(
        on_device,
        mesh=mesh,
        in_specs=(
            P("dom", "blk", None),
            P("dom", "blk", None),
            P("dom", None, "blk"),
            P(None, "blk"),
            P(),
            P(None, "blk"),
        ),
        out_specs=(P("dom", None, "blk"), P("dom", None, "blk")),
        check_vma=False,
    )
```

```python
import jax
import jax.numpy as jnp
from jax import lax
from jax.experimental import pallas as pl
from jax.experimental.pallas import tpu as pltpu
from jax.sharding import PartitionSpec as P

both = ("dom", "blk")
SIDE = 4
STEPS = 8
FARTHEST_FIRST = (2, 1, 3, 0)
FORM_VMEM = 16 * 1024 * 1024
STEP_VMEM = 6 * 1024 * 1024
f32 = jnp.float32
bf16 = jnp.bfloat16


def device_of(t, z, y):
    return t * SIDE * SIDE + (z % SIDE) * SIDE + y % SIDE


def pairs(target, steps):
    return [
        (device_of(t, z, y), device_of(*target(t, z, y)))
        for t in steps
        for z in range(SIDE)
        for y in range(SIDE)
    ]


def by_minor(k):
    return pairs(lambda t, z, y: (t, z + k * (t % 2), y + k * (1 - t % 2)), range(STEPS))


def by_major(k):
    return pairs(lambda t, z, y: (t, z + k * (1 - t % 2), y + k * (t % 2)), range(STEPS))


def together(s, groups):
    return next(group for group in groups if s in group)


def to_next(s, k):
    along_z = s % 2
    steps = together(s, ((0, 4), (2, 6), (1, 5), (3,)))
    return pairs(lambda t, z, y: (t + 1, z + k * along_z, y + k * (1 - along_z)), steps)


def to_earlier(s, k):
    along_z = 1 - s % 2
    steps = together(s, ((7, 3), (5, 1), (6, 4, 2)))
    return pairs(lambda t, z, y: (t - 1, z + k * along_z, y + k * (1 - along_z)), steps)


def permuted(value, where):
    return lax.ppermute(value, both, where)


def ring_near(block, where):
    return permuted(block, where(-1)), permuted(block, where(1))


def ring_far(after, before, where):
    half = after.shape[0] // 2
    return permuted(before[:half], where(1)), permuted(after[half:], where(-1))


def halves(value):
    high = value.astype(bf16)
    return high, (value - high.astype(f32)).astype(bf16)


def product(a, b_high, b_low, dims):
    a_high, a_low = halves(a)

    def one(x, y):
        return lax.dot_general(x, y, (dims, ((), ())), preferred_element_type=f32)

    return one(a_high, b_high) + (one(a_high, b_low) + one(a_low, b_high))


PLAIN = ((1,), (0,))
TURNED = ((1,), (1,))


def cell_start(odd, i, j, rows):
    cell = jnp.where(odd != 0, SIDE * j + i, SIDE * i + j)
    return pl.multiple_of(cell * rows, rows)


def pieces_kernel(
    place, e_in, rhs_in, entering_in, bnd_in, p0, p1, p2, p3, extra, e_ref, rhs, entering, bnd, sems
):
    sources, targets = (rhs_in, entering_in, bnd_in, e_in), (rhs, entering, bnd, e_ref)
    copies = [pltpu.make_async_copy(x, y, sems.at[n]) for n, (x, y) in enumerate(zip(sources, targets))]
    for copy in copies:
        copy.start()
    for copy in copies:
        copy.wait()
    rows = e_ref.shape[0]
    odd, minor = place[0], place[2]
    tail = bnd.shape[0] // SIDE
    for i in range(SIDE):
        cols = slice(rows * i, rows * (i + 1))
        for k, out in enumerate((p0, p1, p2, p3)):
            start = cell_start(odd, i, (minor + k) % SIDE, rows)
            out[:rows, cols] = e_ref[:, pl.ds(start, rows)]
            if k:
                out[rows:, cols] = bnd[tail * i : tail * (i + 1), :]
        source = rhs if i < SIDE // 2 else entering
        top = 2 * tail * (i % (SIDE // 2))
        extra[:, cols] = source[top : top + 2 * tail, :]


def spread_panel(out, source, top, height, start, rows):
    cols = pl.ds(pl.multiple_of(start, rows), rows)
    for q in range(SIDE):
        out[height * q : height * (q + 1), cols] = source[top : top + height, rows * q : rows * (q + 1)]


def near_kernel(
    place, bnd, g_own, g_after, g_before, e_own, e_after, e_before, got1, got2, got3,
    total, e_high, e_low, far_high, far_low, block_high, block_low, panels, bound,
    g_near, e_near, chunk, extra, tails, sems,
):
    odd, major, minor, is_last = place[0], place[1], place[2], place[4]
    rows = g_own.shape[0]
    panel = rows * SIDE
    lead, tail = extra.shape[0] // 3, tails.shape[0] // 3
    copies = []
    for n, source in enumerate((g_own, g_after, g_before)):
        copies.append((source, g_near.at[pl.ds(rows * n, rows)]))
    for n, source in enumerate((e_own, e_after, e_before)):
        copies.append((source.at[pl.ds(0, panel)], e_near.at[pl.ds(panel * n, panel)]))
    for n, source in enumerate((e_own, e_after, e_before)):
        copies.append((source.at[pl.ds(panel, lead)], extra.at[pl.ds(lead * n, lead)]))
    for n, source in enumerate((got1, got2, got3)):
        copies.append((source.at[pl.ds(rows, tail)], tails.at[pl.ds(tail * n, tail)]))
    copies = [pltpu.make_async_copy(x, y, sems.at[n]) for n, (x, y) in enumerate(copies)]
    for copy in copies:
        copy.start()
    for copy in copies[:3]:
        copy.wait()

    def collect(i):
        for c in range(SIDE):
            start = cell_start(odd, (major + i) % SIDE, (minor + c) % SIDE, rows)
            chunk[:, rows * c : rows * (c + 1)] = g_near[:, pl.ds(start, rows)]
        return chunk[...]

    high, low = halves(collect(2))
    far_high[...] = high
    far_low[...] = low
    for i in range(SIDE):
        start = cell_start(odd, i, minor, rows)
        high, low = halves(g_near[:, pl.ds(start, rows)])
        block_high[:, rows * i : rows * (i + 1)] = high
        block_low[:, rows * i : rows * (i + 1)] = low
    for n, i in enumerate((0, 1, 3)):
        copies[3 + n].wait()
        span = slice(panel * n, panel * (n + 1))
        high, low = halves(e_near[span, :])
        e_high[span, :] = high
        e_low[span, :] = low
        term = product(collect(i), high, low, PLAIN)
        if n == 0:
            total[...] = term
        else:
            total[...] += term

    for copy in copies[6:]:
        copy.wait()
    for n, i in enumerate((0, 1, 3)):
        spread_panel(panels, extra, lead * n, lead, (major + i) % SIDE * rows, rows)
    spread_panel(panels, extra, 0, lead, (major + 2) % SIDE * rows, rows)
    keep = is_last != 0
    bound[:, pl.ds(pl.multiple_of(minor * rows, rows), rows)] = jnp.where(keep, bnd[...], 0.0)
    for n in range(3):
        spot = (minor - n + SIDE - 1) % SIDE * rows
        spread_panel(bound, tails, tail * n, tail, spot, rows)
    bound[...] = jnp.where(keep, bound[...], 0.0)


def far_kernel(
    place, near, e_high, e_low, far_high, far_low, block_high, block_low, panels_near,
    g_top, g_bottom, e_top, e_bottom,
    w_high, w_low, base, partial, g_high_out, g_low_out,
    total, g_far, e_far, chunk, panels, g_high, g_low, sems,
):
    odd, major, minor, is_first = (place[i] for i in range(4))
    rows = g_far.shape[0]
    panel = rows * SIDE
    half = rows // 2
    lead = e_far.shape[0] - panel
    arrow = panels.shape[0] // 2
    edge = e_far.shape[0] // 2
    copies = [
        (g_top, g_far.at[pl.ds(0, half)]),
        (g_bottom, g_far.at[pl.ds(half, half)]),
        (e_top, e_far.at[pl.ds(0, edge)]),
        (e_bottom, e_far.at[pl.ds(edge, edge)]),
    ]
    copies = [pltpu.make_async_copy(x, y, sems.at[n]) for n, (x, y) in enumerate(copies)]
    for copy in copies:
        copy.start()
    panels[...] = panels_near[...]

    def target(j):
        return pl.ds(pl.multiple_of((minor + j) % SIDE * rows, rows), rows)

    for n, j in enumerate((0, 1, 3)):
        g_high[target(j), :] = block_high[rows * n : rows * (n + 1), :]
        g_low[target(j), :] = block_low[rows * n : rows * (n + 1), :]

    copies[0].wait()
    copies[1].wait()
    for i in range(SIDE):
        start = cell_start(odd, i, minor, rows)
        high, low = halves(g_far[:, pl.ds(start, rows)])
        g_high[target(2), rows * i : rows * (i + 1)] = high
        g_low[target(2), rows * i : rows * (i + 1)] = low
    kept = [
        pltpu.make_async_copy(g_high, g_high_out, sems.at[4]),
        pltpu.make_async_copy(g_low, g_low_out, sems.at[5]),
    ]
    for copy in kept:
        copy.start()

    def collect(i):
        for c in range(SIDE):
            start = cell_start(odd, (major + i) % SIDE, (minor + c) % SIDE, rows)
            chunk[:, rows * c : rows * (c + 1)] = g_far[:, pl.ds(start, rows)]
        return chunk[...]

    far = None
    for n, i in enumerate((0, 1, 3)):
        span = slice(panel * n, panel * (n + 1))
        term = product(collect(i), e_high[span, :], e_low[span, :], PLAIN)
        far = term if far is None else far + term
    for copy in copies[2:]:
        copy.wait()
    high, low = halves(e_far[:panel, :])
    far = far + product(collect(2), high, low, PLAIN)

    def one(x, y):
        return lax.dot_general(x, y, (PLAIN, ((), ())), preferred_element_type=f32)

    total[...] = near[...] + (one(far_high[...], high) + (one(far_high[...], low) + one(far_low[...], high)))
    for n, j in enumerate((0, 1, 3)):
        part_high, part_low = halves(total[rows * n : rows * (n + 1), :])
        w_high[target(j), :] = part_high
        w_low[target(j), :] = part_low
    part_high, part_low = halves(far)
    w_high[target(2), :] = part_high
    w_low[target(2), :] = part_low
    spread_panel(panels, e_far, panel, lead, (major + 2) % SIDE * rows, rows)
    base[...] = product(panels[:arrow, :], g_high[...], g_low[...], TURNED)
    first = jnp.where(is_first != 0, panels[arrow:, :], 0.0)
    partial[...] = base[...] - product(first, w_high[...], w_low[...], TURNED)
    for copy in kept:
        copy.wait()


def forward_kernel(flag, old, r0, r1, r2, r3, base, w_high, w_low, partial):
    @pl.when(flag[0] != 0)
    def _():
        arrived = (r0[...] + r1[...]) + (r2[...] + r3[...])
        partial[...] = base[...] - product(arrived, w_high[...], w_low[...], TURNED)

    @pl.when(flag[0] == 0)
    def _():
        partial[...] = old[...]


def turn_kernel(place, own, r1, r2, r3, tip, bound, w_high, w_low, rows_out, tip_term, combined, partial):
    arrow_panel = (own[...] + r1[...]) + (r2[...] + r3[...])
    panel_high, panel_low = halves(arrow_panel)
    tip_term[...] = product(tip[...], panel_high, panel_low, PLAIN)
    combined[...] = tip_term[...] + bound[...]
    partial[...] = -product(combined[...], w_high[...], w_low[...], PLAIN)
    width = rows_out.shape[1]
    minor = place[2]
    chosen = arrow_panel[:, :width]
    for j in range(1, SIDE):
        chosen = jnp.where(minor == j, arrow_panel[:, width * j : width * (j + 1)], chosen)
    rows_out[...] = chosen


def backward_kernel(flag, old, r0, r1, r2, r3, tip_term, w_high, w_low, combined, partial):
    @pl.when(flag[0] != 0)
    def _():
        combined[...] = tip_term[...] + ((r0[...] + r1[...]) + (r2[...] + r3[...]))
        partial[...] = -product(combined[...], w_high[...], w_low[...], PLAIN)

    @pl.when(flag[0] == 0)
    def _():
        combined[...] = old[...]
        partial[...] = jnp.zeros_like(partial)


def closing_kernel(
    place, flag, old, r0, r1, r2, r3, tip_term, g_high_in, g_low_in, p0, p1, p2, p3, scratch, g_high, g_low, sems
):
    copies = [
        pltpu.make_async_copy(g_high_in, g_high, sems.at[0]),
        pltpu.make_async_copy(g_low_in, g_low, sems.at[1]),
    ]
    for copy in copies:
        copy.start()
    arrived = (r0[...] + r1[...]) + (r2[...] + r3[...])
    combined = jnp.where(flag[0] != 0, tip_term[...] + arrived, old[...])
    for copy in copies:
        copy.wait()
    scratch[...] = -product(combined, g_high[...], g_low[...], PLAIN)
    width = p0.shape[1]
    major = place[1]
    for k, out in enumerate((p0, p1, p2, p3)):
        start = pl.multiple_of((major + k) % SIDE * width, width)
        out[...] = scratch[:, pl.ds(start, width)]


def call(kernel, scalars, arrays, outs, scratch=(), anywhere=(), vmem=STEP_VMEM, far_outs=()):
    smem = pl.BlockSpec(memory_space=pltpu.SMEM)
    held = pl.BlockSpec(memory_space=pltpu.VMEM)
    return pl.pallas_call(
        kernel,
        out_shape=[jax.ShapeDtypeStruct(shape, dtype) for shape, dtype in [*outs, *far_outs]],
        in_specs=[smem] * len(scalars) + [held] * len(arrays)
        + [pl.BlockSpec(memory_space=pl.ANY)] * len(anywhere),
        out_specs=[held] * len(outs) + [pl.BlockSpec(memory_space=pltpu.HBM)] * len(far_outs),
        scratch_shapes=list(scratch),
        compiler_params=pltpu.CompilerParams(vmem_limit_bytes=vmem),
    )(*scalars, *arrays, *anywhere)


def on_device(ginv, couple, arrow_rhs, arrow_in, tip_cov, bnd_next):
    g_rows = ginv[0]
    e_rows = couple[0]
    rows = g_rows.shape[0]
    panel = rows * SIDE
    arrow = arrow_in.shape[0]
    step = lax.axis_index("dom")
    spot = lax.axis_index("blk")
    odd = step % 2
    z, y = spot // SIDE, spot % SIDE
    major = jnp.where(odd == 0, z, y)
    minor = jnp.where(odd == 0, y, z)
    place = jnp.stack([odd, major, minor, step == 0, step == STEPS - 1]).astype(jnp.int32)
    wide = ((arrow, panel), f32)
    narrow = ((arrow, rows), f32)
    half_block = ((panel, panel), bf16)

    tail = arrow // SIDE
    lead = 2 * tail
    *pieces, extra = call(
        pieces_kernel,
        [place],
        [],
        [((rows, panel), f32)] + [((rows + tail, panel), f32)] * 3 + [((lead, panel), f32)],
        [pltpu.VMEM((rows, panel * SIDE), f32)]
        + [pltpu.VMEM((arrow, rows), f32)] * 3
        + [pltpu.SemaphoreType.DMA((4,))],
        [e_rows, arrow_rhs[0], arrow_in, bnd_next],
    )
    got = {k: permuted(pieces[k], by_minor(k)) for k in FARTHEST_FIRST[:-1]}
    g_after = permuted(g_rows, by_minor(-1))
    g_later, got[2] = lax.optimization_barrier((g_rows, got[2]))
    g_before = permuted(g_later, by_minor(1))
    e_own = jnp.concatenate([pieces[0], got[3][:rows], got[2][:rows], got[1][:rows], extra])
    e_after, e_before = ring_near(e_own, by_major)
    g_far = ring_far(g_after, g_before, by_minor)
    e_far = ring_far(e_after, e_before, by_major)

    three = panel - rows
    *near, bound = call(
        near_kernel,
        [place],
        [bnd_next],
        [((three, panel), f32)]
        + [((3 * panel, panel), bf16)] * 2
        + [((three, panel), bf16)] * 4
        + [((2 * arrow, panel), f32), wide],
        [
            pltpu.VMEM((three, panel * SIDE), f32),
            pltpu.VMEM((3 * panel, panel), f32),
            pltpu.VMEM((three, panel), f32),
            pltpu.VMEM((3 * lead, panel), f32),
            pltpu.VMEM((3 * tail, panel), f32),
            pltpu.SemaphoreType.DMA((12,)),
        ],
        [g_rows, g_after, g_before, e_own, e_after, e_before, got[1], got[2], got[3]],
        vmem=FORM_VMEM,
    )
    w_high, w_low, base, partial, g_high, g_low = call(
        far_kernel,
        [place],
        near,
        [half_block] * 2 + [wide] * 2,
        [
            pltpu.VMEM((three, panel), f32),
            pltpu.VMEM((rows, panel * SIDE), f32),
            pltpu.VMEM((panel + lead, panel), f32),
            pltpu.VMEM((rows, panel), f32),
            pltpu.VMEM((2 * arrow, panel), f32),
            pltpu.VMEM((panel, panel), bf16),
            pltpu.VMEM((panel, panel), bf16),
            pltpu.SemaphoreType.DMA((6,)),
        ],
        [*g_far, *e_far],
        vmem=FORM_VMEM,
        far_outs=[half_block] * 2,
    )
    for s in range(STEPS - 1):
        arrived = [permuted(partial, to_next(s, k)) for k in FARTHEST_FIRST]
        flag = (step == s + 1).astype(jnp.int32)[None]
        (partial,) = call(forward_kernel, [flag], [partial, *arrived, base, w_high, w_low], [wide])
    arrived = [permuted(partial, by_minor(k)) for k in FARTHEST_FIRST[:-1]]
    arrow_local, tip_term, combined, partial = call(
        turn_kernel,
        [place],
        [partial, *arrived, tip_cov, bound, w_high, w_low],
        [narrow] + [wide] * 3,
    )
    for s in range(STEPS - 1, 0, -1):
        arrived = [permuted(partial, to_earlier(s, k)) for k in FARTHEST_FIRST]
        flag = (step == s - 1).astype(jnp.int32)[None]
        if s > 1:
            combined, partial = call(
                backward_kernel, [flag], [combined, *arrived, tip_term, w_high, w_low], [wide] * 2
            )
    parts = call(
        closing_kernel,
        [place, flag],
        [combined, *arrived, tip_term],
        [narrow] * SIDE,
        [
            pltpu.VMEM(*wide),
            pltpu.VMEM((panel, panel), bf16),
            pltpu.VMEM((panel, panel), bf16),
            pltpu.SemaphoreType.DMA((2,)),
        ],
        [g_high, g_low],
    )
    covariance = parts[0]
    for k in FARTHEST_FIRST[:-1]:
        covariance = covariance + permuted(parts[k], by_major(k))
    return (arrow_local[None], covariance[None])


def solution(mesh):
    return jax.shard_map(
        on_device,
        mesh=mesh,
        in_specs=(
            P("dom", "blk", None),
            P("dom", "blk", None),
            P("dom", None, "blk"),
            P(None, "blk"),
            P(),
            P(None, "blk"),
        ),
        out_specs=(P("dom", None, "blk"), P("dom", None, "blk")),
        check_vma=False,
    )
```

```python
import jax
import jax.numpy as jnp
from jax import lax
from jax.experimental import pallas as pl
from jax.experimental.pallas import tpu as pltpu
from jax.sharding import PartitionSpec as P

both = ("dom", "blk")
SIDE = 4
STEPS = 8
FARTHEST_FIRST = (2, 1, 3, 0)
FORM_VMEM = 16 * 1024 * 1024
STEP_VMEM = 6 * 1024 * 1024
f32 = jnp.float32
bf16 = jnp.bfloat16


def device_of(t, z, y):
    return t * SIDE * SIDE + (z % SIDE) * SIDE + y % SIDE


def pairs(target, steps):
    return [
        (device_of(t, z, y), device_of(*target(t, z, y)))
        for t in steps
        for z in range(SIDE)
        for y in range(SIDE)
    ]


def by_minor(k):
    return pairs(lambda t, z, y: (t, z + k * (t % 2), y + k * (1 - t % 2)), range(STEPS))


def by_major(k):
    return pairs(lambda t, z, y: (t, z + k * (1 - t % 2), y + k * (t % 2)), range(STEPS))


def together(s, groups):
    return next(group for group in groups if s in group)


def to_next(s, k):
    along_z = s % 2
    steps = together(s, ((0, 4), (2, 6), (1, 5), (3,)))
    return pairs(lambda t, z, y: (t + 1, z + k * along_z, y + k * (1 - along_z)), steps)


def to_earlier(s, k):
    along_z = 1 - s % 2
    evens = ((6, 4, 2),) if k < 2 else ((6, 2), (4,))
    steps = together(s, ((7, 3), (5, 1), *evens))
    return pairs(lambda t, z, y: (t - 1, z + k * along_z, y + k * (1 - along_z)), steps)


def permuted(value, where):
    return lax.ppermute(value, both, where)


def ring_near(block, where):
    return permuted(block, where(-1)), permuted(block, where(1))


def ring_far(after, before, where):
    half = after.shape[0] // 2
    return permuted(before[:half], where(1)), permuted(after[half:], where(-1))


def halves(value):
    high = value.astype(bf16)
    return high, (value - high.astype(f32)).astype(bf16)


def product(a, b_high, b_low, dims):
    a_high, a_low = halves(a)

    def one(x, y):
        return lax.dot_general(x, y, (dims, ((), ())), preferred_element_type=f32)

    return one(a_high, b_high) + (one(a_high, b_low) + one(a_low, b_high))


PLAIN = ((1,), (0,))
TURNED = ((1,), (1,))


def cell_start(odd, i, j, rows):
    cell = jnp.where(odd != 0, SIDE * j + i, SIDE * i + j)
    return pl.multiple_of(cell * rows, rows)


def pieces_kernel(
    place, e_in, rhs_in, entering_in, bnd_in, p0, p1, p2, p3, extra, e_ref, rhs, entering, bnd, sems
):
    sources, targets = (rhs_in, entering_in, bnd_in, e_in), (rhs, entering, bnd, e_ref)
    copies = [pltpu.make_async_copy(x, y, sems.at[n]) for n, (x, y) in enumerate(zip(sources, targets))]
    for copy in copies:
        copy.start()
    for copy in copies:
        copy.wait()
    rows = e_ref.shape[0]
    odd, minor = place[0], place[2]
    tail = bnd.shape[0] // SIDE
    for i in range(SIDE):
        cols = slice(rows * i, rows * (i + 1))
        for k, out in enumerate((p0, p1, p2, p3)):
            start = cell_start(odd, i, (minor + k) % SIDE, rows)
            out[:rows, cols] = e_ref[:, pl.ds(start, rows)]
            if k:
                out[rows:, cols] = bnd[tail * i : tail * (i + 1), :]
        source = rhs if i < SIDE // 2 else entering
        top = 2 * tail * (i % (SIDE // 2))
        extra[:, cols] = source[top : top + 2 * tail, :]


def spread_panel(out, source, top, height, start, rows):
    cols = pl.ds(pl.multiple_of(start, rows), rows)
    for q in range(SIDE):
        out[height * q : height * (q + 1), cols] = source[top : top + height, rows * q : rows * (q + 1)]


def near_kernel(
    place, bnd, g_own, after_top, after_bottom, before_top, before_bottom,
    e_own, e_after, e_before, got1, got2, got3,
    total, e_high, e_low, far_high, far_low, block_high, block_low, panels, bound,
    g_near, e_near, chunk, extra, tails, sems,
):
    odd, major, minor, is_last = place[0], place[1], place[2], place[4]
    rows = g_own.shape[0]
    panel = rows * SIDE
    lead, tail = extra.shape[0] // 3, tails.shape[0] // 3
    half = rows // 2
    copies = [(g_own, g_near.at[pl.ds(0, rows)])]
    for n, source in enumerate((after_top, after_bottom, before_top, before_bottom)):
        copies.append((source, g_near.at[pl.ds(rows + half * n, half)]))
    for n, source in enumerate((e_own, e_after, e_before)):
        copies.append((source.at[pl.ds(0, panel)], e_near.at[pl.ds(panel * n, panel)]))
    for n, source in enumerate((e_own, e_after, e_before)):
        copies.append((source.at[pl.ds(panel, lead)], extra.at[pl.ds(lead * n, lead)]))
    for n, source in enumerate((got1, got2, got3)):
        copies.append((source.at[pl.ds(rows, tail)], tails.at[pl.ds(tail * n, tail)]))
    copies = [pltpu.make_async_copy(x, y, sems.at[n]) for n, (x, y) in enumerate(copies)]
    for copy in copies:
        copy.start()
    for copy in copies[:5]:
        copy.wait()

    def collect(i):
        for c in range(SIDE):
            start = cell_start(odd, (major + i) % SIDE, (minor + c) % SIDE, rows)
            chunk[:, rows * c : rows * (c + 1)] = g_near[:, pl.ds(start, rows)]
        return chunk[...]

    high, low = halves(collect(2))
    far_high[...] = high
    far_low[...] = low
    for i in range(SIDE):
        start = cell_start(odd, i, minor, rows)
        high, low = halves(g_near[:, pl.ds(start, rows)])
        block_high[:, rows * i : rows * (i + 1)] = high
        block_low[:, rows * i : rows * (i + 1)] = low
    for n, i in enumerate((0, 1, 3)):
        copies[5 + n].wait()
        span = slice(panel * n, panel * (n + 1))
        high, low = halves(e_near[span, :])
        e_high[span, :] = high
        e_low[span, :] = low
        term = product(collect(i), high, low, PLAIN)
        if n == 0:
            total[...] = term
        else:
            total[...] += term

    for copy in copies[8:]:
        copy.wait()
    for n, i in enumerate((0, 1, 3)):
        spread_panel(panels, extra, lead * n, lead, (major + i) % SIDE * rows, rows)
    spread_panel(panels, extra, 0, lead, (major + 2) % SIDE * rows, rows)
    keep = is_last != 0
    bound[:, pl.ds(pl.multiple_of(minor * rows, rows), rows)] = jnp.where(keep, bnd[...], 0.0)
    for n in range(3):
        spot = (minor - n + SIDE - 1) % SIDE * rows
        spread_panel(bound, tails, tail * n, tail, spot, rows)
    bound[...] = jnp.where(keep, bound[...], 0.0)


def far_kernel(
    place, near, e_high, e_low, far_high, far_low, block_high, block_low, panels_near,
    g_top, g_bottom, e_top, e_bottom,
    w_high, w_low, base, partial, g_high_out, g_low_out,
    total, g_far, e_far, chunk, panels, g_high, g_low, sems,
):
    odd, major, minor, is_first = (place[i] for i in range(4))
    rows = g_far.shape[0]
    panel = rows * SIDE
    half = rows // 2
    lead = e_far.shape[0] - panel
    arrow = panels.shape[0] // 2
    edge = e_far.shape[0] // 2
    copies = [
        (g_top, g_far.at[pl.ds(0, half)]),
        (g_bottom, g_far.at[pl.ds(half, half)]),
        (e_top, e_far.at[pl.ds(0, edge)]),
        (e_bottom, e_far.at[pl.ds(edge, edge)]),
    ]
    copies = [pltpu.make_async_copy(x, y, sems.at[n]) for n, (x, y) in enumerate(copies)]
    for copy in copies:
        copy.start()
    panels[...] = panels_near[...]

    def target(j):
        return pl.ds(pl.multiple_of((minor + j) % SIDE * rows, rows), rows)

    for n, j in enumerate((0, 1, 3)):
        g_high[target(j), :] = block_high[rows * n : rows * (n + 1), :]
        g_low[target(j), :] = block_low[rows * n : rows * (n + 1), :]

    copies[0].wait()
    copies[1].wait()
    for i in range(SIDE):
        start = cell_start(odd, i, minor, rows)
        high, low = halves(g_far[:, pl.ds(start, rows)])
        g_high[target(2), rows * i : rows * (i + 1)] = high
        g_low[target(2), rows * i : rows * (i + 1)] = low
    kept = [
        pltpu.make_async_copy(g_high, g_high_out, sems.at[4]),
        pltpu.make_async_copy(g_low, g_low_out, sems.at[5]),
    ]
    for copy in kept:
        copy.start()

    def collect(i):
        for c in range(SIDE):
            start = cell_start(odd, (major + i) % SIDE, (minor + c) % SIDE, rows)
            chunk[:, rows * c : rows * (c + 1)] = g_far[:, pl.ds(start, rows)]
        return chunk[...]

    far = None
    for n, i in enumerate((0, 1, 3)):
        span = slice(panel * n, panel * (n + 1))
        term = product(collect(i), e_high[span, :], e_low[span, :], PLAIN)
        far = term if far is None else far + term
    for copy in copies[2:]:
        copy.wait()
    high, low = halves(e_far[:panel, :])
    far = far + product(collect(2), high, low, PLAIN)

    def one(x, y):
        return lax.dot_general(x, y, (PLAIN, ((), ())), preferred_element_type=f32)

    total[...] = near[...] + (one(far_high[...], high) + (one(far_high[...], low) + one(far_low[...], high)))
    for n, j in enumerate((0, 1, 3)):
        part_high, part_low = halves(total[rows * n : rows * (n + 1), :])
        w_high[target(j), :] = part_high
        w_low[target(j), :] = part_low
    part_high, part_low = halves(far)
    w_high[target(2), :] = part_high
    w_low[target(2), :] = part_low
    spread_panel(panels, e_far, panel, lead, (major + 2) % SIDE * rows, rows)
    base[...] = product(panels[:arrow, :], g_high[...], g_low[...], TURNED)
    first = jnp.where(is_first != 0, panels[arrow:, :], 0.0)
    partial[...] = base[...] - product(first, w_high[...], w_low[...], TURNED)
    for copy in kept:
        copy.wait()


def forward_kernel(flag, old, r0, r1, r2, r3, base, w_high, w_low, partial):
    @pl.when(flag[0] != 0)
    def _():
        arrived = (r0[...] + r1[...]) + (r2[...] + r3[...])
        partial[...] = base[...] - product(arrived, w_high[...], w_low[...], TURNED)

    @pl.when(flag[0] == 0)
    def _():
        partial[...] = old[...]


def turn_kernel(place, own, r1, r2, r3, tip, bound, w_high, w_low, rows_out, tip_term, combined, partial):
    arrow_panel = (own[...] + r1[...]) + (r2[...] + r3[...])
    panel_high, panel_low = halves(arrow_panel)
    tip_term[...] = product(tip[...], panel_high, panel_low, PLAIN)
    combined[...] = tip_term[...] + bound[...]
    partial[...] = -product(combined[...], w_high[...], w_low[...], PLAIN)
    width = rows_out.shape[1]
    minor = place[2]
    chosen = arrow_panel[:, :width]
    for j in range(1, SIDE):
        chosen = jnp.where(minor == j, arrow_panel[:, width * j : width * (j + 1)], chosen)
    rows_out[...] = chosen


def backward_kernel(flag, old, r0, r1, r2, r3, tip_term, w_high, w_low, combined, partial):
    @pl.when(flag[0] != 0)
    def _():
        combined[...] = tip_term[...] + ((r0[...] + r1[...]) + (r2[...] + r3[...]))
        partial[...] = -product(combined[...], w_high[...], w_low[...], PLAIN)

    @pl.when(flag[0] == 0)
    def _():
        combined[...] = old[...]
        partial[...] = jnp.zeros_like(partial)


def closing_kernel(
    place, flag, old, r0, r1, r2, r3, tip_term, g_high_in, g_low_in, p0, p1, p2, p3, scratch, g_high, g_low, sems
):
    copies = [
        pltpu.make_async_copy(g_high_in, g_high, sems.at[0]),
        pltpu.make_async_copy(g_low_in, g_low, sems.at[1]),
    ]
    for copy in copies:
        copy.start()
    arrived = (r0[...] + r1[...]) + (r2[...] + r3[...])
    combined = jnp.where(flag[0] != 0, tip_term[...] + arrived, old[...])
    for copy in copies:
        copy.wait()
    scratch[...] = -product(combined, g_high[...], g_low[...], PLAIN)
    width = p0.shape[1]
    major = place[1]
    for k, out in enumerate((p0, p1, p2, p3)):
        start = pl.multiple_of((major + k) % SIDE * width, width)
        out[...] = scratch[:, pl.ds(start, width)]


def call(kernel, scalars, arrays, outs, scratch=(), anywhere=(), vmem=STEP_VMEM, far_outs=(), space=pl.ANY):
    smem = pl.BlockSpec(memory_space=pltpu.SMEM)
    held = pl.BlockSpec(memory_space=pltpu.VMEM)
    return pl.pallas_call(
        kernel,
        out_shape=[jax.ShapeDtypeStruct(shape, dtype) for shape, dtype in [*outs, *far_outs]],
        in_specs=[smem] * len(scalars) + [held] * len(arrays)
        + [pl.BlockSpec(memory_space=space)] * len(anywhere),
        out_specs=[held] * len(outs) + [pl.BlockSpec(memory_space=pltpu.HBM)] * len(far_outs),
        scratch_shapes=list(scratch),
        compiler_params=pltpu.CompilerParams(vmem_limit_bytes=vmem),
    )(*scalars, *arrays, *anywhere)


def on_device(ginv, couple, arrow_rhs, arrow_in, tip_cov, bnd_next):
    g_rows = ginv[0]
    e_rows = couple[0]
    rows = g_rows.shape[0]
    panel = rows * SIDE
    arrow = arrow_in.shape[0]
    step = lax.axis_index("dom")
    spot = lax.axis_index("blk")
    odd = step % 2
    z, y = spot // SIDE, spot % SIDE
    major = jnp.where(odd == 0, z, y)
    minor = jnp.where(odd == 0, y, z)
    place = jnp.stack([odd, major, minor, step == 0, step == STEPS - 1]).astype(jnp.int32)
    wide = ((arrow, panel), f32)
    narrow = ((arrow, rows), f32)
    half_block = ((panel, panel), bf16)

    tail = arrow // SIDE
    lead = 2 * tail
    *pieces, extra = call(
        pieces_kernel,
        [place],
        [],
        [((rows, panel), f32)] + [((rows + tail, panel), f32)] * 3 + [((lead, panel), f32)],
        [pltpu.VMEM((rows, panel * SIDE), f32)]
        + [pltpu.VMEM((arrow, rows), f32)] * 3
        + [pltpu.SemaphoreType.DMA((4,))],
        [e_rows, arrow_rhs[0], arrow_in, bnd_next],
        space=pltpu.HBM,
    )
    got = {k: permuted(pieces[k], by_minor(k)) for k in FARTHEST_FIRST[:-1]}
    half = rows // 2
    before_top = permuted(g_rows[:half], by_minor(1))
    after_bottom = permuted(g_rows[half:], by_minor(-1))
    e_own = jnp.concatenate([pieces[0], got[3][:rows], got[2][:rows], got[1][:rows], extra])
    e_own, g_later, before_top, after_bottom = lax.optimization_barrier(
        (e_own, g_rows, before_top, after_bottom)
    )
    e_after, e_before = ring_near(e_own, by_major)
    g_far = permuted(before_top, by_minor(1)), permuted(after_bottom, by_minor(-1))
    after_top = permuted(g_later[:half], by_minor(-1))
    before_bottom = permuted(g_later[half:], by_minor(1))
    e_far = ring_far(e_after, e_before, by_major)
    g_near = [g_rows, after_top, after_bottom, before_top, before_bottom]

    three = panel - rows
    *near, bound = call(
        near_kernel,
        [place],
        [bnd_next],
        [((three, panel), f32)]
        + [((3 * panel, panel), bf16)] * 2
        + [((three, panel), bf16)] * 4
        + [((2 * arrow, panel), f32), wide],
        [
            pltpu.VMEM((three, panel * SIDE), f32),
            pltpu.VMEM((3 * panel, panel), f32),
            pltpu.VMEM((three, panel), f32),
            pltpu.VMEM((3 * lead, panel), f32),
            pltpu.VMEM((3 * tail, panel), f32),
            pltpu.SemaphoreType.DMA((14,)),
        ],
        [*g_near, e_own, e_after, e_before, got[1], got[2], got[3]],
        vmem=FORM_VMEM,
    )
    w_high, w_low, base, partial, g_high, g_low = call(
        far_kernel,
        [place],
        near,
        [half_block] * 2 + [wide] * 2,
        [
            pltpu.VMEM((three, panel), f32),
            pltpu.VMEM((rows, panel * SIDE), f32),
            pltpu.VMEM((panel + lead, panel), f32),
            pltpu.VMEM((rows, panel), f32),
            pltpu.VMEM((2 * arrow, panel), f32),
            pltpu.VMEM((panel, panel), bf16),
            pltpu.VMEM((panel, panel), bf16),
            pltpu.SemaphoreType.DMA((6,)),
        ],
        [*g_far, *e_far],
        vmem=FORM_VMEM,
        far_outs=[half_block] * 2,
    )
    for s in range(STEPS - 1):
        arrived = [permuted(partial, to_next(s, k)) for k in FARTHEST_FIRST]
        flag = (step == s + 1).astype(jnp.int32)[None]
        (partial,) = call(forward_kernel, [flag], [partial, *arrived, base, w_high, w_low], [wide])
    arrived = [permuted(partial, by_minor(k)) for k in FARTHEST_FIRST[:-1]]
    arrow_local, tip_term, combined, partial = call(
        turn_kernel,
        [place],
        [partial, *arrived, tip_cov, bound, w_high, w_low],
        [narrow] + [wide] * 3,
    )
    for s in range(STEPS - 1, 0, -1):
        arrived = [permuted(partial, to_earlier(s, k)) for k in FARTHEST_FIRST]
        flag = (step == s - 1).astype(jnp.int32)[None]
        if s > 1:
            combined, partial = call(
                backward_kernel, [flag], [combined, *arrived, tip_term, w_high, w_low], [wide] * 2
            )
    parts = call(
        closing_kernel,
        [place, flag],
        [combined, *arrived, tip_term],
        [narrow] * SIDE,
        [
            pltpu.VMEM(*wide),
            pltpu.VMEM((panel, panel), bf16),
            pltpu.VMEM((panel, panel), bf16),
            pltpu.SemaphoreType.DMA((2,)),
        ],
        [g_high, g_low],
    )
    covariance = parts[0]
    for k in FARTHEST_FIRST[:-1]:
        covariance = covariance + permuted(parts[k], by_major(k))
    return (arrow_local[None], covariance[None])


def solution(mesh):
    return jax.shard_map(
        on_device,
        mesh=mesh,
        in_specs=(
            P("dom", "blk", None),
            P("dom", "blk", None),
            P("dom", None, "blk"),
            P(None, "blk"),
            P(),
            P(None, "blk"),
        ),
        out_specs=(P("dom", None, "blk"), P("dom", None, "blk")),
        check_vma=False,
    )
```

```python
import jax
import jax.numpy as jnp
from jax import lax
from jax.experimental import pallas as pl
from jax.experimental.pallas import tpu as pltpu
from jax.sharding import PartitionSpec as P

both = ("dom", "blk")
SIDE = 4
STEPS = 8
FARTHEST_FIRST = (2, 1, 3, 0)
FORM_VMEM = 16 * 1024 * 1024
STEP_VMEM = 6 * 1024 * 1024
f32 = jnp.float32
bf16 = jnp.bfloat16


def device_of(t, z, y):
    return t * SIDE * SIDE + (z % SIDE) * SIDE + y % SIDE


def pairs(target, steps):
    return [
        (device_of(t, z, y), device_of(*target(t, z, y)))
        for t in steps
        for z in range(SIDE)
        for y in range(SIDE)
    ]


def by_minor(k):
    return pairs(lambda t, z, y: (t, z + k * (t % 2), y + k * (1 - t % 2)), range(STEPS))


def by_major(k):
    return pairs(lambda t, z, y: (t, z + k * (1 - t % 2), y + k * (t % 2)), range(STEPS))


def together(s, groups):
    return next(group for group in groups if s in group)


def in_row(x, k):
    steps = [2 * c for c in together(x, ((0, 2), (1, 3)))]
    return pairs(lambda t, z, y: (t, z, y + k), steps)


def to_next_chip(x, k):
    return pairs(lambda t, z, y: (t + 2, z + k, y), [2 * x])


def to_earlier_chip(x, k):
    return pairs(lambda t, z, y: (t - 2, z + k, y), [2 * c for c in together(x, ((3, 1), (2,)))])


def to_even_core():
    return pairs(lambda t, z, y: (t - 1, z, y), range(1, STEPS, 2))


def to_odd_core():
    return pairs(lambda t, z, y: (t + 1, z, y), range(0, STEPS, 2))


def permuted(value, where):
    return lax.ppermute(value, both, where)


def ring_near(block, where):
    return permuted(block, where(-1)), permuted(block, where(1))


def ring_far(after, before, where):
    half = after.shape[0] // 2
    return permuted(before[:half], where(1)), permuted(after[half:], where(-1))


def halves(value):
    high = value.astype(bf16)
    return high, (value - high.astype(f32)).astype(bf16)


def product(a, b_high, b_low, dims):
    a_high, a_low = halves(a)

    def one(x, y):
        return lax.dot_general(x, y, (dims, ((), ())), preferred_element_type=f32)

    return one(a_high, b_high) + (one(a_high, b_low) + one(a_low, b_high))


PLAIN = ((1,), (0,))
TURNED = ((1,), (1,))


def cell_start(odd, i, j, rows):
    cell = jnp.where(odd != 0, SIDE * j + i, SIDE * i + j)
    return pl.multiple_of(cell * rows, rows)


def pieces_kernel(
    place, e_in, rhs_in, entering_in, bnd_in, p0, p1, p2, p3, extra, e_ref, rhs, entering, bnd, sems
):
    sources, targets = (rhs_in, entering_in, bnd_in, e_in), (rhs, entering, bnd, e_ref)
    copies = [pltpu.make_async_copy(x, y, sems.at[n]) for n, (x, y) in enumerate(zip(sources, targets))]
    for copy in copies:
        copy.start()
    for copy in copies:
        copy.wait()
    rows = e_ref.shape[0]
    odd, minor = place[0], place[2]
    tail = bnd.shape[0] // SIDE
    for i in range(SIDE):
        cols = slice(rows * i, rows * (i + 1))
        for k, out in enumerate((p0, p1, p2, p3)):
            start = cell_start(odd, i, (minor + k) % SIDE, rows)
            out[:rows, cols] = e_ref[:, pl.ds(start, rows)]
            if k:
                out[rows:, cols] = bnd[tail * i : tail * (i + 1), :]
        source = rhs if i < SIDE // 2 else entering
        top = 2 * tail * (i % (SIDE // 2))
        extra[:, cols] = source[top : top + 2 * tail, :]


def spread_panel(out, source, top, height, start, rows):
    cols = pl.ds(pl.multiple_of(start, rows), rows)
    for q in range(SIDE):
        out[height * q : height * (q + 1), cols] = source[top : top + height, rows * q : rows * (q + 1)]


def near_kernel(
    place, bnd, g_own, g_after, g_before, e_own, e_after, e_before, got1, got2, got3,
    total, e_high, e_low, far_high, far_low, block_high, block_low, panels, bound,
    g_near, e_near, chunk, extra, tails, sems,
):
    odd, major, minor, is_last = place[0], place[1], place[2], place[4]
    rows = g_own.shape[0]
    panel = rows * SIDE
    lead, tail = extra.shape[0] // 3, tails.shape[0] // 3
    copies = []
    for n, source in enumerate((g_own, g_after, g_before)):
        copies.append((source, g_near.at[pl.ds(rows * n, rows)]))
    for n, source in enumerate((e_own, e_after, e_before)):
        copies.append((source.at[pl.ds(0, panel)], e_near.at[pl.ds(panel * n, panel)]))
    for n, source in enumerate((e_own, e_after, e_before)):
        copies.append((source.at[pl.ds(panel, lead)], extra.at[pl.ds(lead * n, lead)]))
    for n, source in enumerate((got1, got2, got3)):
        copies.append((source.at[pl.ds(rows, tail)], tails.at[pl.ds(tail * n, tail)]))
    copies = [pltpu.make_async_copy(x, y, sems.at[n]) for n, (x, y) in enumerate(copies)]
    for copy in copies:
        copy.start()
    for copy in copies[:3]:
        copy.wait()

    def collect(i):
        for c in range(SIDE):
            start = cell_start(odd, (major + i) % SIDE, (minor + c) % SIDE, rows)
            chunk[:, rows * c : rows * (c + 1)] = g_near[:, pl.ds(start, rows)]
        return chunk[...]

    high, low = halves(collect(2))
    far_high[...] = high
    far_low[...] = low
    for i in range(SIDE):
        start = cell_start(odd, i, minor, rows)
        high, low = halves(g_near[:, pl.ds(start, rows)])
        block_high[:, rows * i : rows * (i + 1)] = high
        block_low[:, rows * i : rows * (i + 1)] = low
    for n, i in enumerate((0, 1, 3)):
        copies[3 + n].wait()
        span = slice(panel * n, panel * (n + 1))
        high, low = halves(e_near[span, :])
        e_high[span, :] = high
        e_low[span, :] = low
        term = product(collect(i), high, low, PLAIN)
        if n == 0:
            total[...] = term
        else:
            total[...] += term

    for copy in copies[6:]:
        copy.wait()
    for n, i in enumerate((0, 1, 3)):
        spread_panel(panels, extra, lead * n, lead, (major + i) % SIDE * rows, rows)
    spread_panel(panels, extra, 0, lead, (major + 2) % SIDE * rows, rows)
    keep = is_last != 0
    bound[:, pl.ds(pl.multiple_of(minor * rows, rows), rows)] = jnp.where(keep, bnd[...], 0.0)
    for n in range(3):
        spot = (minor - n + SIDE - 1) % SIDE * rows
        spread_panel(bound, tails, tail * n, tail, spot, rows)
    bound[...] = jnp.where(keep, bound[...], 0.0)


def far_kernel(
    place, near, e_high, e_low, far_high, far_low, block_high, block_low, panels_near, bound,
    g_top, g_bottom, e_top, e_bottom,
    w_high, w_low, base, partial, pack, g_high_out, g_low_out,
    total, g_far, e_far, chunk, panels, g_high, g_low, sems,
):
    odd, major, minor, is_first = (place[i] for i in range(4))
    rows = g_far.shape[0]
    panel = rows * SIDE
    half = rows // 2
    lead = e_far.shape[0] - panel
    arrow = panels.shape[0] // 2
    edge = e_far.shape[0] // 2
    copies = [
        (g_top, g_far.at[pl.ds(0, half)]),
        (g_bottom, g_far.at[pl.ds(half, half)]),
        (e_top, e_far.at[pl.ds(0, edge)]),
        (e_bottom, e_far.at[pl.ds(edge, edge)]),
    ]
    copies = [pltpu.make_async_copy(x, y, sems.at[n]) for n, (x, y) in enumerate(copies)]
    for copy in copies:
        copy.start()
    panels[...] = panels_near[...]

    def target(j):
        return pl.ds(pl.multiple_of((minor + j) % SIDE * rows, rows), rows)

    for n, j in enumerate((0, 1, 3)):
        g_high[target(j), :] = block_high[rows * n : rows * (n + 1), :]
        g_low[target(j), :] = block_low[rows * n : rows * (n + 1), :]

    copies[0].wait()
    copies[1].wait()
    for i in range(SIDE):
        start = cell_start(odd, i, minor, rows)
        high, low = halves(g_far[:, pl.ds(start, rows)])
        g_high[target(2), rows * i : rows * (i + 1)] = high
        g_low[target(2), rows * i : rows * (i + 1)] = low
    kept = [
        pltpu.make_async_copy(g_high, g_high_out, sems.at[4]),
        pltpu.make_async_copy(g_low, g_low_out, sems.at[5]),
    ]
    for copy in kept:
        copy.start()

    def collect(i):
        for c in range(SIDE):
            start = cell_start(odd, (major + i) % SIDE, (minor + c) % SIDE, rows)
            chunk[:, rows * c : rows * (c + 1)] = g_far[:, pl.ds(start, rows)]
        return chunk[...]

    far = None
    for n, i in enumerate((0, 1, 3)):
        span = slice(panel * n, panel * (n + 1))
        term = product(collect(i), e_high[span, :], e_low[span, :], PLAIN)
        far = term if far is None else far + term
    for copy in copies[2:]:
        copy.wait()
    high, low = halves(e_far[:panel, :])
    far = far + product(collect(2), high, low, PLAIN)

    def one(x, y):
        return lax.dot_general(x, y, (PLAIN, ((), ())), preferred_element_type=f32)

    total[...] = near[...] + (one(far_high[...], high) + (one(far_high[...], low) + one(far_low[...], high)))
    for n, j in enumerate((0, 1, 3)):
        part_high, part_low = halves(total[rows * n : rows * (n + 1), :])
        w_high[target(j), :] = part_high
        w_low[target(j), :] = part_low
        pack[target(j), :] = total[rows * n : rows * (n + 1), :]
    part_high, part_low = halves(far)
    pack[target(2), :] = far
    pack[panel + arrow :, :] = bound[...]
    w_high[target(2), :] = part_high
    w_low[target(2), :] = part_low
    spread_panel(panels, e_far, panel, lead, (major + 2) % SIDE * rows, rows)
    base[...] = product(panels[:arrow, :], g_high[...], g_low[...], TURNED)
    pack[panel : panel + arrow, :] = base[...]
    first = jnp.where(is_first != 0, panels[arrow:, :], 0.0)
    partial[...] = base[...] - product(first, w_high[...], w_low[...], TURNED)
    for copy in kept:
        copy.wait()


def unpack_kernel(pack, w_high, w_low, base, bound):
    panel, arrow = w_high.shape[0], base.shape[0]
    high, low = halves(pack[:panel, :])
    w_high[...] = high
    w_low[...] = low
    base[...] = pack[panel : panel + arrow, :]
    bound[...] = pack[panel + arrow :, :]


def forward_odd_kernel(flag, old, old_panel, even, r1, r2, r3, base, w_high, w_low, partial, arrow_panel):
    @pl.when(flag[0] != 0)
    def _():
        arrow_panel[...] = (even[...] + r1[...]) + (r2[...] + r3[...])
        partial[...] = base[...] - product(arrow_panel[...], w_high[...], w_low[...], TURNED)

    @pl.when(flag[0] == 0)
    def _():
        partial[...] = old[...]
        arrow_panel[...] = old_panel[...]


def forward_even_kernel(flag, old, r0, r1, r2, r3, base, w_high, w_low, partial):
    @pl.when(flag[0] != 0)
    def _():
        arrived = (r0[...] + r1[...]) + (r2[...] + r3[...])
        partial[...] = base[...] - product(arrived, w_high[...], w_low[...], TURNED)

    @pl.when(flag[0] == 0)
    def _():
        partial[...] = old[...]


def turn_kernel(
    own, r1, r2, r3, even_panel, tip, bound, w_high, w_low, odd_panel, tip_even, tip_odd, combined, partial
):
    odd_panel[...] = (own[...] + r1[...]) + (r2[...] + r3[...])
    panel_high, panel_low = halves(odd_panel[...])
    tip_odd[...] = product(tip[...], panel_high, panel_low, PLAIN)
    combined[...] = tip_odd[...] + bound[...]
    partial[...] = -product(combined[...], w_high[...], w_low[...], PLAIN)
    panel_high, panel_low = halves(even_panel[...])
    tip_even[...] = product(tip[...], panel_high, panel_low, PLAIN)


def backward_kernel(flag, old, r0, r1, r2, r3, tip_term, w_high, w_low, combined, partial):
    @pl.when(flag[0] != 0)
    def _():
        combined[...] = tip_term[...] + ((r0[...] + r1[...]) + (r2[...] + r3[...]))
        partial[...] = -product(combined[...], w_high[...], w_low[...], PLAIN)

    @pl.when(flag[0] == 0)
    def _():
        combined[...] = old[...]
        partial[...] = jnp.zeros_like(partial)


def closing_kernel(
    place, flag, old, r0, r1, r2, r3, tip_term, even_panel, odd_rows, g_high_in, g_low_in,
    p0, p1, p2, p3, rows_out, scratch, g_high, g_low, sems
):
    copies = [
        pltpu.make_async_copy(g_high_in, g_high, sems.at[0]),
        pltpu.make_async_copy(g_low_in, g_low, sems.at[1]),
    ]
    for copy in copies:
        copy.start()
    odd, major, minor = place[0], place[1], place[2]
    arrow, width = p0.shape
    arrived = (r0[...] + r1[...]) + (r2[...] + r3[...])
    combined = jnp.where(flag[0] != 0, tip_term[...] + arrived, old[...])
    combined = jnp.where(odd != 0, odd_rows[:arrow, :], combined)
    for copy in copies:
        copy.wait()
    scratch[...] = -product(combined, g_high[...], g_low[...], PLAIN)
    for k, out in enumerate((p0, p1, p2, p3)):
        start = pl.multiple_of((major + k) % SIDE * width, width)
        out[...] = scratch[:, pl.ds(start, width)]
    cols = pl.ds(pl.multiple_of(minor * width, width), width)
    rows_out[...] = jnp.where(odd != 0, odd_rows[arrow:, cols], even_panel[:, cols])


def call(kernel, scalars, arrays, outs, scratch=(), anywhere=(), vmem=STEP_VMEM, far_outs=()):
    smem = pl.BlockSpec(memory_space=pltpu.SMEM)
    held = pl.BlockSpec(memory_space=pltpu.VMEM)
    return pl.pallas_call(
        kernel,
        out_shape=[jax.ShapeDtypeStruct(shape, dtype) for shape, dtype in [*outs, *far_outs]],
        in_specs=[smem] * len(scalars) + [held] * len(arrays)
        + [pl.BlockSpec(memory_space=pl.ANY)] * len(anywhere),
        out_specs=[held] * len(outs) + [pl.BlockSpec(memory_space=pltpu.HBM)] * len(far_outs),
        scratch_shapes=list(scratch),
        compiler_params=pltpu.CompilerParams(vmem_limit_bytes=vmem),
    )(*scalars, *arrays, *anywhere)


def on_device(ginv, couple, arrow_rhs, arrow_in, tip_cov, bnd_next):
    g_rows = ginv[0]
    e_rows = couple[0]
    rows = g_rows.shape[0]
    panel = rows * SIDE
    arrow = arrow_in.shape[0]
    step = lax.axis_index("dom")
    spot = lax.axis_index("blk")
    odd = step % 2
    z, y = spot // SIDE, spot % SIDE
    major = jnp.where(odd == 0, z, y)
    minor = jnp.where(odd == 0, y, z)
    place = jnp.stack([odd, major, minor, step == 0, step == STEPS - 1]).astype(jnp.int32)
    wide = ((arrow, panel), f32)
    narrow = ((arrow, rows), f32)
    half_block = ((panel, panel), bf16)

    tail = arrow // SIDE
    lead = 2 * tail
    *pieces, extra = call(
        pieces_kernel,
        [place],
        [],
        [((rows, panel), f32)] + [((rows + tail, panel), f32)] * 3 + [((lead, panel), f32)],
        [pltpu.VMEM((rows, panel * SIDE), f32)]
        + [pltpu.VMEM((arrow, rows), f32)] * 3
        + [pltpu.SemaphoreType.DMA((4,))],
        [e_rows, arrow_rhs[0], arrow_in, bnd_next],
    )
    got = {k: permuted(pieces[k], by_minor(k)) for k in FARTHEST_FIRST[:-1]}
    g_after = permuted(g_rows, by_minor(-1))
    g_later, got[2] = lax.optimization_barrier((g_rows, got[2]))
    g_before = permuted(g_later, by_minor(1))
    e_own = jnp.concatenate([pieces[0], got[3][:rows], got[2][:rows], got[1][:rows], extra])
    e_after, e_before = ring_near(e_own, by_major)
    g_far = ring_far(g_after, g_before, by_minor)
    e_far = ring_far(e_after, e_before, by_major)

    three = panel - rows
    *near, bound = call(
        near_kernel,
        [place],
        [bnd_next],
        [((three, panel), f32)]
        + [((3 * panel, panel), bf16)] * 2
        + [((three, panel), bf16)] * 4
        + [((2 * arrow, panel), f32), wide],
        [
            pltpu.VMEM((three, panel * SIDE), f32),
            pltpu.VMEM((3 * panel, panel), f32),
            pltpu.VMEM((three, panel), f32),
            pltpu.VMEM((3 * lead, panel), f32),
            pltpu.VMEM((3 * tail, panel), f32),
            pltpu.SemaphoreType.DMA((12,)),
        ],
        [g_rows, g_after, g_before, e_own, e_after, e_before, got[1], got[2], got[3]],
        vmem=FORM_VMEM,
    )
    w_high, w_low, base, even, pack, g_high, g_low = call(
        far_kernel,
        [place],
        [*near, bound],
        [half_block] * 2 + [wide] * 2 + [((panel + 2 * arrow, panel), f32)],
        [
            pltpu.VMEM((three, panel), f32),
            pltpu.VMEM((rows, panel * SIDE), f32),
            pltpu.VMEM((panel + lead, panel), f32),
            pltpu.VMEM((rows, panel), f32),
            pltpu.VMEM((2 * arrow, panel), f32),
            pltpu.VMEM((panel, panel), bf16),
            pltpu.VMEM((panel, panel), bf16),
            pltpu.SemaphoreType.DMA((6,)),
        ],
        [*g_far, *e_far],
        vmem=FORM_VMEM,
        far_outs=[half_block] * 2,
    )
    chips = STEPS // 2
    w_odd_high, w_odd_low, base_odd, bound = call(
        unpack_kernel, [], [permuted(pack, to_even_core())], [half_block] * 2 + [wide] * 2
    )

    def at(x):
        return (step == 2 * x).astype(jnp.int32)[None]

    odd_partial = even_panel = even
    for x in range(chips):
        arrived = [permuted(even, in_row(x, k)) for k in FARTHEST_FIRST[:-1]]
        odd_partial, even_panel = call(
            forward_odd_kernel,
            [at(x)],
            [odd_partial, even_panel, even, *arrived, base_odd, w_odd_high, w_odd_low],
            [wide] * 2,
        )
        if x < chips - 1:
            arrived = [permuted(odd_partial, to_next_chip(x, k)) for k in FARTHEST_FIRST]
            (even,) = call(forward_even_kernel, [at(x + 1)], [even, *arrived, base, w_high, w_low], [wide])

    arrived = [permuted(odd_partial, by_major(k)) for k in FARTHEST_FIRST[:-1]]
    odd_panel, tip_even, tip_odd, odd_combined, partial = call(
        turn_kernel,
        [],
        [odd_partial, *arrived, even_panel, tip_cov, bound, w_odd_high, w_odd_low],
        [wide] * 5,
    )
    even_combined = tip_even
    for x in range(chips - 1, -1, -1):
        arrived = [partial, *(permuted(partial, in_row(x, k)) for k in FARTHEST_FIRST[:-1])]
        if x > 0:
            even_combined, partial = call(
                backward_kernel,
                [at(x)],
                [even_combined, *arrived, tip_even, w_high, w_low],
                [wide] * 2,
            )
            hopped = [permuted(partial, to_earlier_chip(x, k)) for k in FARTHEST_FIRST]
            odd_combined, partial = call(
                backward_kernel,
                [at(x - 1)],
                [odd_combined, *hopped, tip_odd, w_odd_high, w_odd_low],
                [wide] * 2,
            )
    odd_rows = permuted(jnp.concatenate([odd_combined, odd_panel]), to_odd_core())
    *parts, arrow_local = call(
        closing_kernel,
        [place, at(0)],
        [even_combined, *arrived, tip_even, even_panel, odd_rows],
        [narrow] * (SIDE + 1),
        [
            pltpu.VMEM(*wide),
            pltpu.VMEM((panel, panel), bf16),
            pltpu.VMEM((panel, panel), bf16),
            pltpu.SemaphoreType.DMA((2,)),
        ],
        [g_high, g_low],
    )
    covariance = parts[0]
    for k in FARTHEST_FIRST[:-1]:
        covariance = covariance + permuted(parts[k], by_major(k))
    return (arrow_local[None], covariance[None])


def solution(mesh):
    return jax.shard_map(
        on_device,
        mesh=mesh,
        in_specs=(
            P("dom", "blk", None),
            P("dom", "blk", None),
            P("dom", None, "blk"),
            P(None, "blk"),
            P(),
            P(None, "blk"),
        ),
        out_specs=(P("dom", None, "blk"), P("dom", None, "blk")),
        check_vma=False,
    )
```

```python
import jax
import jax.numpy as jnp
from jax import lax
from jax.experimental import pallas as pl
from jax.experimental.pallas import tpu as pltpu
from jax.sharding import PartitionSpec as P

both = ("dom", "blk")
SIDE = 4
STEPS = 8
FARTHEST_FIRST = (2, 1, 3, 0)
FORM_VMEM = 16 * 1024 * 1024
STEP_VMEM = 6 * 1024 * 1024
f32 = jnp.float32
bf16 = jnp.bfloat16


def device_of(t, z, y):
    return t * SIDE * SIDE + (z % SIDE) * SIDE + y % SIDE


def pairs(target, steps):
    return [
        (device_of(t, z, y), device_of(*target(t, z, y)))
        for t in steps
        for z in range(SIDE)
        for y in range(SIDE)
    ]


def by_minor(k):
    return pairs(lambda t, z, y: (t, z + k * (t % 2), y + k * (1 - t % 2)), range(STEPS))


def by_major(k):
    return pairs(lambda t, z, y: (t, z + k * (1 - t % 2), y + k * (t % 2)), range(STEPS))


def together(s, groups):
    return next(group for group in groups if s in group)


def to_next(s, k):
    along_z = s % 2
    steps = together(s, ((0, 4), (2, 6), (1, 5), (3,)))
    return pairs(lambda t, z, y: (t + 1, z + k * along_z, y + k * (1 - along_z)), steps)


def to_earlier(s, k):
    along_z = 1 - s % 2
    evens = ((6, 4, 2),) if k < 2 else ((6, 2), (4,))
    steps = together(s, ((7, 3), (5, 1), *evens))
    return pairs(lambda t, z, y: (t - 1, z + k * along_z, y + k * (1 - along_z)), steps)


def permuted(value, where):
    return lax.ppermute(value, both, where)


def ring_near(block, where):
    return permuted(block, where(-1)), permuted(block, where(1))


def ring_far(after, before, where):
    half = after.shape[0] // 2
    return permuted(before[:half], where(1)), permuted(after[half:], where(-1))


def halves(value):
    high = value.astype(bf16)
    return high, (value - high.astype(f32)).astype(bf16)


def product(a, b_high, b_low, dims):
    a_high, a_low = halves(a)

    def one(x, y):
        return lax.dot_general(x, y, (dims, ((), ())), preferred_element_type=f32)

    return one(a_high, b_high) + (one(a_high, b_low) + one(a_low, b_high))


PLAIN = ((1,), (0,))
TURNED = ((1,), (1,))


def cell_start(odd, i, j, rows):
    cell = jnp.where(odd != 0, SIDE * j + i, SIDE * i + j)
    return pl.multiple_of(cell * rows, rows)


def pieces_kernel(place, e_ref, bnd, p0, p1, p2, p3):
    rows = e_ref.shape[0]
    odd, minor = place[0], place[2]
    tail = bnd.shape[0] // SIDE
    for i in range(SIDE):
        cols = slice(rows * i, rows * (i + 1))
        for k, out in enumerate((p0, p1, p2, p3)):
            start = cell_start(odd, i, (minor + k) % SIDE, rows)
            out[:rows, cols] = e_ref[:, pl.ds(start, rows)]
            if k:
                out[rows:, cols] = bnd[tail * i : tail * (i + 1), :]


def extra_kernel(rhs, entering, extra):
    height, rows = extra.shape[0], rhs.shape[1]
    for i in range(SIDE):
        source = rhs if i < SIDE // 2 else entering
        top = height * (i % (SIDE // 2))
        extra[:, rows * i : rows * (i + 1)] = source[top : top + height, :]


def spread_panel(out, source, top, height, start, rows):
    cols = pl.ds(pl.multiple_of(start, rows), rows)
    for q in range(SIDE):
        out[height * q : height * (q + 1), cols] = source[top : top + height, rows * q : rows * (q + 1)]


def near_kernel(
    place, bnd, g_own, g_after, g_before, e_own, e_after, e_before, got1, got2, got3,
    total, e_high, e_low, far_high, far_low, block_high, block_low, panels, bound,
    g_near, e_near, chunk, extra, tails, sems,
):
    odd, major, minor, is_last = place[0], place[1], place[2], place[4]
    rows = g_own.shape[0]
    panel = rows * SIDE
    lead, tail = extra.shape[0] // 3, tails.shape[0] // 3
    copies = []
    for n, source in enumerate((g_own, g_after, g_before)):
        copies.append((source, g_near.at[pl.ds(rows * n, rows)]))
    for n, source in enumerate((e_own, e_after, e_before)):
        copies.append((source.at[pl.ds(0, panel)], e_near.at[pl.ds(panel * n, panel)]))
    for n, source in enumerate((e_own, e_after, e_before)):
        copies.append((source.at[pl.ds(panel, lead)], extra.at[pl.ds(lead * n, lead)]))
    for n, source in enumerate((got1, got2, got3)):
        copies.append((source.at[pl.ds(rows, tail)], tails.at[pl.ds(tail * n, tail)]))
    copies = [pltpu.make_async_copy(x, y, sems.at[n]) for n, (x, y) in enumerate(copies)]
    for copy in copies:
        copy.start()
    for copy in copies[:3]:
        copy.wait()

    def collect(i):
        for c in range(SIDE):
            start = cell_start(odd, (major + i) % SIDE, (minor + c) % SIDE, rows)
            chunk[:, rows * c : rows * (c + 1)] = g_near[:, pl.ds(start, rows)]
        return chunk[...]

    high, low = halves(collect(2))
    far_high[...] = high
    far_low[...] = low
    for i in range(SIDE):
        start = cell_start(odd, i, minor, rows)
        high, low = halves(g_near[:, pl.ds(start, rows)])
        block_high[:, rows * i : rows * (i + 1)] = high
        block_low[:, rows * i : rows * (i + 1)] = low
    for n, i in enumerate((0, 1, 3)):
        copies[3 + n].wait()
        span = slice(panel * n, panel * (n + 1))
        high, low = halves(e_near[span, :])
        e_high[span, :] = high
        e_low[span, :] = low
        term = product(collect(i), high, low, PLAIN)
        if n == 0:
            total[...] = term
        else:
            total[...] += term

    for copy in copies[6:]:
        copy.wait()
    for n, i in enumerate((0, 1, 3)):
        spread_panel(panels, extra, lead * n, lead, (major + i) % SIDE * rows, rows)
    spread_panel(panels, extra, 0, lead, (major + 2) % SIDE * rows, rows)
    keep = is_last != 0
    bound[:, pl.ds(pl.multiple_of(minor * rows, rows), rows)] = jnp.where(keep, bnd[...], 0.0)
    for n in range(3):
        spot = (minor - n + SIDE - 1) % SIDE * rows
        spread_panel(bound, tails, tail * n, tail, spot, rows)
    bound[...] = jnp.where(keep, bound[...], 0.0)


def far_kernel(
    place, near, e_high, e_low, far_high, far_low, block_high, block_low, panels_near,
    g_top, g_bottom, e_top, e_bottom,
    w_high, w_low, base, partial, g_high_out, g_low_out,
    total, g_far, e_far, chunk, panels, g_high, g_low, sems,
):
    odd, major, minor, is_first = (place[i] for i in range(4))
    rows = g_far.shape[0]
    panel = rows * SIDE
    half = rows // 2
    lead = e_far.shape[0] - panel
    arrow = panels.shape[0] // 2
    edge = e_far.shape[0] // 2
    copies = [
        (g_top, g_far.at[pl.ds(0, half)]),
        (g_bottom, g_far.at[pl.ds(half, half)]),
        (e_top, e_far.at[pl.ds(0, edge)]),
        (e_bottom, e_far.at[pl.ds(edge, edge)]),
    ]
    copies = [pltpu.make_async_copy(x, y, sems.at[n]) for n, (x, y) in enumerate(copies)]
    for copy in copies:
        copy.start()
    panels[...] = panels_near[...]

    def target(j):
        return pl.ds(pl.multiple_of((minor + j) % SIDE * rows, rows), rows)

    for n, j in enumerate((0, 1, 3)):
        g_high[target(j), :] = block_high[rows * n : rows * (n + 1), :]
        g_low[target(j), :] = block_low[rows * n : rows * (n + 1), :]

    copies[0].wait()
    copies[1].wait()
    for i in range(SIDE):
        start = cell_start(odd, i, minor, rows)
        high, low = halves(g_far[:, pl.ds(start, rows)])
        g_high[target(2), rows * i : rows * (i + 1)] = high
        g_low[target(2), rows * i : rows * (i + 1)] = low
    kept = [
        pltpu.make_async_copy(g_high, g_high_out, sems.at[4]),
        pltpu.make_async_copy(g_low, g_low_out, sems.at[5]),
    ]
    for copy in kept:
        copy.start()

    def collect(i):
        for c in range(SIDE):
            start = cell_start(odd, (major + i) % SIDE, (minor + c) % SIDE, rows)
            chunk[:, rows * c : rows * (c + 1)] = g_far[:, pl.ds(start, rows)]
        return chunk[...]

    far = None
    for n, i in enumerate((0, 1, 3)):
        span = slice(panel * n, panel * (n + 1))
        term = product(collect(i), e_high[span, :], e_low[span, :], PLAIN)
        far = term if far is None else far + term
    for copy in copies[2:]:
        copy.wait()
    high, low = halves(e_far[:panel, :])
    far = far + product(collect(2), high, low, PLAIN)

    def one(x, y):
        return lax.dot_general(x, y, (PLAIN, ((), ())), preferred_element_type=f32)

    total[...] = near[...] + (one(far_high[...], high) + (one(far_high[...], low) + one(far_low[...], high)))
    for n, j in enumerate((0, 1, 3)):
        part_high, part_low = halves(total[rows * n : rows * (n + 1), :])
        w_high[target(j), :] = part_high
        w_low[target(j), :] = part_low
    part_high, part_low = halves(far)
    w_high[target(2), :] = part_high
    w_low[target(2), :] = part_low
    spread_panel(panels, e_far, panel, lead, (major + 2) % SIDE * rows, rows)
    base[...] = product(panels[:arrow, :], g_high[...], g_low[...], TURNED)
    first = jnp.where(is_first != 0, panels[arrow:, :], 0.0)
    partial[...] = base[...] - product(first, w_high[...], w_low[...], TURNED)
    for copy in kept:
        copy.wait()


def forward_kernel(flag, old, r0, r1, r2, r3, base, w_high, w_low, partial):
    @pl.when(flag[0] != 0)
    def _():
        arrived = (r0[...] + r1[...]) + (r2[...] + r3[...])
        partial[...] = base[...] - product(arrived, w_high[...], w_low[...], TURNED)

    @pl.when(flag[0] == 0)
    def _():
        partial[...] = old[...]


def turn_kernel(place, own, r1, r2, r3, tip, bound, w_high, w_low, rows_out, tip_term, combined, partial):
    arrow_panel = (own[...] + r1[...]) + (r2[...] + r3[...])
    panel_high, panel_low = halves(arrow_panel)
    tip_term[...] = product(tip[...], panel_high, panel_low, PLAIN)
    combined[...] = tip_term[...] + bound[...]
    partial[...] = -product(combined[...], w_high[...], w_low[...], PLAIN)
    width = rows_out.shape[1]
    minor = place[2]
    chosen = arrow_panel[:, :width]
    for j in range(1, SIDE):
        chosen = jnp.where(minor == j, arrow_panel[:, width * j : width * (j + 1)], chosen)
    rows_out[...] = chosen


def backward_kernel(flag, old, r0, r1, r2, r3, tip_term, w_high, w_low, combined, partial):
    @pl.when(flag[0] != 0)
    def _():
        combined[...] = tip_term[...] + ((r0[...] + r1[...]) + (r2[...] + r3[...]))
        partial[...] = -product(combined[...], w_high[...], w_low[...], PLAIN)

    @pl.when(flag[0] == 0)
    def _():
        combined[...] = old[...]
        partial[...] = jnp.zeros_like(partial)


def closing_kernel(
    place, flag, old, r0, r1, r2, r3, tip_term, g_high_in, g_low_in, p0, p1, p2, p3, scratch, g_high, g_low, sems
):
    copies = [
        pltpu.make_async_copy(g_high_in, g_high, sems.at[0]),
        pltpu.make_async_copy(g_low_in, g_low, sems.at[1]),
    ]
    for copy in copies:
        copy.start()
    arrived = (r0[...] + r1[...]) + (r2[...] + r3[...])
    combined = jnp.where(flag[0] != 0, tip_term[...] + arrived, old[...])
    for copy in copies:
        copy.wait()
    scratch[...] = -product(combined, g_high[...], g_low[...], PLAIN)
    width = p0.shape[1]
    major = place[1]
    for k, out in enumerate((p0, p1, p2, p3)):
        start = pl.multiple_of((major + k) % SIDE * width, width)
        out[...] = scratch[:, pl.ds(start, width)]


def call(kernel, scalars, arrays, outs, scratch=(), anywhere=(), vmem=STEP_VMEM, far_outs=()):
    smem = pl.BlockSpec(memory_space=pltpu.SMEM)
    held = pl.BlockSpec(memory_space=pltpu.VMEM)
    return pl.pallas_call(
        kernel,
        out_shape=[jax.ShapeDtypeStruct(shape, dtype) for shape, dtype in [*outs, *far_outs]],
        in_specs=[smem] * len(scalars) + [held] * len(arrays)
        + [pl.BlockSpec(memory_space=pl.ANY)] * len(anywhere),
        out_specs=[held] * len(outs) + [pl.BlockSpec(memory_space=pltpu.HBM)] * len(far_outs),
        scratch_shapes=list(scratch),
        compiler_params=pltpu.CompilerParams(vmem_limit_bytes=vmem),
    )(*scalars, *arrays, *anywhere)


def on_device(ginv, couple, arrow_rhs, arrow_in, tip_cov, bnd_next):
    g_rows = ginv[0]
    e_rows = couple[0]
    rows = g_rows.shape[0]
    panel = rows * SIDE
    arrow = arrow_in.shape[0]
    step = lax.axis_index("dom")
    spot = lax.axis_index("blk")
    odd = step % 2
    z, y = spot // SIDE, spot % SIDE
    major = jnp.where(odd == 0, z, y)
    minor = jnp.where(odd == 0, y, z)
    place = jnp.stack([odd, major, minor, step == 0, step == STEPS - 1]).astype(jnp.int32)
    wide = ((arrow, panel), f32)
    narrow = ((arrow, rows), f32)
    half_block = ((panel, panel), bf16)

    tail = arrow // SIDE
    lead = 2 * tail
    pieces = call(
        pieces_kernel,
        [place],
        [e_rows, bnd_next],
        [((rows, panel), f32)] + [((rows + tail, panel), f32)] * 3,
    )
    got = {k: permuted(pieces[k], by_minor(k)) for k in FARTHEST_FIRST[:-1]}
    g_after = permuted(g_rows, by_minor(-1))
    g_later, rhs, entering, got[2] = lax.optimization_barrier((g_rows, arrow_rhs[0], arrow_in, got[2]))
    (extra,) = call(extra_kernel, [], [rhs, entering], [((lead, panel), f32)])
    g_before = permuted(g_later, by_minor(1))
    e_own = jnp.concatenate([pieces[0], got[3][:rows], got[2][:rows], got[1][:rows], extra])
    e_after, e_before = ring_near(e_own, by_major)
    g_far = ring_far(g_after, g_before, by_minor)
    e_far = ring_far(e_after, e_before, by_major)

    three = panel - rows
    *near, bound = call(
        near_kernel,
        [place],
        [bnd_next],
        [((three, panel), f32)]
        + [((3 * panel, panel), bf16)] * 2
        + [((three, panel), bf16)] * 4
        + [((2 * arrow, panel), f32), wide],
        [
            pltpu.VMEM((three, panel * SIDE), f32),
            pltpu.VMEM((3 * panel, panel), f32),
            pltpu.VMEM((three, panel), f32),
            pltpu.VMEM((3 * lead, panel), f32),
            pltpu.VMEM((3 * tail, panel), f32),
            pltpu.SemaphoreType.DMA((12,)),
        ],
        [g_rows, g_after, g_before, e_own, e_after, e_before, got[1], got[2], got[3]],
        vmem=FORM_VMEM,
    )
    w_high, w_low, base, partial, g_high, g_low = call(
        far_kernel,
        [place],
        near,
        [half_block] * 2 + [wide] * 2,
        [
            pltpu.VMEM((three, panel), f32),
            pltpu.VMEM((rows, panel * SIDE), f32),
            pltpu.VMEM((panel + lead, panel), f32),
            pltpu.VMEM((rows, panel), f32),
            pltpu.VMEM((2 * arrow, panel), f32),
            pltpu.VMEM((panel, panel), bf16),
            pltpu.VMEM((panel, panel), bf16),
            pltpu.SemaphoreType.DMA((6,)),
        ],
        [*g_far, *e_far],
        vmem=FORM_VMEM,
        far_outs=[half_block] * 2,
    )
    for s in range(STEPS - 1):
        arrived = [permuted(partial, to_next(s, k)) for k in FARTHEST_FIRST]
        flag = (step == s + 1).astype(jnp.int32)[None]
        (partial,) = call(forward_kernel, [flag], [partial, *arrived, base, w_high, w_low], [wide])
    arrived = [permuted(partial, by_minor(k)) for k in FARTHEST_FIRST[:-1]]
    arrow_local, tip_term, combined, partial = call(
        turn_kernel,
        [place],
        [partial, *arrived, tip_cov, bound, w_high, w_low],
        [narrow] + [wide] * 3,
    )
    for s in range(STEPS - 1, 0, -1):
        arrived = [permuted(partial, to_earlier(s, k)) for k in FARTHEST_FIRST]
        flag = (step == s - 1).astype(jnp.int32)[None]
        if s > 1:
            combined, partial = call(
                backward_kernel, [flag], [combined, *arrived, tip_term, w_high, w_low], [wide] * 2
            )
    parts = call(
        closing_kernel,
        [place, flag],
        [combined, *arrived, tip_term],
        [narrow] * SIDE,
        [
            pltpu.VMEM(*wide),
            pltpu.VMEM((panel, panel), bf16),
            pltpu.VMEM((panel, panel), bf16),
            pltpu.SemaphoreType.DMA((2,)),
        ],
        [g_high, g_low],
    )
    covariance = parts[0]
    for k in FARTHEST_FIRST[:-1]:
        covariance = covariance + permuted(parts[k], by_major(k))
    return (arrow_local[None], covariance[None])


def solution(mesh):
    return jax.shard_map(
        on_device,
        mesh=mesh,
        in_specs=(
            P("dom", "blk", None),
            P("dom", "blk", None),
            P("dom", None, "blk"),
            P(None, "blk"),
            P(),
            P(None, "blk"),
        ),
        out_specs=(P("dom", None, "blk"), P("dom", None, "blk")),
        check_vma=False,
    )
```

```python
import jax
import jax.numpy as jnp
from jax import lax
from jax.experimental import pallas as pl
from jax.experimental.pallas import tpu as pltpu
from jax.sharding import PartitionSpec as P

both = ("dom", "blk")
SIDE = 4
STEPS = 8
FARTHEST_FIRST = (2, 1, 3, 0)
FORM_VMEM = 16 * 1024 * 1024
STEP_VMEM = 6 * 1024 * 1024
f32 = jnp.float32
bf16 = jnp.bfloat16


def transposed(t):
    return (t + 1) % 2


def device_of(t, z, y):
    return t * SIDE * SIDE + (z % SIDE) * SIDE + y % SIDE


def pairs(target, steps):
    return [
        (device_of(t, z, y), device_of(*target(t, z, y)))
        for t in steps
        for z in range(SIDE)
        for y in range(SIDE)
    ]


def by_minor(k):
    return pairs(lambda t, z, y: (t, z + k * transposed(t), y + k * (1 - transposed(t))), range(STEPS))


def by_major(k):
    return pairs(lambda t, z, y: (t, z + k * (1 - transposed(t)), y + k * transposed(t)), range(STEPS))


def together(s, groups):
    return next(group for group in groups if s in group)


def to_next(s, k):
    along_z = transposed(s)
    steps = together(s, ((0, 4), (2, 6), (1, 5), (3,)))
    return pairs(lambda t, z, y: (t + 1, z + k * along_z, y + k * (1 - along_z)), steps)


def to_earlier(s, k):
    along_z = 1 - transposed(s)
    evens = ((6, 4, 2),) if k < 2 else ((6, 2), (4,))
    steps = together(s, ((7, 3), (5, 1), *evens))
    return pairs(lambda t, z, y: (t - 1, z + k * along_z, y + k * (1 - along_z)), steps)


def permuted(value, where):
    return lax.ppermute(value, both, where)


def ring_near(block, where):
    return permuted(block, where(-1)), permuted(block, where(1))


def ring_far(after, before, where):
    half = after.shape[0] // 2
    return permuted(before[:half], where(1)), permuted(after[half:], where(-1))


def halves(value):
    high = value.astype(bf16)
    return high, (value - high.astype(f32)).astype(bf16)


def product(a, b_high, b_low, dims):
    a_high, a_low = halves(a)

    def one(x, y):
        return lax.dot_general(x, y, (dims, ((), ())), preferred_element_type=f32)

    return one(a_high, b_high) + (one(a_high, b_low) + one(a_low, b_high))


PLAIN = ((1,), (0,))
TURNED = ((1,), (1,))


def cell_start(turned, i, j, rows):
    cell = jnp.where(turned != 0, SIDE * j + i, SIDE * i + j)
    return pl.multiple_of(cell * rows, rows)


def pieces_kernel(place, e_ref, bnd, p0, p1, p2, p3):
    rows = e_ref.shape[0]
    turned, minor = place[0], place[2]
    tail = bnd.shape[0] // SIDE
    for i in range(SIDE):
        cols = slice(rows * i, rows * (i + 1))
        for k, out in enumerate((p0, p1, p2, p3)):
            start = cell_start(turned, i, (minor + k) % SIDE, rows)
            out[:rows, cols] = e_ref[:, pl.ds(start, rows)]
            if k:
                out[rows:, cols] = bnd[tail * i : tail * (i + 1), :]


def extra_kernel(rhs, entering, extra):
    height, rows = extra.shape[0], rhs.shape[1]
    for i in range(SIDE):
        source = rhs if i < SIDE // 2 else entering
        top = height * (i % (SIDE // 2))
        extra[:, rows * i : rows * (i + 1)] = source[top : top + height, :]


def spread_panel(out, source, top, height, start, rows):
    cols = pl.ds(pl.multiple_of(start, rows), rows)
    for q in range(SIDE):
        out[height * q : height * (q + 1), cols] = source[top : top + height, rows * q : rows * (q + 1)]


def near_kernel(
    place, bnd, g_own, g_after, g_before, e_own, e_after, e_before, got1, got2, got3,
    total, e_high, e_low, far_high, far_low, block_high, block_low, panels, bound,
    g_near, e_near, chunk, extra, tails, sems,
):
    turned, major, minor, is_last = place[0], place[1], place[2], place[4]
    rows = g_own.shape[0]
    panel = rows * SIDE
    lead, tail = extra.shape[0] // 3, tails.shape[0] // 3
    copies = []
    for n, source in enumerate((g_own, g_after, g_before)):
        copies.append((source, g_near.at[pl.ds(rows * n, rows)]))
    for n, source in enumerate((e_own, e_after, e_before)):
        copies.append((source.at[pl.ds(0, panel)], e_near.at[pl.ds(panel * n, panel)]))
    for n, source in enumerate((e_own, e_after, e_before)):
        copies.append((source.at[pl.ds(panel, lead)], extra.at[pl.ds(lead * n, lead)]))
    for n, source in enumerate((got1, got2, got3)):
        copies.append((source.at[pl.ds(rows, tail)], tails.at[pl.ds(tail * n, tail)]))
    copies = [pltpu.make_async_copy(x, y, sems.at[n]) for n, (x, y) in enumerate(copies)]
    for copy in copies:
        copy.start()
    for copy in copies[:3]:
        copy.wait()

    def collect(i):
        for c in range(SIDE):
            start = cell_start(turned, (major + i) % SIDE, (minor + c) % SIDE, rows)
            chunk[:, rows * c : rows * (c + 1)] = g_near[:, pl.ds(start, rows)]
        return chunk[...]

    high, low = halves(collect(2))
    far_high[...] = high
    far_low[...] = low
    for i in range(SIDE):
        start = cell_start(turned, i, minor, rows)
        high, low = halves(g_near[:, pl.ds(start, rows)])
        block_high[:, rows * i : rows * (i + 1)] = high
        block_low[:, rows * i : rows * (i + 1)] = low
    for n, i in enumerate((0, 1, 3)):
        copies[3 + n].wait()
        span = slice(panel * n, panel * (n + 1))
        high, low = halves(e_near[span, :])
        e_high[span, :] = high
        e_low[span, :] = low
        term = product(collect(i), high, low, PLAIN)
        if n == 0:
            total[...] = term
        else:
            total[...] += term

    for copy in copies[6:]:
        copy.wait()
    for n, i in enumerate((0, 1, 3)):
        spread_panel(panels, extra, lead * n, lead, (major + i) % SIDE * rows, rows)
    spread_panel(panels, extra, 0, lead, (major + 2) % SIDE * rows, rows)
    keep = is_last != 0
    bound[:, pl.ds(pl.multiple_of(minor * rows, rows), rows)] = jnp.where(keep, bnd[...], 0.0)
    for n in range(3):
        spot = (minor - n + SIDE - 1) % SIDE * rows
        spread_panel(bound, tails, tail * n, tail, spot, rows)
    bound[...] = jnp.where(keep, bound[...], 0.0)


def far_kernel(
    place, near, e_high, e_low, far_high, far_low, block_high, block_low, panels_near,
    g_top, g_bottom, e_top, e_bottom,
    w_high, w_low, base, partial, g_high_out, g_low_out,
    total, g_far, e_far, chunk, panels, g_high, g_low, sems,
):
    turned, major, minor, is_first = (place[i] for i in range(4))
    rows = g_far.shape[0]
    panel = rows * SIDE
    half = rows // 2
    lead = e_far.shape[0] - panel
    arrow = panels.shape[0] // 2
    edge = e_far.shape[0] // 2
    copies = [
        (g_top, g_far.at[pl.ds(0, half)]),
        (g_bottom, g_far.at[pl.ds(half, half)]),
        (e_top, e_far.at[pl.ds(0, edge)]),
        (e_bottom, e_far.at[pl.ds(edge, edge)]),
    ]
    copies = [pltpu.make_async_copy(x, y, sems.at[n]) for n, (x, y) in enumerate(copies)]
    for copy in copies:
        copy.start()
    panels[...] = panels_near[...]

    def target(j):
        return pl.ds(pl.multiple_of((minor + j) % SIDE * rows, rows), rows)

    for n, j in enumerate((0, 1, 3)):
        g_high[target(j), :] = block_high[rows * n : rows * (n + 1), :]
        g_low[target(j), :] = block_low[rows * n : rows * (n + 1), :]

    copies[0].wait()
    copies[1].wait()
    for i in range(SIDE):
        start = cell_start(turned, i, minor, rows)
        high, low = halves(g_far[:, pl.ds(start, rows)])
        g_high[target(2), rows * i : rows * (i + 1)] = high
        g_low[target(2), rows * i : rows * (i + 1)] = low
    kept = [
        pltpu.make_async_copy(g_high, g_high_out, sems.at[4]),
        pltpu.make_async_copy(g_low, g_low_out, sems.at[5]),
    ]
    for copy in kept:
        copy.start()

    def collect(i):
        for c in range(SIDE):
            start = cell_start(turned, (major + i) % SIDE, (minor + c) % SIDE, rows)
            chunk[:, rows * c : rows * (c + 1)] = g_far[:, pl.ds(start, rows)]
        return chunk[...]

    far = None
    for n, i in enumerate((0, 1, 3)):
        span = slice(panel * n, panel * (n + 1))
        term = product(collect(i), e_high[span, :], e_low[span, :], PLAIN)
        far = term if far is None else far + term
    for copy in copies[2:]:
        copy.wait()
    high, low = halves(e_far[:panel, :])
    far = far + product(collect(2), high, low, PLAIN)

    def one(x, y):
        return lax.dot_general(x, y, (PLAIN, ((), ())), preferred_element_type=f32)

    total[...] = near[...] + (one(far_high[...], high) + (one(far_high[...], low) + one(far_low[...], high)))
    for n, j in enumerate((0, 1, 3)):
        part_high, part_low = halves(total[rows * n : rows * (n + 1), :])
        w_high[target(j), :] = part_high
        w_low[target(j), :] = part_low
    part_high, part_low = halves(far)
    w_high[target(2), :] = part_high
    w_low[target(2), :] = part_low
    spread_panel(panels, e_far, panel, lead, (major + 2) % SIDE * rows, rows)
    base[...] = product(panels[:arrow, :], g_high[...], g_low[...], TURNED)
    first = jnp.where(is_first != 0, panels[arrow:, :], 0.0)
    partial[...] = base[...] - product(first, w_high[...], w_low[...], TURNED)
    for copy in kept:
        copy.wait()


def transpose_kernel(high, low, high_out, low_out):
    high_out[...] = high[...].astype(f32).T.astype(bf16)
    low_out[...] = low[...].astype(f32).T.astype(bf16)


def forward_kernel(flag, old, r0, r1, r2, r3, base, w_high, w_low, partial):
    @pl.when(flag[0] != 0)
    def _():
        arrived = (r0[...] + r1[...]) + (r2[...] + r3[...])
        partial[...] = base[...] - product(arrived, w_high[...], w_low[...], PLAIN)

    @pl.when(flag[0] == 0)
    def _():
        partial[...] = old[...]


def turn_kernel(place, own, r1, r2, r3, tip, bound, w_high, w_low, rows_out, tip_term, combined, partial):
    arrow_panel = (own[...] + r1[...]) + (r2[...] + r3[...])
    panel_high, panel_low = halves(arrow_panel)
    tip_term[...] = product(tip[...], panel_high, panel_low, PLAIN)
    combined[...] = tip_term[...] + bound[...]
    partial[...] = -product(combined[...], w_high[...], w_low[...], PLAIN)
    width = rows_out.shape[1]
    minor = place[2]
    chosen = arrow_panel[:, :width]
    for j in range(1, SIDE):
        chosen = jnp.where(minor == j, arrow_panel[:, width * j : width * (j + 1)], chosen)
    rows_out[...] = chosen


def backward_kernel(flag, old, r0, r1, r2, r3, tip_term, w_high, w_low, combined, partial):
    @pl.when(flag[0] != 0)
    def _():
        combined[...] = tip_term[...] + ((r0[...] + r1[...]) + (r2[...] + r3[...]))
        partial[...] = -product(combined[...], w_high[...], w_low[...], PLAIN)

    @pl.when(flag[0] == 0)
    def _():
        combined[...] = old[...]
        partial[...] = jnp.zeros_like(partial)


def closing_kernel(
    place, flag, old, r0, r1, r2, r3, tip_term, g_high_in, g_low_in, p0, p1, p2, p3, scratch, g_high, g_low, sems
):
    copies = [
        pltpu.make_async_copy(g_high_in, g_high, sems.at[0]),
        pltpu.make_async_copy(g_low_in, g_low, sems.at[1]),
    ]
    for copy in copies:
        copy.start()
    arrived = (r0[...] + r1[...]) + (r2[...] + r3[...])
    combined = jnp.where(flag[0] != 0, tip_term[...] + arrived, old[...])
    for copy in copies:
        copy.wait()
    scratch[...] = -product(combined, g_high[...], g_low[...], PLAIN)
    width = p0.shape[1]
    major = place[1]
    for k, out in enumerate((p0, p1, p2, p3)):
        start = pl.multiple_of((major + k) % SIDE * width, width)
        out[...] = scratch[:, pl.ds(start, width)]


def call(kernel, scalars, arrays, outs, scratch=(), anywhere=(), vmem=STEP_VMEM, far_outs=()):
    smem = pl.BlockSpec(memory_space=pltpu.SMEM)
    held = pl.BlockSpec(memory_space=pltpu.VMEM)
    return pl.pallas_call(
        kernel,
        out_shape=[jax.ShapeDtypeStruct(shape, dtype) for shape, dtype in [*outs, *far_outs]],
        in_specs=[smem] * len(scalars) + [held] * len(arrays)
        + [pl.BlockSpec(memory_space=pl.ANY)] * len(anywhere),
        out_specs=[held] * len(outs) + [pl.BlockSpec(memory_space=pltpu.HBM)] * len(far_outs),
        scratch_shapes=list(scratch),
        compiler_params=pltpu.CompilerParams(vmem_limit_bytes=vmem),
    )(*scalars, *arrays, *anywhere)


def on_device(ginv, couple, arrow_rhs, arrow_in, tip_cov, bnd_next):
    g_rows = ginv[0]
    e_rows = couple[0]
    rows = g_rows.shape[0]
    panel = rows * SIDE
    arrow = arrow_in.shape[0]
    step = lax.axis_index("dom")
    spot = lax.axis_index("blk")
    turned = transposed(step)
    z, y = spot // SIDE, spot % SIDE
    major = jnp.where(turned == 0, z, y)
    minor = jnp.where(turned == 0, y, z)
    place = jnp.stack([turned, major, minor, step == 0, step == STEPS - 1]).astype(jnp.int32)
    wide = ((arrow, panel), f32)
    narrow = ((arrow, rows), f32)
    half_block = ((panel, panel), bf16)

    tail = arrow // SIDE
    lead = 2 * tail
    pieces = call(
        pieces_kernel,
        [place],
        [e_rows, bnd_next],
        [((rows, panel), f32)] + [((rows + tail, panel), f32)] * 3,
    )
    got = {k: permuted(pieces[k], by_minor(k)) for k in FARTHEST_FIRST[:-1]}
    g_after = permuted(g_rows, by_minor(-1))
    g_later, rhs, entering, got[2] = lax.optimization_barrier((g_rows, arrow_rhs[0], arrow_in, got[2]))
    (extra,) = call(extra_kernel, [], [rhs, entering], [((lead, panel), f32)])
    g_before = permuted(g_later, by_minor(1))
    e_own = jnp.concatenate([pieces[0], got[3][:rows], got[2][:rows], got[1][:rows], extra])
    e_after, e_before = ring_near(e_own, by_major)
    g_far = ring_far(g_after, g_before, by_minor)
    e_far = ring_far(e_after, e_before, by_major)

    three = panel - rows
    *near, bound = call(
        near_kernel,
        [place],
        [bnd_next],
        [((three, panel), f32)]
        + [((3 * panel, panel), bf16)] * 2
        + [((three, panel), bf16)] * 4
        + [((2 * arrow, panel), f32), wide],
        [
            pltpu.VMEM((three, panel * SIDE), f32),
            pltpu.VMEM((3 * panel, panel), f32),
            pltpu.VMEM((three, panel), f32),
            pltpu.VMEM((3 * lead, panel), f32),
            pltpu.VMEM((3 * tail, panel), f32),
            pltpu.SemaphoreType.DMA((12,)),
        ],
        [g_rows, g_after, g_before, e_own, e_after, e_before, got[1], got[2], got[3]],
        vmem=FORM_VMEM,
    )
    w_high, w_low, base, partial, g_high, g_low = call(
        far_kernel,
        [place],
        near,
        [half_block] * 2 + [wide] * 2,
        [
            pltpu.VMEM((three, panel), f32),
            pltpu.VMEM((rows, panel * SIDE), f32),
            pltpu.VMEM((panel + lead, panel), f32),
            pltpu.VMEM((rows, panel), f32),
            pltpu.VMEM((2 * arrow, panel), f32),
            pltpu.VMEM((panel, panel), bf16),
            pltpu.VMEM((panel, panel), bf16),
            pltpu.SemaphoreType.DMA((6,)),
        ],
        [*g_far, *e_far],
        vmem=FORM_VMEM,
        far_outs=[half_block] * 2,
    )
    across = call(transpose_kernel, [], [w_high, w_low], [half_block] * 2)
    for s in range(STEPS - 1):
        arrived = [permuted(partial, to_next(s, k)) for k in FARTHEST_FIRST]
        flag = (step == s + 1).astype(jnp.int32)[None]
        (partial,) = call(forward_kernel, [flag], [partial, *arrived, base, *across], [wide])
    arrived = [permuted(partial, by_minor(k)) for k in FARTHEST_FIRST[:-1]]
    arrow_local, tip_term, combined, partial = call(
        turn_kernel,
        [place],
        [partial, *arrived, tip_cov, bound, w_high, w_low],
        [narrow] + [wide] * 3,
    )
    for s in range(STEPS - 1, 0, -1):
        arrived = [permuted(partial, to_earlier(s, k)) for k in FARTHEST_FIRST]
        flag = (step == s - 1).astype(jnp.int32)[None]
        if s > 1:
            combined, partial = call(
                backward_kernel, [flag], [combined, *arrived, tip_term, w_high, w_low], [wide] * 2
            )
    parts = call(
        closing_kernel,
        [place, flag],
        [combined, *arrived, tip_term],
        [narrow] * SIDE,
        [
            pltpu.VMEM(*wide),
            pltpu.VMEM((panel, panel), bf16),
            pltpu.VMEM((panel, panel), bf16),
            pltpu.SemaphoreType.DMA((2,)),
        ],
        [g_high, g_low],
    )
    covariance = parts[0]
    for k in FARTHEST_FIRST[:-1]:
        covariance = covariance + permuted(parts[k], by_major(k))
    return (arrow_local[None], covariance[None])


def solution(mesh):
    return jax.shard_map(
        on_device,
        mesh=mesh,
        in_specs=(
            P("dom", "blk", None),
            P("dom", "blk", None),
            P("dom", None, "blk"),
            P(None, "blk"),
            P(),
            P(None, "blk"),
        ),
        out_specs=(P("dom", None, "blk"), P("dom", None, "blk")),
        check_vma=False,
    )
```

```python
import jax
import jax.numpy as jnp
from jax import lax
from jax.experimental import pallas as pl
from jax.experimental.pallas import tpu as pltpu
from jax.sharding import PartitionSpec as P

both = ("dom", "blk")
SIDE = 4
STEPS = 8
FARTHEST_FIRST = (2, 1, 3, 0)
FORM_VMEM = 16 * 1024 * 1024
STEP_VMEM = 6 * 1024 * 1024
f32 = jnp.float32
bf16 = jnp.bfloat16


def device_of(t, z, y):
    return t * SIDE * SIDE + (z % SIDE) * SIDE + y % SIDE


def pairs(target, steps):
    return [
        (device_of(t, z, y), device_of(*target(t, z, y)))
        for t in steps
        for z in range(SIDE)
        for y in range(SIDE)
    ]


def by_minor(k):
    return pairs(lambda t, z, y: (t, z + k * (t % 2), y + k * (1 - t % 2)), range(STEPS))


def by_major(k):
    return pairs(lambda t, z, y: (t, z + k * (1 - t % 2), y + k * (t % 2)), range(STEPS))


def together(s, groups):
    return next(group for group in groups if s in group)


def to_next(s, k):
    along_z = s % 2
    steps = together(s, ((0, 4), (2, 6), (1, 5), (3,)))
    return pairs(lambda t, z, y: (t + 1, z + k * along_z, y + k * (1 - along_z)), steps)


def to_earlier(s, k):
    along_z = 1 - s % 2
    evens = ((6, 4, 2),) if k < 2 else ((6, 2), (4,))
    steps = together(s, ((7, 3), (5, 1), *evens))
    return pairs(lambda t, z, y: (t - 1, z + k * along_z, y + k * (1 - along_z)), steps)


def permuted(value, where):
    return lax.ppermute(value, both, where)


def ring_near(block, where):
    return permuted(block, where(-1)), permuted(block, where(1))


def ring_far(after, before, where):
    half = after.shape[0] // 2
    return permuted(before[:half], where(1)), permuted(after[half:], where(-1))


def halves(value):
    high = value.astype(bf16)
    return high, (value - high.astype(f32)).astype(bf16)


def product(a, b_high, b_low, dims):
    a_high, a_low = halves(a)

    def one(x, y):
        return lax.dot_general(x, y, (dims, ((), ())), preferred_element_type=f32)

    rows = a.shape[0]
    by_high = one(jnp.concatenate([a_high, a_low]), b_high)
    return by_high[:rows] + (one(a_high, b_low) + by_high[rows:])


PLAIN = ((1,), (0,))
TURNED = ((1,), (1,))


def cell_start(odd, i, j, rows):
    cell = jnp.where(odd != 0, SIDE * j + i, SIDE * i + j)
    return pl.multiple_of(cell * rows, rows)


def pieces_kernel(place, e_ref, bnd, p0, p1, p2, p3):
    rows = e_ref.shape[0]
    odd, minor = place[0], place[2]
    tail = bnd.shape[0] // SIDE
    for i in range(SIDE):
        cols = slice(rows * i, rows * (i + 1))
        for k, out in enumerate((p0, p1, p2, p3)):
            start = cell_start(odd, i, (minor + k) % SIDE, rows)
            out[:rows, cols] = e_ref[:, pl.ds(start, rows)]
            if k:
                out[rows:, cols] = bnd[tail * i : tail * (i + 1), :]


def extra_kernel(rhs, entering, extra):
    height, rows = extra.shape[0], rhs.shape[1]
    for i in range(SIDE):
        source = rhs if i < SIDE // 2 else entering
        top = height * (i % (SIDE // 2))
        extra[:, rows * i : rows * (i + 1)] = source[top : top + height, :]


def spread_panel(out, source, top, height, start, rows):
    cols = pl.ds(pl.multiple_of(start, rows), rows)
    for q in range(SIDE):
        out[height * q : height * (q + 1), cols] = source[top : top + height, rows * q : rows * (q + 1)]


def near_kernel(
    place, bnd, g_own, g_after, g_before, e_own, e_after, e_before, got1, got2, got3,
    total, e_high, e_low, far_high, far_low, block_high, block_low, panels, bound,
    g_near, e_near, chunk, extra, tails, sems,
):
    odd, major, minor, is_last = place[0], place[1], place[2], place[4]
    rows = g_own.shape[0]
    panel = rows * SIDE
    lead, tail = extra.shape[0] // 3, tails.shape[0] // 3
    copies = []
    for n, source in enumerate((g_own, g_after, g_before)):
        copies.append((source, g_near.at[pl.ds(rows * n, rows)]))
    for n, source in enumerate((e_own, e_after, e_before)):
        copies.append((source.at[pl.ds(0, panel)], e_near.at[pl.ds(panel * n, panel)]))
    for n, source in enumerate((e_own, e_after, e_before)):
        copies.append((source.at[pl.ds(panel, lead)], extra.at[pl.ds(lead * n, lead)]))
    for n, source in enumerate((got1, got2, got3)):
        copies.append((source.at[pl.ds(rows, tail)], tails.at[pl.ds(tail * n, tail)]))
    copies = [pltpu.make_async_copy(x, y, sems.at[n]) for n, (x, y) in enumerate(copies)]
    for copy in copies:
        copy.start()
    for copy in copies[:3]:
        copy.wait()

    def collect(i):
        for c in range(SIDE):
            start = cell_start(odd, (major + i) % SIDE, (minor + c) % SIDE, rows)
            chunk[:, rows * c : rows * (c + 1)] = g_near[:, pl.ds(start, rows)]
        return chunk[...]

    high, low = halves(collect(2))
    far_high[...] = high
    far_low[...] = low
    for i in range(SIDE):
        start = cell_start(odd, i, minor, rows)
        high, low = halves(g_near[:, pl.ds(start, rows)])
        block_high[:, rows * i : rows * (i + 1)] = high
        block_low[:, rows * i : rows * (i + 1)] = low
    for n, i in enumerate((0, 1, 3)):
        copies[3 + n].wait()
        span = slice(panel * n, panel * (n + 1))
        high, low = halves(e_near[span, :])
        e_high[span, :] = high
        e_low[span, :] = low
        term = product(collect(i), high, low, PLAIN)
        if n == 0:
            total[...] = term
        else:
            total[...] += term

    for copy in copies[6:]:
        copy.wait()
    for n, i in enumerate((0, 1, 3)):
        spread_panel(panels, extra, lead * n, lead, (major + i) % SIDE * rows, rows)
    spread_panel(panels, extra, 0, lead, (major + 2) % SIDE * rows, rows)
    keep = is_last != 0
    bound[:, pl.ds(pl.multiple_of(minor * rows, rows), rows)] = jnp.where(keep, bnd[...], 0.0)
    for n in range(3):
        spot = (minor - n + SIDE - 1) % SIDE * rows
        spread_panel(bound, tails, tail * n, tail, spot, rows)
    bound[...] = jnp.where(keep, bound[...], 0.0)


def far_kernel(
    place, near, e_high, e_low, far_high, far_low, block_high, block_low, panels_near,
    g_top, g_bottom, e_top, e_bottom,
    w_high, w_low, base, partial, g_high_out, g_low_out,
    total, g_far, e_far, chunk, panels, g_high, g_low, sems,
):
    odd, major, minor, is_first = (place[i] for i in range(4))
    rows = g_far.shape[0]
    panel = rows * SIDE
    half = rows // 2
    lead = e_far.shape[0] - panel
    arrow = panels.shape[0] // 2
    edge = e_far.shape[0] // 2
    copies = [
        (g_top, g_far.at[pl.ds(0, half)]),
        (g_bottom, g_far.at[pl.ds(half, half)]),
        (e_top, e_far.at[pl.ds(0, edge)]),
        (e_bottom, e_far.at[pl.ds(edge, edge)]),
    ]
    copies = [pltpu.make_async_copy(x, y, sems.at[n]) for n, (x, y) in enumerate(copies)]
    for copy in copies:
        copy.start()
    panels[...] = panels_near[...]

    def target(j):
        return pl.ds(pl.multiple_of((minor + j) % SIDE * rows, rows), rows)

    for n, j in enumerate((0, 1, 3)):
        g_high[target(j), :] = block_high[rows * n : rows * (n + 1), :]
        g_low[target(j), :] = block_low[rows * n : rows * (n + 1), :]

    copies[0].wait()
    copies[1].wait()
    for i in range(SIDE):
        start = cell_start(odd, i, minor, rows)
        high, low = halves(g_far[:, pl.ds(start, rows)])
        g_high[target(2), rows * i : rows * (i + 1)] = high
        g_low[target(2), rows * i : rows * (i + 1)] = low
    kept = [
        pltpu.make_async_copy(g_high, g_high_out, sems.at[4]),
        pltpu.make_async_copy(g_low, g_low_out, sems.at[5]),
    ]
    for copy in kept:
        copy.start()

    def collect(i):
        for c in range(SIDE):
            start = cell_start(odd, (major + i) % SIDE, (minor + c) % SIDE, rows)
            chunk[:, rows * c : rows * (c + 1)] = g_far[:, pl.ds(start, rows)]
        return chunk[...]

    far = None
    for n, i in enumerate((0, 1, 3)):
        span = slice(panel * n, panel * (n + 1))
        term = product(collect(i), e_high[span, :], e_low[span, :], PLAIN)
        far = term if far is None else far + term
    for copy in copies[2:]:
        copy.wait()
    high, low = halves(e_far[:panel, :])
    far = far + product(collect(2), high, low, PLAIN)

    def one(x, y):
        return lax.dot_general(x, y, (PLAIN, ((), ())), preferred_element_type=f32)

    total[...] = near[...] + (one(far_high[...], high) + (one(far_high[...], low) + one(far_low[...], high)))
    for n, j in enumerate((0, 1, 3)):
        part_high, part_low = halves(total[rows * n : rows * (n + 1), :])
        w_high[target(j), :] = part_high
        w_low[target(j), :] = part_low
    part_high, part_low = halves(far)
    w_high[target(2), :] = part_high
    w_low[target(2), :] = part_low
    spread_panel(panels, e_far, panel, lead, (major + 2) % SIDE * rows, rows)
    base[...] = product(panels[:arrow, :], g_high[...], g_low[...], TURNED)
    first = jnp.where(is_first != 0, panels[arrow:, :], 0.0)
    partial[...] = base[...] - product(first, w_high[...], w_low[...], TURNED)
    for copy in kept:
        copy.wait()


def forward_kernel(flag, old, r0, r1, r2, r3, base, w_high, w_low, partial):
    @pl.when(flag[0] != 0)
    def _():
        arrived = (r0[...] + r1[...]) + (r2[...] + r3[...])
        partial[...] = base[...] - product(arrived, w_high[...], w_low[...], TURNED)

    @pl.when(flag[0] == 0)
    def _():
        partial[...] = old[...]


def turn_kernel(place, own, r1, r2, r3, tip, bound, w_high, w_low, rows_out, tip_term, combined, partial):
    arrow_panel = (own[...] + r1[...]) + (r2[...] + r3[...])
    panel_high, panel_low = halves(arrow_panel)
    tip_term[...] = product(tip[...], panel_high, panel_low, PLAIN)
    combined[...] = tip_term[...] + bound[...]
    partial[...] = -product(combined[...], w_high[...], w_low[...], PLAIN)
    width = rows_out.shape[1]
    minor = place[2]
    chosen = arrow_panel[:, :width]
    for j in range(1, SIDE):
        chosen = jnp.where(minor == j, arrow_panel[:, width * j : width * (j + 1)], chosen)
    rows_out[...] = chosen


def backward_kernel(flag, old, r0, r1, r2, r3, tip_term, w_high, w_low, combined, partial):
    @pl.when(flag[0] != 0)
    def _():
        combined[...] = tip_term[...] + ((r0[...] + r1[...]) + (r2[...] + r3[...]))
        partial[...] = -product(combined[...], w_high[...], w_low[...], PLAIN)

    @pl.when(flag[0] == 0)
    def _():
        combined[...] = old[...]
        partial[...] = jnp.zeros_like(partial)


def closing_kernel(
    place, flag, old, r0, r1, r2, r3, tip_term, g_high_in, g_low_in, p0, p1, p2, p3, scratch, g_high, g_low, sems
):
    copies = [
        pltpu.make_async_copy(g_high_in, g_high, sems.at[0]),
        pltpu.make_async_copy(g_low_in, g_low, sems.at[1]),
    ]
    for copy in copies:
        copy.start()
    arrived = (r0[...] + r1[...]) + (r2[...] + r3[...])
    combined = jnp.where(flag[0] != 0, tip_term[...] + arrived, old[...])
    for copy in copies:
        copy.wait()
    scratch[...] = -product(combined, g_high[...], g_low[...], PLAIN)
    width = p0.shape[1]
    major = place[1]
    for k, out in enumerate((p0, p1, p2, p3)):
        start = pl.multiple_of((major + k) % SIDE * width, width)
        out[...] = scratch[:, pl.ds(start, width)]


def call(kernel, scalars, arrays, outs, scratch=(), anywhere=(), vmem=STEP_VMEM, far_outs=()):
    smem = pl.BlockSpec(memory_space=pltpu.SMEM)
    held = pl.BlockSpec(memory_space=pltpu.VMEM)
    return pl.pallas_call(
        kernel,
        out_shape=[jax.ShapeDtypeStruct(shape, dtype) for shape, dtype in [*outs, *far_outs]],
        in_specs=[smem] * len(scalars) + [held] * len(arrays)
        + [pl.BlockSpec(memory_space=pl.ANY)] * len(anywhere),
        out_specs=[held] * len(outs) + [pl.BlockSpec(memory_space=pltpu.HBM)] * len(far_outs),
        scratch_shapes=list(scratch),
        compiler_params=pltpu.CompilerParams(vmem_limit_bytes=vmem),
    )(*scalars, *arrays, *anywhere)


def on_device(ginv, couple, arrow_rhs, arrow_in, tip_cov, bnd_next):
    g_rows = ginv[0]
    e_rows = couple[0]
    rows = g_rows.shape[0]
    panel = rows * SIDE
    arrow = arrow_in.shape[0]
    step = lax.axis_index("dom")
    spot = lax.axis_index("blk")
    odd = step % 2
    z, y = spot // SIDE, spot % SIDE
    major = jnp.where(odd == 0, z, y)
    minor = jnp.where(odd == 0, y, z)
    place = jnp.stack([odd, major, minor, step == 0, step == STEPS - 1]).astype(jnp.int32)
    wide = ((arrow, panel), f32)
    narrow = ((arrow, rows), f32)
    half_block = ((panel, panel), bf16)

    tail = arrow // SIDE
    lead = 2 * tail
    pieces = call(
        pieces_kernel,
        [place],
        [e_rows, bnd_next],
        [((rows, panel), f32)] + [((rows + tail, panel), f32)] * 3,
    )
    got = {k: permuted(pieces[k], by_minor(k)) for k in FARTHEST_FIRST[:-1]}
    g_after = permuted(g_rows, by_minor(-1))
    g_later, rhs, entering, got[2] = lax.optimization_barrier((g_rows, arrow_rhs[0], arrow_in, got[2]))
    (extra,) = call(extra_kernel, [], [rhs, entering], [((lead, panel), f32)])
    g_before = permuted(g_later, by_minor(1))
    e_own = jnp.concatenate([pieces[0], got[3][:rows], got[2][:rows], got[1][:rows], extra])
    e_after, e_before = ring_near(e_own, by_major)
    g_far = ring_far(g_after, g_before, by_minor)
    e_far = ring_far(e_after, e_before, by_major)

    three = panel - rows
    *near, bound = call(
        near_kernel,
        [place],
        [bnd_next],
        [((three, panel), f32)]
        + [((3 * panel, panel), bf16)] * 2
        + [((three, panel), bf16)] * 4
        + [((2 * arrow, panel), f32), wide],
        [
            pltpu.VMEM((three, panel * SIDE), f32),
            pltpu.VMEM((3 * panel, panel), f32),
            pltpu.VMEM((three, panel), f32),
            pltpu.VMEM((3 * lead, panel), f32),
            pltpu.VMEM((3 * tail, panel), f32),
            pltpu.SemaphoreType.DMA((12,)),
        ],
        [g_rows, g_after, g_before, e_own, e_after, e_before, got[1], got[2], got[3]],
        vmem=FORM_VMEM,
    )
    w_high, w_low, base, partial, g_high, g_low = call(
        far_kernel,
        [place],
        near,
        [half_block] * 2 + [wide] * 2,
        [
            pltpu.VMEM((three, panel), f32),
            pltpu.VMEM((rows, panel * SIDE), f32),
            pltpu.VMEM((panel + lead, panel), f32),
            pltpu.VMEM((rows, panel), f32),
            pltpu.VMEM((2 * arrow, panel), f32),
            pltpu.VMEM((panel, panel), bf16),
            pltpu.VMEM((panel, panel), bf16),
            pltpu.SemaphoreType.DMA((6,)),
        ],
        [*g_far, *e_far],
        vmem=FORM_VMEM,
        far_outs=[half_block] * 2,
    )
    for s in range(STEPS - 1):
        arrived = [permuted(partial, to_next(s, k)) for k in FARTHEST_FIRST]
        flag = (step == s + 1).astype(jnp.int32)[None]
        (partial,) = call(forward_kernel, [flag], [partial, *arrived, base, w_high, w_low], [wide])
    arrived = [permuted(partial, by_minor(k)) for k in FARTHEST_FIRST[:-1]]
    arrow_local, tip_term, combined, partial = call(
        turn_kernel,
        [place],
        [partial, *arrived, tip_cov, bound, w_high, w_low],
        [narrow] + [wide] * 3,
    )
    for s in range(STEPS - 1, 0, -1):
        arrived = [permuted(partial, to_earlier(s, k)) for k in FARTHEST_FIRST]
        flag = (step == s - 1).astype(jnp.int32)[None]
        if s > 1:
            combined, partial = call(
                backward_kernel, [flag], [combined, *arrived, tip_term, w_high, w_low], [wide] * 2
            )
    parts = call(
        closing_kernel,
        [place, flag],
        [combined, *arrived, tip_term],
        [narrow] * SIDE,
        [
            pltpu.VMEM(*wide),
            pltpu.VMEM((panel, panel), bf16),
            pltpu.VMEM((panel, panel), bf16),
            pltpu.SemaphoreType.DMA((2,)),
        ],
        [g_high, g_low],
    )
    covariance = parts[0]
    for k in FARTHEST_FIRST[:-1]:
        covariance = covariance + permuted(parts[k], by_major(k))
    return (arrow_local[None], covariance[None])


def solution(mesh):
    return jax.shard_map(
        on_device,
        mesh=mesh,
        in_specs=(
            P("dom", "blk", None),
            P("dom", "blk", None),
            P("dom", None, "blk"),
            P(None, "blk"),
            P(),
            P(None, "blk"),
        ),
        out_specs=(P("dom", None, "blk"), P("dom", None, "blk")),
        check_vma=False,
    )
```

```python
import jax
import jax.numpy as jnp
from jax import lax
from jax.experimental import pallas as pl
from jax.experimental.pallas import tpu as pltpu
from jax.sharding import PartitionSpec as P

both = ("dom", "blk")
SIDE = 4
STEPS = 8
FARTHEST_FIRST = (2, 1, 3, 0)
FORM_VMEM = 16 * 1024 * 1024
STEP_VMEM = 6 * 1024 * 1024
f32 = jnp.float32
bf16 = jnp.bfloat16


def device_of(t, z, y):
    return t * SIDE * SIDE + (z % SIDE) * SIDE + y % SIDE


def pairs(target, steps):
    return [
        (device_of(t, z, y), device_of(*target(t, z, y)))
        for t in steps
        for z in range(SIDE)
        for y in range(SIDE)
    ]


def by_minor(k):
    return pairs(lambda t, z, y: (t, z + k * (t % 2), y + k * (1 - t % 2)), range(STEPS))


def by_major(k):
    return pairs(lambda t, z, y: (t, z + k * (1 - t % 2), y + k * (t % 2)), range(STEPS))


def together(s, groups):
    return next(group for group in groups if s in group)


def to_next(s, k):
    along_z = s % 2
    steps = together(s, ((0, 4), (2, 6), (1, 5), (3,)))
    return pairs(lambda t, z, y: (t + 1, z + k * along_z, y + k * (1 - along_z)), steps)


def to_earlier(s, k):
    along_z = 1 - s % 2
    evens = ((6, 4, 2),) if k < 2 else ((6, 2), (4,))
    steps = together(s, ((7, 3), (5, 1), *evens))
    return pairs(lambda t, z, y: (t - 1, z + k * along_z, y + k * (1 - along_z)), steps)


def permuted(value, where):
    return lax.ppermute(value, both, where)


def ring_near(block, where):
    return permuted(block, where(-1)), permuted(block, where(1))


def ring_far(after, before, where):
    half = after.shape[0] // 2
    return permuted(before[:half], where(1)), permuted(after[half:], where(-1))


def halves(value):
    high = value.astype(bf16)
    return high, (value - high.astype(f32)).astype(bf16)


def product(a, b_high, b_low, dims):
    a_high, a_low = halves(a)

    def one(x, y):
        return lax.dot_general(x, y, (dims, ((), ())), preferred_element_type=f32)

    rows = a.shape[0]
    by_high = one(jnp.concatenate([a_high, a_low]), b_high)
    return by_high[:rows] + (one(a_high, b_low) + by_high[rows:])


PLAIN = ((1,), (0,))
TURNED = ((1,), (1,))


def cell_start(odd, i, j, rows):
    cell = jnp.where(odd != 0, SIDE * j + i, SIDE * i + j)
    return pl.multiple_of(cell * rows, rows)


def pieces_kernel(place, e_ref, bnd, p0, p1, p2, p3):
    rows = e_ref.shape[0]
    odd, minor = place[0], place[2]
    tail = bnd.shape[0] // SIDE
    for i in range(SIDE):
        cols = slice(rows * i, rows * (i + 1))
        for k, out in enumerate((p0, p1, p2, p3)):
            start = cell_start(odd, i, (minor + k) % SIDE, rows)
            out[:rows, cols] = e_ref[:, pl.ds(start, rows)]
            if k:
                out[rows:, cols] = bnd[tail * i : tail * (i + 1), :]


def extra_kernel(rhs, entering, extra):
    height, rows = extra.shape[0], rhs.shape[1]
    for i in range(SIDE):
        source = rhs if i < SIDE // 2 else entering
        top = height * (i % (SIDE // 2))
        extra[:, rows * i : rows * (i + 1)] = source[top : top + height, :]


def spread_panel(out, source, top, height, start, rows):
    cols = pl.ds(pl.multiple_of(start, rows), rows)
    for q in range(SIDE):
        out[height * q : height * (q + 1), cols] = source[top : top + height, rows * q : rows * (q + 1)]


def near_kernel(
    place, bnd, g_own, g_after, g_before, e_own, e_after, e_before, got1, got2, got3,
    total, e_high, e_low, far_high, far_low, block_high, block_low, panels, bound,
    g_near, e_near, chunk, extra, tails, sems,
):
    odd, major, minor, is_last = place[0], place[1], place[2], place[4]
    rows = g_own.shape[0]
    panel = rows * SIDE
    lead, tail = extra.shape[0] // 3, tails.shape[0] // 3
    copies = []
    for n, source in enumerate((g_own, g_after, g_before)):
        copies.append((source, g_near.at[pl.ds(rows * n, rows)]))
    for n, source in enumerate((e_own, e_after, e_before)):
        copies.append((source.at[pl.ds(0, panel)], e_near.at[pl.ds(panel * n, panel)]))
    for n, source in enumerate((e_own, e_after, e_before)):
        copies.append((source.at[pl.ds(panel, lead)], extra.at[pl.ds(lead * n, lead)]))
    for n, source in enumerate((got1, got2, got3)):
        copies.append((source.at[pl.ds(rows, tail)], tails.at[pl.ds(tail * n, tail)]))
    copies = [pltpu.make_async_copy(x, y, sems.at[n]) for n, (x, y) in enumerate(copies)]
    for copy in copies:
        copy.start()
    for copy in copies[:3]:
        copy.wait()

    def collect(i):
        for c in range(SIDE):
            start = cell_start(odd, (major + i) % SIDE, (minor + c) % SIDE, rows)
            chunk[:, rows * c : rows * (c + 1)] = g_near[:, pl.ds(start, rows)]
        return chunk[...]

    high, low = halves(collect(2))
    far_high[...] = high
    far_low[...] = low
    for i in range(SIDE):
        start = cell_start(odd, i, minor, rows)
        high, low = halves(g_near[:, pl.ds(start, rows)])
        block_high[:, rows * i : rows * (i + 1)] = high
        block_low[:, rows * i : rows * (i + 1)] = low
    for n, i in enumerate((0, 1, 3)):
        copies[3 + n].wait()
        span = slice(panel * n, panel * (n + 1))
        high, low = halves(e_near[span, :])
        e_high[span, :] = high
        e_low[span, :] = low
        term = product(collect(i), high, low, PLAIN)
        if n == 0:
            total[...] = term
        else:
            total[...] += term

    for copy in copies[6:]:
        copy.wait()
    for n, i in enumerate((0, 1, 3)):
        spread_panel(panels, extra, lead * n, lead, (major + i) % SIDE * rows, rows)
    spread_panel(panels, extra, 0, lead, (major + 2) % SIDE * rows, rows)
    keep = is_last != 0
    bound[:, pl.ds(pl.multiple_of(minor * rows, rows), rows)] = jnp.where(keep, bnd[...], 0.0)
    for n in range(3):
        spot = (minor - n + SIDE - 1) % SIDE * rows
        spread_panel(bound, tails, tail * n, tail, spot, rows)
    bound[...] = jnp.where(keep, bound[...], 0.0)


def far_kernel(
    place, near, e_high, e_low, far_high, far_low, block_high, block_low, panels_near,
    g_top, g_bottom, e_top, e_bottom,
    w_high, w_low, base, partial, g_high_out, g_low_out,
    total, g_far, e_far, chunk, panels, g_high, g_low, sems,
):
    odd, major, minor, is_first = (place[i] for i in range(4))
    rows = g_far.shape[0]
    panel = rows * SIDE
    half = rows // 2
    lead = e_far.shape[0] - panel
    arrow = panels.shape[0] // 2
    edge = e_far.shape[0] // 2
    copies = [
        (g_top, g_far.at[pl.ds(0, half)]),
        (g_bottom, g_far.at[pl.ds(half, half)]),
        (e_top, e_far.at[pl.ds(0, edge)]),
        (e_bottom, e_far.at[pl.ds(edge, edge)]),
    ]
    copies = [pltpu.make_async_copy(x, y, sems.at[n]) for n, (x, y) in enumerate(copies)]
    for copy in copies:
        copy.start()
    panels[...] = panels_near[...]

    def target(j):
        return pl.ds(pl.multiple_of((minor + j) % SIDE * rows, rows), rows)

    for n, j in enumerate((0, 1, 3)):
        g_high[target(j), :] = block_high[rows * n : rows * (n + 1), :]
        g_low[target(j), :] = block_low[rows * n : rows * (n + 1), :]

    copies[0].wait()
    copies[1].wait()
    for i in range(SIDE):
        start = cell_start(odd, i, minor, rows)
        high, low = halves(g_far[:, pl.ds(start, rows)])
        g_high[target(2), rows * i : rows * (i + 1)] = high
        g_low[target(2), rows * i : rows * (i + 1)] = low
    kept = [
        pltpu.make_async_copy(g_high, g_high_out, sems.at[4]),
        pltpu.make_async_copy(g_low, g_low_out, sems.at[5]),
    ]
    for copy in kept:
        copy.start()

    def collect(i):
        for c in range(SIDE):
            start = cell_start(odd, (major + i) % SIDE, (minor + c) % SIDE, rows)
            chunk[:, rows * c : rows * (c + 1)] = g_far[:, pl.ds(start, rows)]
        return chunk[...]

    far = None
    for n, i in enumerate((0, 1, 3)):
        span = slice(panel * n, panel * (n + 1))
        term = product(collect(i), e_high[span, :], e_low[span, :], PLAIN)
        far = term if far is None else far + term
    for copy in copies[2:]:
        copy.wait()
    high, low = halves(e_far[:panel, :])
    far = far + product(collect(2), high, low, PLAIN)

    def one(x, y):
        return lax.dot_general(x, y, (PLAIN, ((), ())), preferred_element_type=f32)

    total[...] = near[...] + (one(far_high[...], high) + (one(far_high[...], low) + one(far_low[...], high)))
    for n, j in enumerate((0, 1, 3)):
        part_high, part_low = halves(total[rows * n : rows * (n + 1), :])
        w_high[target(j), :] = part_high
        w_low[target(j), :] = part_low
    part_high, part_low = halves(far)
    w_high[target(2), :] = part_high
    w_low[target(2), :] = part_low
    spread_panel(panels, e_far, panel, lead, (major + 2) % SIDE * rows, rows)
    base[...] = product(panels[:arrow, :], g_high[...], g_low[...], TURNED)
    first = jnp.where(is_first != 0, panels[arrow:, :], 0.0)
    partial[...] = base[...] - product(first, w_high[...], w_low[...], TURNED)
    for copy in kept:
        copy.wait()


def forward_kernel(flag, old, r0, r1, r2, r3, base, w_high, w_low, partial):
    @pl.when(flag[0] != 0)
    def _():
        arrived = (r0[...] + r1[...]) + (r2[...] + r3[...])
        partial[...] = base[...] - product(arrived, w_high[...], w_low[...], TURNED)

    @pl.when(flag[0] == 0)
    def _():
        partial[...] = old[...]


def turn_kernel(place, own, r1, r2, r3, tip, bound, w_high, w_low, arrow_panel, combined, partial):
    arrow_panel[...] = (own[...] + r1[...]) + (r2[...] + r3[...])

    @pl.when(place[4] != 0)
    def _():
        panel_high, panel_low = halves(arrow_panel[...])
        combined[...] = product(tip[...], panel_high, panel_low, PLAIN) + bound[...]
        partial[...] = -product(combined[...], w_high[...], w_low[...], PLAIN)

    @pl.when(place[4] == 0)
    def _():
        combined[...] = jnp.zeros_like(combined)
        partial[...] = jnp.zeros_like(partial)


def tip_kernel(place, arrow_panel, tip, tip_term, rows_out):
    panel_high, panel_low = halves(arrow_panel[...])
    tip_term[...] = product(tip[...], panel_high, panel_low, PLAIN)
    width = rows_out.shape[1]
    start = pl.multiple_of(place[2] * width, width)
    rows_out[...] = arrow_panel[:, pl.ds(start, width)]


def backward_kernel(flag, old, r0, r1, r2, r3, tip_term, w_high, w_low, combined, partial):
    @pl.when(flag[0] != 0)
    def _():
        combined[...] = tip_term[...] + ((r0[...] + r1[...]) + (r2[...] + r3[...]))
        partial[...] = -product(combined[...], w_high[...], w_low[...], PLAIN)

    @pl.when(flag[0] == 0)
    def _():
        combined[...] = old[...]
        partial[...] = jnp.zeros_like(partial)


def closing_kernel(
    place, flag, old, r0, r1, r2, r3, tip_term, g_high_in, g_low_in, p0, p1, p2, p3, scratch, g_high, g_low, sems
):
    copies = [
        pltpu.make_async_copy(g_high_in, g_high, sems.at[0]),
        pltpu.make_async_copy(g_low_in, g_low, sems.at[1]),
    ]
    for copy in copies:
        copy.start()
    arrived = (r0[...] + r1[...]) + (r2[...] + r3[...])
    combined = jnp.where(flag[0] != 0, tip_term[...] + arrived, old[...])
    for copy in copies:
        copy.wait()
    scratch[...] = -product(combined, g_high[...], g_low[...], PLAIN)
    width = p0.shape[1]
    major = place[1]
    for k, out in enumerate((p0, p1, p2, p3)):
        start = pl.multiple_of((major + k) % SIDE * width, width)
        out[...] = scratch[:, pl.ds(start, width)]


def call(kernel, scalars, arrays, outs, scratch=(), anywhere=(), vmem=STEP_VMEM, far_outs=()):
    smem = pl.BlockSpec(memory_space=pltpu.SMEM)
    held = pl.BlockSpec(memory_space=pltpu.VMEM)
    return pl.pallas_call(
        kernel,
        out_shape=[jax.ShapeDtypeStruct(shape, dtype) for shape, dtype in [*outs, *far_outs]],
        in_specs=[smem] * len(scalars) + [held] * len(arrays)
        + [pl.BlockSpec(memory_space=pl.ANY)] * len(anywhere),
        out_specs=[held] * len(outs) + [pl.BlockSpec(memory_space=pltpu.HBM)] * len(far_outs),
        scratch_shapes=list(scratch),
        compiler_params=pltpu.CompilerParams(vmem_limit_bytes=vmem),
    )(*scalars, *arrays, *anywhere)


def on_device(ginv, couple, arrow_rhs, arrow_in, tip_cov, bnd_next):
    g_rows = ginv[0]
    e_rows = couple[0]
    rows = g_rows.shape[0]
    panel = rows * SIDE
    arrow = arrow_in.shape[0]
    step = lax.axis_index("dom")
    spot = lax.axis_index("blk")
    odd = step % 2
    z, y = spot // SIDE, spot % SIDE
    major = jnp.where(odd == 0, z, y)
    minor = jnp.where(odd == 0, y, z)
    place = jnp.stack([odd, major, minor, step == 0, step == STEPS - 1]).astype(jnp.int32)
    wide = ((arrow, panel), f32)
    narrow = ((arrow, rows), f32)
    half_block = ((panel, panel), bf16)

    tail = arrow // SIDE
    lead = 2 * tail
    pieces = call(
        pieces_kernel,
        [place],
        [e_rows, bnd_next],
        [((rows, panel), f32)] + [((rows + tail, panel), f32)] * 3,
    )
    got = {k: permuted(pieces[k], by_minor(k)) for k in FARTHEST_FIRST[:-1]}
    g_after = permuted(g_rows, by_minor(-1))
    g_later, rhs, entering, got[2] = lax.optimization_barrier((g_rows, arrow_rhs[0], arrow_in, got[2]))
    (extra,) = call(extra_kernel, [], [rhs, entering], [((lead, panel), f32)])
    g_before = permuted(g_later, by_minor(1))
    e_own = jnp.concatenate([pieces[0], got[3][:rows], got[2][:rows], got[1][:rows], extra])
    e_after, e_before = ring_near(e_own, by_major)
    g_far = ring_far(g_after, g_before, by_minor)
    e_far = ring_far(e_after, e_before, by_major)

    three = panel - rows
    *near, bound = call(
        near_kernel,
        [place],
        [bnd_next],
        [((three, panel), f32)]
        + [((3 * panel, panel), bf16)] * 2
        + [((three, panel), bf16)] * 4
        + [((2 * arrow, panel), f32), wide],
        [
            pltpu.VMEM((three, panel * SIDE), f32),
            pltpu.VMEM((3 * panel, panel), f32),
            pltpu.VMEM((three, panel), f32),
            pltpu.VMEM((3 * lead, panel), f32),
            pltpu.VMEM((3 * tail, panel), f32),
            pltpu.SemaphoreType.DMA((12,)),
        ],
        [g_rows, g_after, g_before, e_own, e_after, e_before, got[1], got[2], got[3]],
        vmem=FORM_VMEM,
    )
    w_high, w_low, base, partial, g_high, g_low = call(
        far_kernel,
        [place],
        near,
        [half_block] * 2 + [wide] * 2,
        [
            pltpu.VMEM((three, panel), f32),
            pltpu.VMEM((rows, panel * SIDE), f32),
            pltpu.VMEM((panel + lead, panel), f32),
            pltpu.VMEM((rows, panel), f32),
            pltpu.VMEM((2 * arrow, panel), f32),
            pltpu.VMEM((panel, panel), bf16),
            pltpu.VMEM((panel, panel), bf16),
            pltpu.SemaphoreType.DMA((6,)),
        ],
        [*g_far, *e_far],
        vmem=FORM_VMEM,
        far_outs=[half_block] * 2,
    )
    for s in range(STEPS - 1):
        arrived = [permuted(partial, to_next(s, k)) for k in FARTHEST_FIRST]
        flag = (step == s + 1).astype(jnp.int32)[None]
        (partial,) = call(forward_kernel, [flag], [partial, *arrived, base, w_high, w_low], [wide])
    arrived = [permuted(partial, by_minor(k)) for k in FARTHEST_FIRST[:-1]]
    arrow_panel, combined, partial = call(
        turn_kernel,
        [place],
        [partial, *arrived, tip_cov, bound, w_high, w_low],
        [wide] * 3,
    )
    tip_term, arrow_local = call(tip_kernel, [place], [arrow_panel, tip_cov], [wide, narrow])
    for s in range(STEPS - 1, 0, -1):
        arrived = [permuted(partial, to_earlier(s, k)) for k in FARTHEST_FIRST]
        flag = (step == s - 1).astype(jnp.int32)[None]
        if s > 1:
            combined, partial = call(
                backward_kernel, [flag], [combined, *arrived, tip_term, w_high, w_low], [wide] * 2
            )
    parts = call(
        closing_kernel,
        [place, flag],
        [combined, *arrived, tip_term],
        [narrow] * SIDE,
        [
            pltpu.VMEM(*wide),
            pltpu.VMEM((panel, panel), bf16),
            pltpu.VMEM((panel, panel), bf16),
            pltpu.SemaphoreType.DMA((2,)),
        ],
        [g_high, g_low],
    )
    covariance = parts[0]
    for k in FARTHEST_FIRST[:-1]:
        covariance = covariance + permuted(parts[k], by_major(k))
    return (arrow_local[None], covariance[None])


def solution(mesh):
    return jax.shard_map(
        on_device,
        mesh=mesh,
        in_specs=(
            P("dom", "blk", None),
            P("dom", "blk", None),
            P("dom", None, "blk"),
            P(None, "blk"),
            P(),
            P(None, "blk"),
        ),
        out_specs=(P("dom", None, "blk"), P("dom", None, "blk")),
        check_vma=False,
    )
```

```python
import jax
import jax.numpy as jnp
from jax import lax
from jax.experimental import pallas as pl
from jax.experimental.pallas import tpu as pltpu
from jax.sharding import PartitionSpec as P

both = ("dom", "blk")
SIDE = 4
STEPS = 8
FARTHEST_FIRST = (2, 3, 1, 0)
FORM_VMEM = 16 * 1024 * 1024
STEP_VMEM = 6 * 1024 * 1024
f32 = jnp.float32
bf16 = jnp.bfloat16


def device_of(t, z, y):
    return t * SIDE * SIDE + (z % SIDE) * SIDE + y % SIDE


def pairs(target, steps):
    return [
        (device_of(t, z, y), device_of(*target(t, z, y)))
        for t in steps
        for z in range(SIDE)
        for y in range(SIDE)
    ]


def by_minor(k):
    return pairs(lambda t, z, y: (t, z + k * (t % 2), y + k * (1 - t % 2)), range(STEPS))


def by_major(k):
    return pairs(lambda t, z, y: (t, z + k * (1 - t % 2), y + k * (t % 2)), range(STEPS))


def together(s, groups):
    return next(group for group in groups if s in group)


def to_next(s, k):
    along_z = s % 2
    steps = together(s, ((0, 4), (2, 6), (1, 5), (3,)))
    return pairs(lambda t, z, y: (t + 1, z + k * along_z, y + k * (1 - along_z)), steps)


def to_earlier(s, k):
    along_z = 1 - s % 2
    evens = ((6, 4, 2),) if k < 2 else ((6, 2), (4,))
    steps = together(s, ((7, 3), (5, 1), *evens))
    return pairs(lambda t, z, y: (t - 1, z + k * along_z, y + k * (1 - along_z)), steps)


def permuted(value, where):
    return lax.ppermute(value, both, where)


def ring_near(block, where):
    return permuted(block, where(-1)), permuted(block, where(1))


def ring_far(after, before, where):
    half = after.shape[0] // 2
    return permuted(before[:half], where(1)), permuted(after[half:], where(-1))


def halves(value):
    high = value.astype(bf16)
    return high, (value - high.astype(f32)).astype(bf16)


def product(a, b_high, b_low, dims):
    a_high, a_low = halves(a)

    def one(x, y):
        return lax.dot_general(x, y, (dims, ((), ())), preferred_element_type=f32)

    rows = a.shape[0]
    by_high = one(jnp.concatenate([a_high, a_low]), b_high)
    return by_high[:rows] + (one(a_high, b_low) + by_high[rows:])


PLAIN = ((1,), (0,))
TURNED = ((1,), (1,))


def cell_start(odd, i, j, rows):
    cell = jnp.where(odd != 0, SIDE * j + i, SIDE * i + j)
    return pl.multiple_of(cell * rows, rows)


def pieces_kernel(place, e_ref, bnd, p0, p1, p2, p3):
    rows = e_ref.shape[0]
    odd, minor = place[0], place[2]
    tail = bnd.shape[0] // SIDE
    for i in range(SIDE):
        cols = slice(rows * i, rows * (i + 1))
        for k, out in enumerate((p0, p1, p2, p3)):
            start = cell_start(odd, i, (minor + k) % SIDE, rows)
            out[:rows, cols] = e_ref[:, pl.ds(start, rows)]
            if k:
                out[rows:, cols] = bnd[tail * i : tail * (i + 1), :]


def extra_kernel(rhs, entering, extra):
    height, rows = extra.shape[0], rhs.shape[1]
    for i in range(SIDE):
        source = rhs if i < SIDE // 2 else entering
        top = height * (i % (SIDE // 2))
        extra[:, rows * i : rows * (i + 1)] = source[top : top + height, :]


def spread_panel(out, source, top, height, start, rows):
    cols = pl.ds(pl.multiple_of(start, rows), rows)
    for q in range(SIDE):
        out[height * q : height * (q + 1), cols] = source[top : top + height, rows * q : rows * (q + 1)]


def near_kernel(
    place, bnd, g_own, g_after, g_before, e_own, e_after, e_before, got1, got2, got3,
    total, e_high, e_low, far_high, far_low, block_high, block_low, panels, bound,
    g_near, e_near, chunk, extra, tails, sems,
):
    odd, major, minor, is_last = place[0], place[1], place[2], place[4]
    rows = g_own.shape[0]
    panel = rows * SIDE
    lead, tail = extra.shape[0] // 3, tails.shape[0] // 3
    copies = []
    for n, source in enumerate((g_own, g_after, g_before)):
        copies.append((source, g_near.at[pl.ds(rows * n, rows)]))
    for n, source in enumerate((e_own, e_after, e_before)):
        copies.append((source.at[pl.ds(0, panel)], e_near.at[pl.ds(panel * n, panel)]))
    for n, source in enumerate((e_own, e_after, e_before)):
        copies.append((source.at[pl.ds(panel, lead)], extra.at[pl.ds(lead * n, lead)]))
    for n, source in enumerate((got1, got2, got3)):
        copies.append((source.at[pl.ds(rows, tail)], tails.at[pl.ds(tail * n, tail)]))
    copies = [pltpu.make_async_copy(x, y, sems.at[n]) for n, (x, y) in enumerate(copies)]
    for copy in copies:
        copy.start()
    for copy in copies[:3]:
        copy.wait()

    def collect(i):
        for c in range(SIDE):
            start = cell_start(odd, (major + i) % SIDE, (minor + c) % SIDE, rows)
            chunk[:, rows * c : rows * (c + 1)] = g_near[:, pl.ds(start, rows)]
        return chunk[...]

    high, low = halves(collect(2))
    far_high[...] = high
    far_low[...] = low
    for i in range(SIDE):
        start = cell_start(odd, i, minor, rows)
        high, low = halves(g_near[:, pl.ds(start, rows)])
        block_high[:, rows * i : rows * (i + 1)] = high
        block_low[:, rows * i : rows * (i + 1)] = low
    for n, i in enumerate((0, 1, 3)):
        copies[3 + n].wait()
        span = slice(panel * n, panel * (n + 1))
        high, low = halves(e_near[span, :])
        e_high[span, :] = high
        e_low[span, :] = low
        term = product(collect(i), high, low, PLAIN)
        if n == 0:
            total[...] = term
        else:
            total[...] += term

    for copy in copies[6:]:
        copy.wait()
    for n, i in enumerate((0, 1, 3)):
        spread_panel(panels, extra, lead * n, lead, (major + i) % SIDE * rows, rows)
    spread_panel(panels, extra, 0, lead, (major + 2) % SIDE * rows, rows)
    keep = is_last != 0
    bound[:, pl.ds(pl.multiple_of(minor * rows, rows), rows)] = jnp.where(keep, bnd[...], 0.0)
    for n in range(3):
        spot = (minor - n + SIDE - 1) % SIDE * rows
        spread_panel(bound, tails, tail * n, tail, spot, rows)
    bound[...] = jnp.where(keep, bound[...], 0.0)


def far_kernel(
    place, near, e_high, e_low, far_high, far_low, block_high, block_low, panels_near,
    g_top, g_bottom, e_top, e_bottom,
    w_high, w_low, base, partial, g_high_out, g_low_out,
    total, g_far, e_far, chunk, panels, g_high, g_low, sems,
):
    odd, major, minor, is_first = (place[i] for i in range(4))
    rows = g_far.shape[0]
    panel = rows * SIDE
    half = rows // 2
    lead = e_far.shape[0] - panel
    arrow = panels.shape[0] // 2
    edge = e_far.shape[0] // 2
    copies = [
        (g_top, g_far.at[pl.ds(0, half)]),
        (g_bottom, g_far.at[pl.ds(half, half)]),
        (e_top, e_far.at[pl.ds(0, edge)]),
        (e_bottom, e_far.at[pl.ds(edge, edge)]),
    ]
    copies = [pltpu.make_async_copy(x, y, sems.at[n]) for n, (x, y) in enumerate(copies)]
    for copy in copies:
        copy.start()
    panels[...] = panels_near[...]

    def target(j):
        return pl.ds(pl.multiple_of((minor + j) % SIDE * rows, rows), rows)

    for n, j in enumerate((0, 1, 3)):
        g_high[target(j), :] = block_high[rows * n : rows * (n + 1), :]
        g_low[target(j), :] = block_low[rows * n : rows * (n + 1), :]

    copies[0].wait()
    copies[1].wait()
    for i in range(SIDE):
        start = cell_start(odd, i, minor, rows)
        high, low = halves(g_far[:, pl.ds(start, rows)])
        g_high[target(2), rows * i : rows * (i + 1)] = high
        g_low[target(2), rows * i : rows * (i + 1)] = low
    kept = [
        pltpu.make_async_copy(g_high, g_high_out, sems.at[4]),
        pltpu.make_async_copy(g_low, g_low_out, sems.at[5]),
    ]
    for copy in kept:
        copy.start()

    def collect(i):
        for c in range(SIDE):
            start = cell_start(odd, (major + i) % SIDE, (minor + c) % SIDE, rows)
            chunk[:, rows * c : rows * (c + 1)] = g_far[:, pl.ds(start, rows)]
        return chunk[...]

    far = None
    for n, i in enumerate((0, 1, 3)):
        span = slice(panel * n, panel * (n + 1))
        term = product(collect(i), e_high[span, :], e_low[span, :], PLAIN)
        far = term if far is None else far + term
    for copy in copies[2:]:
        copy.wait()
    high, low = halves(e_far[:panel, :])
    far = far + product(collect(2), high, low, PLAIN)

    def one(x, y):
        return lax.dot_general(x, y, (PLAIN, ((), ())), preferred_element_type=f32)

    total[...] = near[...] + (one(far_high[...], high) + (one(far_high[...], low) + one(far_low[...], high)))
    for n, j in enumerate((0, 1, 3)):
        part_high, part_low = halves(total[rows * n : rows * (n + 1), :])
        w_high[target(j), :] = part_high
        w_low[target(j), :] = part_low
    part_high, part_low = halves(far)
    w_high[target(2), :] = part_high
    w_low[target(2), :] = part_low
    spread_panel(panels, e_far, panel, lead, (major + 2) % SIDE * rows, rows)
    base[...] = product(panels[:arrow, :], g_high[...], g_low[...], TURNED)
    first = jnp.where(is_first != 0, panels[arrow:, :], 0.0)
    partial[...] = base[...] - product(first, w_high[...], w_low[...], TURNED)
    for copy in kept:
        copy.wait()


def forward_kernel(flag, old, r0, r1, r2, r3, base, w_high, w_low, partial):
    @pl.when(flag[0] != 0)
    def _():
        arrived = (r0[...] + r1[...]) + (r2[...] + r3[...])
        partial[...] = base[...] - product(arrived, w_high[...], w_low[...], TURNED)

    @pl.when(flag[0] == 0)
    def _():
        partial[...] = old[...]


def turn_kernel(place, own, r1, r2, r3, tip, bound, w_high, w_low, arrow_panel, combined, partial):
    arrow_panel[...] = (own[...] + r1[...]) + (r2[...] + r3[...])

    @pl.when(place[4] != 0)
    def _():
        panel_high, panel_low = halves(arrow_panel[...])
        combined[...] = product(tip[...], panel_high, panel_low, PLAIN) + bound[...]
        partial[...] = -product(combined[...], w_high[...], w_low[...], PLAIN)

    @pl.when(place[4] == 0)
    def _():
        combined[...] = jnp.zeros_like(combined)
        partial[...] = jnp.zeros_like(partial)


def tip_kernel(place, arrow_panel, tip, tip_term, rows_out):
    panel_high, panel_low = halves(arrow_panel[...])
    tip_term[...] = product(tip[...], panel_high, panel_low, PLAIN)
    width = rows_out.shape[1]
    start = pl.multiple_of(place[2] * width, width)
    rows_out[...] = arrow_panel[:, pl.ds(start, width)]


def backward_kernel(flag, old, r0, r1, r2, r3, tip_term, w_high, w_low, combined, partial):
    @pl.when(flag[0] != 0)
    def _():
        combined[...] = tip_term[...] + ((r0[...] + r1[...]) + (r2[...] + r3[...]))
        partial[...] = -product(combined[...], w_high[...], w_low[...], PLAIN)

    @pl.when(flag[0] == 0)
    def _():
        combined[...] = old[...]
        partial[...] = jnp.zeros_like(partial)


def closing_kernel(
    place, flag, old, r0, r1, r2, r3, tip_term, g_high_in, g_low_in, p0, p1, p2, p3, scratch, g_high, g_low, sems
):
    copies = [
        pltpu.make_async_copy(g_high_in, g_high, sems.at[0]),
        pltpu.make_async_copy(g_low_in, g_low, sems.at[1]),
    ]
    for copy in copies:
        copy.start()
    arrived = (r0[...] + r1[...]) + (r2[...] + r3[...])
    combined = jnp.where(flag[0] != 0, tip_term[...] + arrived, old[...])
    high, low = halves(combined)
    count = combined.shape[0]

    def one(x, y):
        return lax.dot_general(x, y, (PLAIN, ((), ())), preferred_element_type=f32)

    copies[0].wait()
    by_high = one(jnp.concatenate([high, low]), g_high[...])
    copies[1].wait()
    scratch[...] = -(by_high[:count] + (one(high, g_low[...]) + by_high[count:]))
    width = p0.shape[1]
    major = place[1]
    for k, out in enumerate((p0, p1, p2, p3)):
        start = pl.multiple_of((major + k) % SIDE * width, width)
        out[...] = scratch[:, pl.ds(start, width)]


def call(kernel, scalars, arrays, outs, scratch=(), anywhere=(), vmem=STEP_VMEM, far_outs=()):
    smem = pl.BlockSpec(memory_space=pltpu.SMEM)
    held = pl.BlockSpec(memory_space=pltpu.VMEM)
    return pl.pallas_call(
        kernel,
        out_shape=[jax.ShapeDtypeStruct(shape, dtype) for shape, dtype in [*outs, *far_outs]],
        in_specs=[smem] * len(scalars) + [held] * len(arrays)
        + [pl.BlockSpec(memory_space=pl.ANY)] * len(anywhere),
        out_specs=[held] * len(outs) + [pl.BlockSpec(memory_space=pltpu.HBM)] * len(far_outs),
        scratch_shapes=list(scratch),
        compiler_params=pltpu.CompilerParams(vmem_limit_bytes=vmem),
    )(*scalars, *arrays, *anywhere)


def on_device(ginv, couple, arrow_rhs, arrow_in, tip_cov, bnd_next):
    g_rows = ginv[0]
    e_rows = couple[0]
    rows = g_rows.shape[0]
    panel = rows * SIDE
    arrow = arrow_in.shape[0]
    step = lax.axis_index("dom")
    spot = lax.axis_index("blk")
    odd = step % 2
    z, y = spot // SIDE, spot % SIDE
    major = jnp.where(odd == 0, z, y)
    minor = jnp.where(odd == 0, y, z)
    place = jnp.stack([odd, major, minor, step == 0, step == STEPS - 1]).astype(jnp.int32)
    wide = ((arrow, panel), f32)
    narrow = ((arrow, rows), f32)
    half_block = ((panel, panel), bf16)

    tail = arrow // SIDE
    lead = 2 * tail
    pieces = call(
        pieces_kernel,
        [place],
        [e_rows, bnd_next],
        [((rows, panel), f32)] + [((rows + tail, panel), f32)] * 3,
    )
    got = {k: permuted(pieces[k], by_minor(k)) for k in FARTHEST_FIRST[:-1]}
    g_after = permuted(g_rows, by_minor(-1))
    g_later, rhs, entering, got[2] = lax.optimization_barrier((g_rows, arrow_rhs[0], arrow_in, got[2]))
    (extra,) = call(extra_kernel, [], [rhs, entering], [((lead, panel), f32)])
    g_before = permuted(g_later, by_minor(1))
    e_own = jnp.concatenate([pieces[0], got[3][:rows], got[2][:rows], got[1][:rows], extra])
    e_after, e_before = ring_near(e_own, by_major)
    g_far = ring_far(g_after, g_before, by_minor)
    e_far = ring_far(e_after, e_before, by_major)

    three = panel - rows
    *near, bound = call(
        near_kernel,
        [place],
        [bnd_next],
        [((three, panel), f32)]
        + [((3 * panel, panel), bf16)] * 2
        + [((three, panel), bf16)] * 4
        + [((2 * arrow, panel), f32), wide],
        [
            pltpu.VMEM((three, panel * SIDE), f32),
            pltpu.VMEM((3 * panel, panel), f32),
            pltpu.VMEM((three, panel), f32),
            pltpu.VMEM((3 * lead, panel), f32),
            pltpu.VMEM((3 * tail, panel), f32),
            pltpu.SemaphoreType.DMA((12,)),
        ],
        [g_rows, g_after, g_before, e_own, e_after, e_before, got[1], got[2], got[3]],
        vmem=FORM_VMEM,
    )
    w_high, w_low, base, partial, g_high, g_low = call(
        far_kernel,
        [place],
        near,
        [half_block] * 2 + [wide] * 2,
        [
            pltpu.VMEM((three, panel), f32),
            pltpu.VMEM((rows, panel * SIDE), f32),
            pltpu.VMEM((panel + lead, panel), f32),
            pltpu.VMEM((rows, panel), f32),
            pltpu.VMEM((2 * arrow, panel), f32),
            pltpu.VMEM((panel, panel), bf16),
            pltpu.VMEM((panel, panel), bf16),
            pltpu.SemaphoreType.DMA((6,)),
        ],
        [*g_far, *e_far],
        vmem=FORM_VMEM,
        far_outs=[half_block] * 2,
    )
    for s in range(STEPS - 1):
        arrived = [permuted(partial, to_next(s, k)) for k in FARTHEST_FIRST]
        flag = (step == s + 1).astype(jnp.int32)[None]
        (partial,) = call(forward_kernel, [flag], [partial, *arrived, base, w_high, w_low], [wide])
    arrived = [permuted(partial, by_minor(k)) for k in FARTHEST_FIRST[:-1]]
    arrow_panel, combined, partial = call(
        turn_kernel,
        [place],
        [partial, *arrived, tip_cov, bound, w_high, w_low],
        [wide] * 3,
    )
    tip_term, arrow_local = call(tip_kernel, [place], [arrow_panel, tip_cov], [wide, narrow])
    for s in range(STEPS - 1, 0, -1):
        arrived = [permuted(partial, to_earlier(s, k)) for k in FARTHEST_FIRST]
        flag = (step == s - 1).astype(jnp.int32)[None]
        if s > 1:
            combined, partial = call(
                backward_kernel, [flag], [combined, *arrived, tip_term, w_high, w_low], [wide] * 2
            )
    parts = call(
        closing_kernel,
        [place, flag],
        [combined, *arrived, tip_term],
        [narrow] * SIDE,
        [
            pltpu.VMEM(*wide),
            pltpu.VMEM((panel, panel), bf16),
            pltpu.VMEM((panel, panel), bf16),
            pltpu.SemaphoreType.DMA((2,)),
        ],
        [g_high, g_low],
    )
    covariance = parts[0]
    for k in FARTHEST_FIRST[:-1]:
        covariance = covariance + permuted(parts[k], by_major(k))
    return (arrow_local[None], covariance[None])


def solution(mesh):
    return jax.shard_map(
        on_device,
        mesh=mesh,
        in_specs=(
            P("dom", "blk", None),
            P("dom", "blk", None),
            P("dom", None, "blk"),
            P(None, "blk"),
            P(),
            P(None, "blk"),
        ),
        out_specs=(P("dom", None, "blk"), P("dom", None, "blk")),
        check_vma=False,
    )
```

```python
import jax
import jax.numpy as jnp
from jax import lax
from jax.experimental import pallas as pl
from jax.experimental.pallas import tpu as pltpu
from jax.sharding import PartitionSpec as P

both = ("dom", "blk")
SIDE = 4
STEPS = 8
FARTHEST_FIRST = (2, 1, 3, 0)
FORM_VMEM = 16 * 1024 * 1024
STEP_VMEM = 6 * 1024 * 1024
f32 = jnp.float32
bf16 = jnp.bfloat16


def device_of(t, z, y):
    return t * SIDE * SIDE + (z % SIDE) * SIDE + y % SIDE


def pairs(target, steps):
    return [
        (device_of(t, z, y), device_of(*target(t, z, y)))
        for t in steps
        for z in range(SIDE)
        for y in range(SIDE)
    ]


def by_minor(k):
    return pairs(lambda t, z, y: (t, z + k * (t % 2), y + k * (1 - t % 2)), range(STEPS))


def by_major(k):
    return pairs(lambda t, z, y: (t, z + k * (1 - t % 2), y + k * (t % 2)), range(STEPS))


def together(s, groups):
    return next(group for group in groups if s in group)


def to_next(s, k):
    along_z = s % 2
    steps = together(s, ((0, 4), (2, 6), (1, 5), (3,)))
    return pairs(lambda t, z, y: (t + 1, z + k * along_z, y + k * (1 - along_z)), steps)


def to_earlier(s, k):
    along_z = 1 - s % 2
    evens = ((6, 4, 2),) if k < 2 else ((6, 2), (4,))
    steps = together(s, ((7, 3), (5, 1), *evens))
    return pairs(lambda t, z, y: (t - 1, z + k * along_z, y + k * (1 - along_z)), steps)


def permuted(value, where):
    return lax.ppermute(value, both, where)


def ring_near(block, where):
    return permuted(block, where(-1)), permuted(block, where(1))


def ring_far(after, before, where):
    half = after.shape[0] // 2
    return permuted(before[:half], where(1)), permuted(after[half:], where(-1))


def halves(value):
    high = value.astype(bf16)
    return high, (value - high.astype(f32)).astype(bf16)


def product(a, b_high, b_low, dims):
    a_high, a_low = halves(a)

    def one(x, y):
        return lax.dot_general(x, y, (dims, ((), ())), preferred_element_type=f32)

    rows = a.shape[0]
    by_high = one(jnp.concatenate([a_high, a_low]), b_high)
    return by_high[:rows] + (one(a_high, b_low) + by_high[rows:])


PLAIN = ((1,), (0,))
TURNED = ((1,), (1,))


def cell_start(odd, i, j, rows):
    cell = jnp.where(odd != 0, SIDE * j + i, SIDE * i + j)
    return pl.multiple_of(cell * rows, rows)


def pieces_kernel(place, e_ref, bnd, p0, p1, p2, p3):
    rows = e_ref.shape[0]
    odd, minor = place[0], place[2]
    tail = bnd.shape[0] // SIDE
    for i in range(SIDE):
        cols = slice(rows * i, rows * (i + 1))
        for k, out in enumerate((p0, p1, p2, p3)):
            start = cell_start(odd, i, (minor + k) % SIDE, rows)
            out[:rows, cols] = e_ref[:, pl.ds(start, rows)]
            if k:
                out[rows:, cols] = bnd[tail * i : tail * (i + 1), :]


def extra_kernel(rhs, entering, extra):
    height, rows = extra.shape[0], rhs.shape[1]
    for i in range(SIDE):
        source = rhs if i < SIDE // 2 else entering
        top = height * (i % (SIDE // 2))
        extra[:, rows * i : rows * (i + 1)] = source[top : top + height, :]


def spread_panel(out, source, top, height, start, rows):
    cols = pl.ds(pl.multiple_of(start, rows), rows)
    for q in range(SIDE):
        out[height * q : height * (q + 1), cols] = source[top : top + height, rows * q : rows * (q + 1)]


def near_kernel(
    place, bnd, g_own, g_after, g_before, e_own, e_after, e_before, got1, got2, got3,
    total, e_high, e_low, far_high, far_low, block_high, block_low, panels, bound,
    g_near, e_near, chunk, extra, tails, sems,
):
    odd, major, minor, is_last = place[0], place[1], place[2], place[4]
    rows = g_own.shape[0]
    panel = rows * SIDE
    lead, tail = extra.shape[0] // 3, tails.shape[0] // 3
    copies = []
    for n, source in enumerate((g_own, g_after, g_before)):
        copies.append((source, g_near.at[pl.ds(rows * n, rows)]))
    for n, source in enumerate((e_own, e_after, e_before)):
        copies.append((source.at[pl.ds(0, panel)], e_near.at[pl.ds(panel * n, panel)]))
    for n, source in enumerate((e_own, e_after, e_before)):
        copies.append((source.at[pl.ds(panel, lead)], extra.at[pl.ds(lead * n, lead)]))
    for n, source in enumerate((got1, got2, got3)):
        copies.append((source.at[pl.ds(rows, tail)], tails.at[pl.ds(tail * n, tail)]))
    copies = [pltpu.make_async_copy(x, y, sems.at[n]) for n, (x, y) in enumerate(copies)]
    for copy in copies:
        copy.start()
    for copy in copies[:3]:
        copy.wait()

    def collect(i):
        for c in range(SIDE):
            start = cell_start(odd, (major + i) % SIDE, (minor + c) % SIDE, rows)
            chunk[:, rows * c : rows * (c + 1)] = g_near[:, pl.ds(start, rows)]
        return chunk[...]

    high, low = halves(collect(2))
    far_high[...] = high
    far_low[...] = low
    for i in range(SIDE):
        start = cell_start(odd, i, minor, rows)
        high, low = halves(g_near[:, pl.ds(start, rows)])
        block_high[:, rows * i : rows * (i + 1)] = high
        block_low[:, rows * i : rows * (i + 1)] = low
    for n, i in enumerate((0, 1, 3)):
        copies[3 + n].wait()
        span = slice(panel * n, panel * (n + 1))
        high, low = halves(e_near[span, :])
        e_high[span, :] = high
        e_low[span, :] = low
        term = product(collect(i), high, low, PLAIN)
        if n == 0:
            total[...] = term
        else:
            total[...] += term

    for copy in copies[6:]:
        copy.wait()
    for n, i in enumerate((0, 1, 3)):
        spread_panel(panels, extra, lead * n, lead, (major + i) % SIDE * rows, rows)
    spread_panel(panels, extra, 0, lead, (major + 2) % SIDE * rows, rows)
    keep = is_last != 0
    bound[:, pl.ds(pl.multiple_of(minor * rows, rows), rows)] = jnp.where(keep, bnd[...], 0.0)
    for n in range(3):
        spot = (minor - n + SIDE - 1) % SIDE * rows
        spread_panel(bound, tails, tail * n, tail, spot, rows)
    bound[...] = jnp.where(keep, bound[...], 0.0)


def far_kernel(
    place, near, e_high, e_low, far_high, far_low, block_high, block_low, panels_near,
    g_top, g_bottom, e_top, e_bottom,
    w_high, w_low, base, partial, g_high_out, g_low_out,
    total, g_far, e_far, chunk, panels, g_high, g_low, sems,
):
    odd, major, minor, is_first = (place[i] for i in range(4))
    rows = g_far.shape[0]
    panel = rows * SIDE
    half = rows // 2
    lead = e_far.shape[0] - panel
    arrow = panels.shape[0] // 2
    edge = e_far.shape[0] // 2
    copies = [
        (g_top, g_far.at[pl.ds(0, half)]),
        (g_bottom, g_far.at[pl.ds(half, half)]),
        (e_top, e_far.at[pl.ds(0, edge)]),
        (e_bottom, e_far.at[pl.ds(edge, edge)]),
    ]
    copies = [pltpu.make_async_copy(x, y, sems.at[n]) for n, (x, y) in enumerate(copies)]
    for copy in copies:
        copy.start()
    panels[...] = panels_near[...]

    def target(j):
        return pl.ds(pl.multiple_of((minor + j) % SIDE * rows, rows), rows)

    for n, j in enumerate((0, 1, 3)):
        g_high[target(j), :] = block_high[rows * n : rows * (n + 1), :]
        g_low[target(j), :] = block_low[rows * n : rows * (n + 1), :]

    copies[0].wait()
    copies[1].wait()
    for i in range(SIDE):
        start = cell_start(odd, i, minor, rows)
        high, low = halves(g_far[:, pl.ds(start, rows)])
        g_high[target(2), rows * i : rows * (i + 1)] = high
        g_low[target(2), rows * i : rows * (i + 1)] = low
    kept = [
        pltpu.make_async_copy(g_high, g_high_out, sems.at[4]),
        pltpu.make_async_copy(g_low, g_low_out, sems.at[5]),
    ]
    for copy in kept:
        copy.start()

    def collect(i):
        for c in range(SIDE):
            start = cell_start(odd, (major + i) % SIDE, (minor + c) % SIDE, rows)
            chunk[:, rows * c : rows * (c + 1)] = g_far[:, pl.ds(start, rows)]
        return chunk[...]

    far = None
    for n, i in enumerate((0, 1, 3)):
        span = slice(panel * n, panel * (n + 1))
        term = product(collect(i), e_high[span, :], e_low[span, :], PLAIN)
        far = term if far is None else far + term
    for copy in copies[2:]:
        copy.wait()
    high, low = halves(e_far[:panel, :])
    far = far + product(collect(2), high, low, PLAIN)

    def one(x, y):
        return lax.dot_general(x, y, (PLAIN, ((), ())), preferred_element_type=f32)

    total[...] = near[...] + (one(far_high[...], high) + (one(far_high[...], low) + one(far_low[...], high)))
    for n, j in enumerate((0, 1, 3)):
        part_high, part_low = halves(total[rows * n : rows * (n + 1), :])
        w_high[target(j), :] = part_high
        w_low[target(j), :] = part_low
    part_high, part_low = halves(far)
    w_high[target(2), :] = part_high
    w_low[target(2), :] = part_low
    spread_panel(panels, e_far, panel, lead, (major + 2) % SIDE * rows, rows)
    base[...] = product(panels[:arrow, :], g_high[...], g_low[...], TURNED)
    first = jnp.where(is_first != 0, panels[arrow:, :], 0.0)
    partial[...] = base[...] - product(first, w_high[...], w_low[...], TURNED)
    for copy in kept:
        copy.wait()


def forward_kernel(flag, old, r0, r1, r2, r3, base, w_high, w_low, partial):
    @pl.when(flag[0] != 0)
    def _():
        arrived = (r0[...] + r1[...]) + (r2[...] + r3[...])
        partial[...] = base[...] - product(arrived, w_high[...], w_low[...], TURNED)

    @pl.when(flag[0] == 0)
    def _():
        partial[...] = old[...]


def turn_kernel(place, own, r1, r2, r3, tip, bound, w_high, w_low, arrow_panel, combined, partial):
    arrow_panel[...] = (own[...] + r1[...]) + (r2[...] + r3[...])

    @pl.when(place[4] != 0)
    def _():
        panel_high, panel_low = halves(arrow_panel[...])
        combined[...] = product(tip[...], panel_high, panel_low, PLAIN) + bound[...]
        partial[...] = -product(combined[...], w_high[...], w_low[...], PLAIN)

    @pl.when(place[4] == 0)
    def _():
        combined[...] = jnp.zeros_like(combined)
        partial[...] = jnp.zeros_like(partial)


def tip_kernel(place, arrow_panel, tip, tip_term, rows_out):
    panel_high, panel_low = halves(arrow_panel[...])
    tip_term[...] = product(tip[...], panel_high, panel_low, PLAIN)
    width = rows_out.shape[1]
    start = pl.multiple_of(place[2] * width, width)
    rows_out[...] = arrow_panel[:, pl.ds(start, width)]


def backward_kernel(flag, old, r0, r1, r2, r3, tip_term, w_high, w_low, combined, partial):
    @pl.when(flag[0] != 0)
    def _():
        combined[...] = tip_term[...] + ((r0[...] + r1[...]) + (r2[...] + r3[...]))
        partial[...] = -product(combined[...], w_high[...], w_low[...], PLAIN)

    @pl.when(flag[0] == 0)
    def _():
        combined[...] = old[...]
        partial[...] = jnp.zeros_like(partial)


def closing_kernel(
    place, flag, old, r0, r1, r2, r3, tip_term, g_high_in, g_low_in, p0, p1, p2, p3, scratch, g_high, g_low, sems
):
    copies = [
        pltpu.make_async_copy(g_high_in, g_high, sems.at[0]),
        pltpu.make_async_copy(g_low_in, g_low, sems.at[1]),
    ]
    for copy in copies:
        copy.start()
    arrived = (r0[...] + r1[...]) + (r2[...] + r3[...])
    combined = jnp.where(flag[0] != 0, tip_term[...] + arrived, old[...])
    high, low = halves(combined)
    count = combined.shape[0]

    def one(x, y):
        return lax.dot_general(x, y, (PLAIN, ((), ())), preferred_element_type=f32)

    copies[0].wait()
    by_high = one(jnp.concatenate([high, low]), g_high[...])
    copies[1].wait()
    scratch[...] = -(by_high[:count] + (one(high, g_low[...]) + by_high[count:]))
    width = p0.shape[1]
    major = place[1]
    for k, out in enumerate((p0, p1, p2, p3)):
        start = pl.multiple_of((major + k) % SIDE * width, width)
        out[...] = scratch[:, pl.ds(start, width)]


def call(kernel, scalars, arrays, outs, scratch=(), anywhere=(), vmem=STEP_VMEM, far_outs=()):
    smem = pl.BlockSpec(memory_space=pltpu.SMEM)
    held = pl.BlockSpec(memory_space=pltpu.VMEM)
    return pl.pallas_call(
        kernel,
        out_shape=[jax.ShapeDtypeStruct(shape, dtype) for shape, dtype in [*outs, *far_outs]],
        in_specs=[smem] * len(scalars) + [held] * len(arrays)
        + [pl.BlockSpec(memory_space=pl.ANY)] * len(anywhere),
        out_specs=[held] * len(outs) + [pl.BlockSpec(memory_space=pltpu.HBM)] * len(far_outs),
        scratch_shapes=list(scratch),
        compiler_params=pltpu.CompilerParams(vmem_limit_bytes=vmem),
    )(*scalars, *arrays, *anywhere)


def on_device(ginv, couple, arrow_rhs, arrow_in, tip_cov, bnd_next):
    g_rows = ginv[0]
    e_rows = couple[0]
    rows = g_rows.shape[0]
    panel = rows * SIDE
    arrow = arrow_in.shape[0]
    step = lax.axis_index("dom")
    spot = lax.axis_index("blk")
    odd = step % 2
    z, y = spot // SIDE, spot % SIDE
    major = jnp.where(odd == 0, z, y)
    minor = jnp.where(odd == 0, y, z)
    place = jnp.stack([odd, major, minor, step == 0, step == STEPS - 1]).astype(jnp.int32)
    wide = ((arrow, panel), f32)
    narrow = ((arrow, rows), f32)
    half_block = ((panel, panel), bf16)

    tail = arrow // SIDE
    lead = 2 * tail
    pieces = call(
        pieces_kernel,
        [place],
        [e_rows, bnd_next],
        [((rows, panel), f32)] + [((rows + tail, panel), f32)] * 3,
    )
    got = {k: permuted(pieces[k], by_minor(k)) for k in FARTHEST_FIRST[:-1]}
    g_after = permuted(g_rows, by_minor(-1))
    g_later, rhs, entering, got[2] = lax.optimization_barrier((g_rows, arrow_rhs[0], arrow_in, got[2]))
    (extra,) = call(extra_kernel, [], [rhs, entering], [((lead, panel), f32)])
    g_before = permuted(g_later, by_minor(1))
    e_own = jnp.concatenate([pieces[0], got[3][:rows], got[2][:rows], got[1][:rows], extra])
    e_after, e_before = ring_near(e_own, by_major)
    g_far = ring_far(g_after, g_before, by_minor)
    e_far = ring_far(e_after, e_before, by_major)

    three = panel - rows
    *near, bound = call(
        near_kernel,
        [place],
        [bnd_next],
        [((three, panel), f32)]
        + [((3 * panel, panel), bf16)] * 2
        + [((three, panel), bf16)] * 4
        + [((2 * arrow, panel), f32), wide],
        [
            pltpu.VMEM((three, panel * SIDE), f32),
            pltpu.VMEM((3 * panel, panel), f32),
            pltpu.VMEM((three, panel), f32),
            pltpu.VMEM((3 * lead, panel), f32),
            pltpu.VMEM((3 * tail, panel), f32),
            pltpu.SemaphoreType.DMA((12,)),
        ],
        [g_rows, g_after, g_before, e_own, e_after, e_before, got[1], got[2], got[3]],
        vmem=FORM_VMEM,
    )
    w_high, w_low, base, partial, g_high, g_low = call(
        far_kernel,
        [place],
        near,
        [half_block] * 2 + [wide] * 2,
        [
            pltpu.VMEM((three, panel), f32),
            pltpu.VMEM((rows, panel * SIDE), f32),
            pltpu.VMEM((panel + lead, panel), f32),
            pltpu.VMEM((rows, panel), f32),
            pltpu.VMEM((2 * arrow, panel), f32),
            pltpu.VMEM((panel, panel), bf16),
            pltpu.VMEM((panel, panel), bf16),
            pltpu.SemaphoreType.DMA((6,)),
        ],
        [*g_far, *e_far],
        vmem=FORM_VMEM,
        far_outs=[half_block] * 2,
    )
    for s in range(STEPS - 1):
        arrived = [permuted(partial, to_next(s, k)) for k in FARTHEST_FIRST]
        flag = (step == s + 1).astype(jnp.int32)[None]
        (partial,) = call(forward_kernel, [flag], [partial, *arrived, base, w_high, w_low], [wide])
    arrived = [permuted(partial, by_minor(k)) for k in FARTHEST_FIRST[:-1]]
    arrow_panel, combined, partial = call(
        turn_kernel,
        [place],
        [partial, *arrived, tip_cov, bound, w_high, w_low],
        [wide] * 3,
    )
    tip_term, arrow_local = call(tip_kernel, [place], [arrow_panel, tip_cov], [wide, narrow])
    for s in range(STEPS - 1, 0, -1):
        arrived = [permuted(partial, to_earlier(s, k)) for k in FARTHEST_FIRST]
        flag = (step == s - 1).astype(jnp.int32)[None]
        if s > 1:
            combined, partial = call(
                backward_kernel, [flag], [combined, *arrived, tip_term, w_high, w_low], [wide] * 2
            )
    parts = call(
        closing_kernel,
        [place, flag],
        [combined, *arrived, tip_term],
        [narrow] * SIDE,
        [
            pltpu.VMEM(*wide),
            pltpu.VMEM((panel, panel), bf16),
            pltpu.VMEM((panel, panel), bf16),
            pltpu.SemaphoreType.DMA((2,)),
        ],
        [g_high, g_low],
    )
    covariance = parts[0]
    for k in FARTHEST_FIRST[:-1]:
        covariance = covariance + permuted(parts[k], by_major(k))
    return (arrow_local[None], covariance[None])


def solution(mesh):
    return jax.shard_map(
        on_device,
        mesh=mesh,
        in_specs=(
            P("dom", "blk", None),
            P("dom", "blk", None),
            P("dom", None, "blk"),
            P(None, "blk"),
            P(),
            P(None, "blk"),
        ),
        out_specs=(P("dom", None, "blk"), P("dom", None, "blk")),
        check_vma=False,
    )
```
